256 devices in a mesh: vox: 16 (over z, core), dir: 16 (over x, y).
Axes of the slice: x: 4, y: 4, z: 8, core: 2. Of those that a mesh axis runs over, the one named last changes fastest.
Arguments:
- signals: bfloat16 [1152, 2, 4, 2048], P('dir', None, None, 'vox'), may hold values from -6 to 6
- basis: float32 [1152, 45], P('dir'), may hold values from -0.1875 to 0.1875
- response: float32 [3, 5], replicated, may hold values from 0.1 to 1
- shell_index: int32 [1152], P('dir'), may hold values from 0 to 2
- brain_mask: int32 [2, 4, 2048], P(None, None, 'vox'), may hold values 0 or 1
- fodf: float32 [45, 2, 4, 2048], P(None, None, None, 'vox'), may hold values from -4 to 4
- aux_field: float32 [45, 2, 2, 4, 2048], P(None, None, None, None, 'vox'), may hold values from -2.4 to 2.4
- grad_dual: float32 [45, 2, 2, 4, 2048], P(None, None, None, None, 'vox'), may hold values from -0.8 to 0.8
- sym_dual: float32 [45, 3, 2, 4, 2048], P(None, None, None, None, 'vox'), may hold values from -0.8 to 0.8
- data_dual: float32 [1152, 2, 4, 2048], P('dir', None, None, 'vox'), may hold values from -3 to 3
Outputs:
- fodf_out: float32 [45, 2, 4, 2048], P(None, None, None, 'vox')
- aux_out: float32 [45, 2, 2, 4, 2048], P(None, None, None, None, 'vox')
The draws below stay inside these ranges and needn't reach their ends.
All inputs are finite; a program needn't handle non-finite values. No bound on the sum of `brain_mask` on one device may be relied on, other than what follows from the above.
Results may differ from the reference program's by a relative error of at most 0.0003.
Values sent between devices are 32-bit elements; how exact they have to be, the bound alone decides.
A program may use at most 64 MiB of HBM per device.

```python
import math
import jax
import jax.numpy as jnp
import numpy as np
from jax import lax

NCOEF = 45
NORDER = 5
NSHELL = 3
PLANES = 2
ROWS = 4
ITERS = 2
COLS = 2048
DIRS = 1152


def scaled_field(noise, key, scale):
    shape = (1,) * (noise.ndim - 3) + noise.shape[-3:]
    spread = jnp.exp(jax.random.uniform(key, shape, jnp.float32, math.log(0.2), math.log(2.0)))
    return scale * spread * noise


def draw_fodf(key, part):
    key = jax.random.fold_in(key, 11)
    noise_key, spread_key = jax.random.split(key)
    shape = (NCOEF, PLANES, ROWS, COLS)
    noise = jnp.clip(jax.random.normal(noise_key, shape, jnp.float32), -4.0, 4.0)
    return scaled_field(noise, spread_key, 0.5)


def draw_aux_field(key, part):
    key = jax.random.fold_in(key, 23)
    noise_key, spread_key = jax.random.split(key)
    shape = (NCOEF, 2, PLANES, ROWS, COLS)
    noise = jnp.clip(jax.random.normal(noise_key, shape, jnp.float32), -4.0, 4.0)
    return scaled_field(noise, spread_key, 0.3)


def draw_grad_dual(key, part):
    key = jax.random.fold_in(key, 37)
    noise_key, spread_key = jax.random.split(key)
    shape = (NCOEF, 2, PLANES, ROWS, COLS)
    noise = jnp.clip(jax.random.normal(noise_key, shape, jnp.float32), -4.0, 4.0)
    return scaled_field(noise, spread_key, 0.1)


def draw_sym_dual(key, part):
    key = jax.random.fold_in(key, 41)
    noise_key, spread_key = jax.random.split(key)
    shape = (NCOEF, 3, PLANES, ROWS, COLS)
    noise = jnp.clip(jax.random.normal(noise_key, shape, jnp.float32), -4.0, 4.0)
    return scaled_field(noise, spread_key, 0.1)


def set_ends(drawn, rng, low, high):
    shape = drawn.shape
    index_at = [jax.random.randint(jax.random.fold_in(rng, axis), (), 0, shape[axis]) for axis in range(len(shape))]
    drawn = drawn.at[tuple(index_at)].set(low)
    longest = shape.index(max(shape))
    index_at[longest] = (index_at[longest] + 1) % shape[longest]
    return drawn.at[tuple(index_at)].set(high)


def level_of(stream_key, extent, pieces, least, high):
    level, own = 1.0, jax.random.fold_in(stream_key, 6)
    for axis_at, parts in pieces:
        steps = jnp.exp(jax.random.uniform(jax.random.fold_in(own, axis_at), (parts,), jnp.float32, least / len(pieces), high / len(pieces)))
        level = level * jnp.repeat(steps, extent[axis_at] // parts).reshape([-1 if axis == axis_at else 1 for axis in range(len(extent))])
    return level


def bell_draw(own_key, dims, scale, bound, cuts=(), kind=jnp.bfloat16):
    level = level_of(own_key, dims, cuts, -0.22, 0.18) if cuts else 1.0
    result = jax.random.normal(own_key, dims, jnp.float32) * scale * level
    return jnp.minimum(jnp.maximum(result, -bound), bound).astype(kind)


def setup_inputs(seed: int = 0) -> dict:
    keys = jax.random.split(jax.random.key(seed), 11)
    signals = bell_draw(keys[0], (DIRS, PLANES, ROWS, COLS), 1.0, 6.0, ((0, 16), (3, 16)))
    basis = bell_draw(keys[1], (DIRS, NCOEF), DIRS ** -0.5, 0.1875, ((0, 16),), jnp.float32)
    response = jnp.clip(jnp.exp(jax.random.uniform(keys[2], (NSHELL, NORDER), jnp.float32, math.log(0.1), math.log(1.0))), 0.1, 1.0)
    shell_index = set_ends(jax.random.randint(keys[3], (DIRS,), 0, NSHELL), jax.random.fold_in(keys[3], 1), 0, NSHELL - 1).astype(jnp.int32)
    brain_mask = set_ends((jax.random.randint(keys[4], (PLANES, ROWS, COLS), 0, 4) < 3).astype(jnp.int32), jax.random.fold_in(keys[4], 1), 0, 1)
    fodf = draw_fodf(jax.random.fold_in(keys[10], 71), 0)
    aux_field = draw_aux_field(jax.random.fold_in(keys[10], 71), 0)
    grad_dual = draw_grad_dual(jax.random.fold_in(keys[10], 71), 0)
    sym_dual = draw_sym_dual(jax.random.fold_in(keys[10], 71), 0)
    data_dual = bell_draw(keys[9], (DIRS, PLANES, ROWS, COLS), 0.5, 3.0, ((0, 16), (3, 16)), jnp.float32)
    return dict(signals=signals, basis=basis, response=response, shell_index=shell_index, brain_mask=brain_mask, fodf=fodf, aux_field=aux_field, grad_dual=grad_dual, sym_dual=sym_dual, data_dual=data_dual)


sigma_step = 0.25
tau_step = 0.3
alpha_one = 1.0
alpha_zero = 1.5
order_table = np.repeat(np.arange(5), [1, 5, 9, 13, 17]).astype(np.int32)
highest = lax.Precision.HIGHEST

def build_kernel(basis, response, shell_index):
    nshell, norder = response.shape
    shell_hot = (shell_index[:, None] == lax.broadcasted_iota(jnp.int32, (1, nshell), 1)).astype(jnp.float32)
    per_order = jnp.dot(shell_hot, response, precision=highest)
    order_hot = (jnp.asarray(order_table)[None, :] == lax.broadcasted_iota(jnp.int32, (norder, 1), 0)).astype(jnp.float32)
    return basis * jnp.dot(per_order, order_hot, precision=highest)

def rows_forward(field):
    step = field[..., 1:, :] - field[..., :-1, :]
    return jnp.concatenate([step, jnp.zeros_like(field[..., :1, :])], -2)

def rows_backward(field):
    count = field.shape[-2]
    keep = (lax.broadcasted_iota(jnp.int32, (count, 1), 0) < count - 1).astype(field.dtype)
    prior = jnp.concatenate([jnp.zeros_like(field[..., :1, :]), field[..., :-1, :]], -2)
    return field * keep - prior

def cols_forward(field, keep_next):
    upcoming = jnp.concatenate([field[..., 1:], jnp.zeros_like(field[..., :1])], -1)
    return (upcoming - field) * keep_next

def cols_backward(field, keep_next):
    prior = jnp.concatenate([jnp.zeros_like(field[..., :1]), field[..., :-1]], -1)
    return field * keep_next - prior

def reference(signals, basis, response, shell_index, brain_mask, fodf, aux_field, grad_dual, sym_dual, data_dual):
    ncoef, planes, rows, cols = fodf.shape
    keep_next = (lax.broadcasted_iota(jnp.int32, (cols,), 0) < cols - 1).astype(fodf.dtype)
    kernel = build_kernel(basis, response, shell_index)
    mask_flat = brain_mask.reshape(1, -1).astype(fodf.dtype)
    sig_flat = signals.reshape(signals.shape[0], -1).astype(jnp.float32)
    dual_flat = data_dual.reshape(data_dual.shape[0], -1)
    u_cur, w_cur, p_cur, q_cur = (fodf, aux_field, grad_dual, sym_dual)
    ubar, wbar = (fodf, aux_field)
    for step in range(ITERS):
        grad_u = jnp.stack([rows_forward(ubar), cols_forward(ubar, keep_next)], 1)
        p_tilde = p_cur + sigma_step * (grad_u - wbar)
        e_rows = rows_backward(wbar[:, 0])
        e_cols = cols_backward(wbar[:, 1], keep_next)
        e_mixed = 0.5 * (cols_backward(wbar[:, 0], keep_next) + rows_backward(wbar[:, 1]))
        q_tilde = q_cur + sigma_step * jnp.stack([e_rows, e_cols, e_mixed], 1)
        p_sq = lax.optimization_barrier(jnp.sum(p_tilde * p_tilde, axis=(0, 1)))
        q_sq = lax.optimization_barrier(jnp.sum(q_tilde[:, 0] ** 2 + q_tilde[:, 1] ** 2 + 2.0 * q_tilde[:, 2] ** 2, axis=0))
        p_cur = p_tilde / jnp.maximum(1.0, jnp.sqrt(p_sq) / alpha_one)
        q_cur = q_tilde / jnp.maximum(1.0, jnp.sqrt(q_sq) / alpha_zero)
        predicted = jnp.dot(kernel, ubar.reshape(ncoef, -1), precision=highest)
        dual_flat = mask_flat * (dual_flat + sigma_step * (predicted - sig_flat)) / (1.0 + sigma_step)
        adjoint = lax.dot_general(kernel, dual_flat, (((0,), (0,)), ((), ())), precision=highest).reshape(fodf.shape)
        div_p = rows_backward(p_cur[:, 0]) + cols_backward(p_cur[:, 1], keep_next)
        u_next = u_cur - tau_step * (adjoint - div_p)
        div_rows = rows_forward(q_cur[:, 0]) + cols_forward(q_cur[:, 2], keep_next)
        div_cols = cols_forward(q_cur[:, 1], keep_next) + rows_forward(q_cur[:, 2])
        w_next = w_cur + tau_step * (p_cur + jnp.stack([div_rows, div_cols], 1))
        ubar = 2.0 * u_next - u_cur
        wbar = 2.0 * w_next - w_cur
        u_cur, w_cur = (u_next, w_next)
    return (u_cur, w_cur)
```

```python
import functools

import jax
import jax.numpy as jnp
import numpy as np
from jax import lax
from jax.experimental import pallas as pl
from jax.experimental.pallas import tpu as pltpu
from jax.sharding import PartitionSpec as P

MESH = pl.DeviceIdType.MESH
f32 = jnp.float32
bf16 = jnp.bfloat16

SIGMA = 0.25
TAU = 0.3
ALPHA1 = 1.0
ALPHA0 = 1.5
ORDER_STARTS = (1, 6, 15, 28)

NC = 45
CP = 48
HALF = 24
ND = 72
NR = 8
SIDE = 4


def split(x):
    hi = x.astype(bf16)
    return hi, (x - hi.astype(f32)).astype(bf16)


def mm(a, b):
    return jnp.dot(a, b, preferred_element_type=f32)


def mm3(ah, al, x):
    xh, xl = split(x)
    return mm(ah, xh) + mm(ah, xl) + mm(al, xh)


def rows_of(pr):
    start = pr * CP
    return pl.ds(start if isinstance(start, int) else pl.multiple_of(start, 8), CP)


def kernel(
    nvox,
    sig_hbm, basis_hbm, resp_hbm, shell_hbm, mask_hbm, fodf_hbm, aux_hbm, grad_hbm, sym_hbm, dual_hbm,
    u_hbm, w_hbm,
    sig, basis, resp, shell, mask, u0, w0, p0, q0, y0, sigf,
    kt, ta, tb, fa, fb, ra, rb, hg,
    halo, halo_l, halo_r, edge, edge_l, edge_r, edge_c, edge_in, wk,
    p1r, p1c, q1a, q1b, q1c, wbr, wbc, w1r, w1c, pbr, pbc, ub, v2r, v2c, u1, ub1, gu, p2r, p2c,
    uo, wo,
    in_sem, out_sem, sa_s, sa_r, sb_s, sb_r, ga_s, ga_r, gb_s, gb_r, ec_s, ec_r, vox_s, vox_r,
):
    me = lax.axis_index("dir")
    vox = lax.axis_index("vox")
    mx, my = me // SIDE, lax.rem(me, SIDE)
    npeer = SIDE * SIDE
    order = sorted(range(1, npeer), key=lambda k: -(min(k // SIDE, SIDE - k // SIDE) + min(k % SIDE, SIDE - k % SIDE)))

    def peer(k):
        return lax.rem(mx + k // SIDE, SIDE) * SIDE + lax.rem(my + k % SIDE, SIDE)

    def source(k):
        return lax.rem(mx + SIDE - k // SIDE, SIDE) * SIDE + lax.rem(my + SIDE - k % SIDE, SIDE)

    right, left = lax.rem(vox + 1, nvox), lax.rem(vox + nvox - 1, nvox)

    def load(i, src, dst):
        return pltpu.make_async_copy(src, dst, in_sem.at[i])

    loads = [
        load(0, basis_hbm, basis),
        load(1, resp_hbm, resp),
        load(2, shell_hbm, shell),
        load(3, mask_hbm, mask),
        load(4, fodf_hbm, u0.at[pl.ds(0, NC * NR)]),
        load(5, sig_hbm, sig),
        load(6, dual_hbm, y0),
        load(7, aux_hbm, w0.at[pl.ds(0, NC * 2 * NR)]),
        load(8, grad_hbm, p0.at[pl.ds(0, NC * 2 * NR)]),
        load(9, sym_hbm, q0.at[pl.ds(0, NC * 3 * NR)]),
    ]
    for c in loads:
        c.start()

    barrier = pltpu.get_barrier_semaphore()
    for k in order:
        pl.semaphore_signal(barrier, inc=1, device_id={"dir": peer(k)}, device_id_type=MESH)
    for n in (left, right):
        pl.semaphore_signal(barrier, inc=1, device_id={"vox": n}, device_id_type=MESH)

    lane = lax.broadcasted_iota(jnp.int32, (1, 128), 1)
    for ref, n in ((u0, 1), (w0, 2), (p0, 2), (q0, 3)):
        ref[pl.ds(NC * n * NR, (CP - NC) * n * NR), :] = jnp.zeros(((CP - NC) * n * NR, 128), f32)

    for c in loads[:3]:
        c.wait()
    kt[...] = jnp.zeros((CP, 128), f32)
    sh = shell[...]
    per_order = [
        jnp.where(sh == 0, resp[0:1, o : o + 1], jnp.where(sh == 1, resp[1:2, o : o + 1], resp[2:3, o : o + 1]))
        for o in range(5)
    ]
    cid = lax.broadcasted_iota(jnp.int32, (NC, 1), 0)
    scale = jnp.broadcast_to(per_order[0], (NC, ND))
    for o, start in enumerate(ORDER_STARTS):
        scale = jnp.where(cid >= start, per_order[o + 1], scale)
    kt[pl.ds(0, NC), pl.ds(0, ND)] = basis[...] * scale
    ktv = kt[...]
    knv = jnp.concatenate([ktv, jnp.zeros((128 - CP, 128), f32)], 0).T[0:ND]
    kth, ktl = split(ktv[:, 0:ND])
    knh128, knl128 = split(knv)
    knh, knl = knh128[:, 0:CP], knl128[:, 0:CP]

    for c in loads[3:7]:
        c.wait()

    def to_f32(i, _):
        at = pl.ds(pl.multiple_of(i * 96, 96), 96)
        sigf[at, :] = sig[at, :].astype(f32)
        return 0

    lax.fori_loop(0, 6, to_f32, 0)

    def natural(ref, pr, n, comp, count):
        return ref[pl.ds(comp * NR + pr, count, stride=n * NR), :]

    def pair(ref, i, count):
        return jnp.concatenate([natural(ref, 2 * i, 1, 0, count), natural(ref, 2 * i + 1, 1, 0, count)], 1)

    def store_pair(ref, i, val):
        ref[rows_of(2 * i), :] = val[:, 0:128]
        ref[rows_of(2 * i + 1), :] = val[:, 128:256]

    def data_step(i, _):
        pred = mm3(knh, knl, pair(u0, i, CP))
        m = jnp.concatenate([mask[pl.ds(2 * i, 1), :], mask[pl.ds(2 * i + 1, 1), :]], 1).astype(f32)
        y = (m * (1.0 / (1.0 + SIGMA))) * (pair(y0, i, ND) + SIGMA * (pred - pair(sigf, i, ND)))
        store_pair(ta, i, mm3(kth, ktl, y))
        return 0

    lax.fori_loop(0, 4, data_step, 0)

    def chunk(d):
        return pl.ds(pl.multiple_of(d * HALF, HALF), HALF)

    def scatter(src, dst, ss, rs, k):
        return pltpu.make_async_remote_copy(
            src_ref=src.at[chunk(peer(k))], dst_ref=dst.at[k], send_sem=ss.at[k], recv_sem=rs.at[k],
            device_id={"dir": peer(k)}, device_id_type=MESH)

    def gather(ref, ss, rs, k, at):
        return pltpu.make_async_remote_copy(
            src_ref=ref.at[chunk(at)], dst_ref=ref.at[chunk(at)], send_sem=ss.at[k], recv_sem=rs.at[k],
            device_id={"dir": peer(k)}, device_id_type=MESH)

    def to_vox(src, dst, n, k):
        return pltpu.make_async_remote_copy(
            src_ref=src, dst_ref=dst, send_sem=vox_s.at[k], recv_sem=vox_r.at[k],
            device_id={"vox": n}, device_id_type=MESH)

    pl.semaphore_wait(barrier, npeer - 1 + 2)
    send_a = [scatter(ta, ra, sa_s, sa_r, k) for k in order]
    for c in send_a:
        c.start()

    slot_of = lane // 8
    j = lax.rem(lane, 8)

    def pack_into(acc, val, pr):
        for h in range(2):
            s = h * NR + pr
            t = pltpu.roll(val[h * HALF : (h + 1) * HALF], 8 * s + 2 if isinstance(s, int) and 8 * s + 2 < 128 else lax.rem(8 * s + 2, 128), 1)
            acc = jnp.where(slot_of == s, t, acc)
        return acc

    zero24 = jnp.zeros((HALF, 128), f32)
    edge[...] = lax.fori_loop(0, NR, lambda pr, acc: pack_into(acc, ta[rows_of(pr), :], pr), zero24)
    edge_right, edge_left = to_vox(edge, edge_l, right, 0), to_vox(edge, edge_r, left, 1)
    edge_right.start()
    edge_left.start()

    def signal_step(i, _):
        s = pair(sigf, i, ND).astype(bf16)
        store_pair(tb, i, mm(kth, s) + mm(ktl, s))
        return 0

    lax.fori_loop(0, 4, signal_step, 0)
    gram = mm3(kth, ktl, knv)
    hpart = gram[0:HALF] + pltpu.roll(gram[HALF:CP], 64, 1)
    for pr in range(NR):
        tb[pl.ds(pr * CP + NC, CP - NC), :] = hpart[3 * pr : 3 * pr + 3]
    send_b = [scatter(tb, rb, sb_s, sb_r, k) for k in order]
    for c in send_b:
        c.start()

    for c in loads[7:]:
        c.wait()

    fields = ((u0, 1, 0), (w0, 2, 0), (w0, 2, 1), (p0, 2, 0), (p0, 2, 1), (q0, 3, 0), (q0, 3, 1), (q0, 3, 2))

    def pack_step(pr, accs):
        return tuple(pack_into(acc, natural(ref, pr, n, comp, CP), pr) for acc, (ref, n, comp) in zip(accs, fields))

    packed = lax.fori_loop(0, NR, pack_step, (zero24,) * 8)
    for f in range(8):
        halo[pl.ds(f * HALF, HALF), :] = packed[f]
    halo_right, halo_left = to_vox(halo, halo_l, right, 2), to_vox(halo, halo_r, left, 3)
    halo_right.start()
    halo_left.start()

    def reduce_chunk(src, scattered, recv, full):
        total = src[chunk(me), :]
        for c, k in zip(scattered, order):
            c.wait_recv()
            total = total + recv[k]
        full[chunk(me), :] = total

    reduce_chunk(ta, send_a, ra, fa)
    give_a = [gather(fa, ga_s, ga_r, k, me) for k in order]
    for c in give_a:
        c.start()

    has_left = vox > 0
    has_right = vox < nvox - 1
    edge_right.wait_recv()
    edge_left.wait_recv()
    near = jnp.where((j == 1) & has_left, edge_l[...], 0.0) + jnp.where((j == 6) & has_right, pltpu.roll(edge_r[...], 4, 1), 0.0)
    edge_c[...] = near[0:8] + pltpu.roll(near[8:16], 1, 1) + pltpu.roll(near[16:24], 2, 1)

    def spread(k):
        return pltpu.make_async_remote_copy(
            src_ref=edge_c, dst_ref=edge_in.at[k], send_sem=ec_s.at[k], recv_sem=ec_r.at[k],
            device_id={"dir": peer(k)}, device_id_type=MESH)

    send_e = [spread(k) for k in order]
    for c in send_e:
        c.start()

    halo_right.wait_recv()
    halo_left.wait_recv()

    def widen(f):
        at = pl.ds(f * HALF, HALF)
        own = halo[at, :]
        far_l = jnp.where(has_left, halo_l[at, :], 0.0)
        far_r = jnp.where(has_right, halo_r[at, :], 0.0)
        return jnp.where(j < 2, far_l, jnp.where(j < 4, own, pltpu.roll(jnp.where(j < 2, own, far_r), 4, 1)))

    col = jnp.where(j < 4, j - 2, j + 122) + vox * 128
    keep_w = ((col >= 0) & (col < nvox * 128 - 1)).astype(f32)
    rid = lax.rem(lane // 8, 4)
    low_w, high_w = (rid < 3).astype(f32), (rid >= 1).astype(f32)

    def fr_w(x):
        return (pltpu.roll(x, 120, 1) - x) * low_w

    def br_w(x):
        return x * low_w - pltpu.roll(x, 8, 1) * high_w

    def fx_w(x):
        return (pltpu.roll(x, 127, 1) - x) * keep_w

    def bx_w(x):
        return x * keep_w - pltpu.roll(x, 1, 1)

    def shrink(sq, alpha):
        return jnp.minimum(1.0, alpha * lax.rsqrt(sq))

    def norm_w(sq):
        n = jnp.sum(sq, 0, keepdims=True)
        return n + pltpu.roll(n, 64, 1)

    def dual_p_w(pr_, pc_, u_, wr_, wc_):
        a = pr_ + SIGMA * (fr_w(u_) - wr_)
        b = pc_ + SIGMA * (fx_w(u_) - wc_)
        s = shrink(norm_w(a * a + b * b), ALPHA1)
        return a * s, b * s

    def dual_q_w(qa_, qb_, qc_, wr_, wc_):
        a = qa_ + SIGMA * br_w(wr_)
        b = qb_ + SIGMA * bx_w(wc_)
        c = qc_ + (0.5 * SIGMA) * (bx_w(wr_) + br_w(wc_))
        s = shrink(norm_w(a * a + b * b + 2.0 * (c * c)), ALPHA0)
        return a * s, b * s, c * s

    uw, wrw, wcw = widen(0), widen(1), widen(2)
    p1rw, p1cw = dual_p_w(widen(3), widen(4), uw, wrw, wcw)
    q1aw, q1bw, q1cw = dual_q_w(widen(5), widen(6), widen(7), wrw, wcw)
    w1rw = wrw + TAU * (p1rw + fr_w(q1aw) + fx_w(q1cw))
    w1cw = wcw + TAU * (p1cw + fx_w(q1bw) + fr_w(q1cw))
    wbrw, wbcw = 2.0 * w1rw - wrw, 2.0 * w1cw - wcw
    _, q2bw, q2cw = dual_q_w(q1aw, q1bw, q1cw, wbrw, wbcw)
    pbrw, pbcw = p1rw - SIGMA * wbrw, p1cw - SIGMA * wbcw
    ubw = uw + TAU * (br_w(p1rw) + bx_w(p1cw))
    for n, val in enumerate((uw, wrw, wcw, p1cw, q1bw, q1cw, wbrw, wbcw, q2bw, q2cw, pbrw, pbcw, ubw)):
        wk[n] = val

    keep = jnp.where(lane + vox * 128 < nvox * 128 - 1, 1.0, 0.0).astype(f32)

    def beside(val, pr, at):
        parts = [pltpu.roll(val, at - 8 * (h * NR + pr), 1) for h in range(2)]
        return jnp.concatenate(parts, 0)

    def nxt(x, far, pr):
        return jnp.where(lane == 127, beside(far, pr, 121), pltpu.roll(x, 127, 1))

    def prv(x, far, pr):
        return jnp.where(lane == 0, beside(far, pr, 127), pltpu.roll(x, 1, 1))

    def fx(x, far, pr):
        return (nxt(x, far, pr) - x) * keep

    def bx(x, far, pr):
        return x * keep - prv(x, far, pr)

    def fr(x, below, r):
        return below - x if r < 3 else jnp.zeros_like(x)

    def br(x, above, r):
        if r == 0:
            return x
        return x - above if r < 3 else -above

    def colsum(x):
        return jnp.sum(x, 0, keepdims=True)

    def dual_one(p, _):
        for r in range(4):
            pr = 4 * p + r
            u = natural(u0, pr, 1, 0, CP)
            below = natural(u0, pr + 1, 1, 0, CP) if r < 3 else None
            wr, wc = natural(w0, pr, 2, 0, CP), natural(w0, pr, 2, 1, CP)
            a = natural(p0, pr, 2, 0, CP) + SIGMA * (fr(u, below, r) - wr)
            b = natural(p0, pr, 2, 1, CP) + SIGMA * (fx(u, wk[0], pr) - wc)
            s = shrink(colsum(a * a + b * b), ALPHA1)
            p1r[rows_of(pr), :] = a * s
            p1c[rows_of(pr), :] = b * s
            wra = natural(w0, pr - 1, 2, 0, CP) if r > 0 else None
            wca = natural(w0, pr - 1, 2, 1, CP) if r > 0 else None
            a = natural(q0, pr, 3, 0, CP) + SIGMA * br(wr, wra, r)
            b = natural(q0, pr, 3, 1, CP) + SIGMA * bx(wc, wk[2], pr)
            c = natural(q0, pr, 3, 2, CP) + (0.5 * SIGMA) * (bx(wr, wk[1], pr) + br(wc, wca, r))
            s = shrink(colsum(a * a + b * b + 2.0 * (c * c)), ALPHA0)
            q1a[rows_of(pr), :] = a * s
            q1b[rows_of(pr), :] = b * s
            q1c[rows_of(pr), :] = c * s
        return 0

    lax.fori_loop(0, 2, dual_one, 0)

    reduce_chunk(tb, send_b, rb, fb)
    give_b = [gather(fb, gb_s, gb_r, k, me) for k in order]
    for c in give_b:
        c.start()

    def primal_one(p, _):
        for r in range(4):
            pr = 4 * p + r
            here = rows_of(pr)
            pr_, pc_ = p1r[here, :], p1c[here, :]
            above = p1r[rows_of(pr - 1), :] if r > 0 else None
            ub[here, :] = natural(u0, pr, 1, 0, CP) + TAU * (br(pr_, above, r) + bx(pc_, wk[3], pr))
            qa, qb, qc = q1a[here, :], q1b[here, :], q1c[here, :]
            qab = q1a[rows_of(pr + 1), :] if r < 3 else None
            qcb = q1c[rows_of(pr + 1), :] if r < 3 else None
            wr, wc = natural(w0, pr, 2, 0, CP), natural(w0, pr, 2, 1, CP)
            dr = TAU * (pr_ + fr(qa, qab, r) + fx(qc, wk[5], pr))
            dc = TAU * (pc_ + fx(qb, wk[4], pr) + fr(qc, qcb, r))
            nr, nc = wr + 2.0 * dr, wc + 2.0 * dc
            w1r[here, :] = wr + dr
            w1c[here, :] = wc + dc
            wbr[here, :] = nr
            wbc[here, :] = nc
            pbr[here, :] = pr_ - SIGMA * nr
            pbc[here, :] = pc_ - SIGMA * nc
        return 0

    lax.fori_loop(0, 2, primal_one, 0)

    def dual_two(p, _):
        for r in range(4):
            pr = 4 * p + r
            here = rows_of(pr)
            wr, wc = wbr[here, :], wbc[here, :]
            wra = wbr[rows_of(pr - 1), :] if r > 0 else None
            wca = wbc[rows_of(pr - 1), :] if r > 0 else None
            a = q1a[here, :] + SIGMA * br(wr, wra, r)
            b = q1b[here, :] + SIGMA * bx(wc, wk[7], pr)
            c = q1c[here, :] + (0.5 * SIGMA) * (bx(wr, wk[6], pr) + br(wc, wca, r))
            s = shrink(colsum(a * a + b * b + 2.0 * (c * c)), ALPHA0)
            q1a[here, :] = a * s
            q1b[here, :] = b * s
            q1c[here, :] = c * s
        return 0

    lax.fori_loop(0, 2, dual_two, 0)

    def aux_two(p, _):
        for r in range(4):
            pr = 4 * p + r
            here = rows_of(pr)
            qa, qb, qc = q1a[here, :], q1b[here, :], q1c[here, :]
            qab = q1a[rows_of(pr + 1), :] if r < 3 else None
            qcb = q1c[rows_of(pr + 1), :] if r < 3 else None
            v2r[here, :] = w1r[here, :] + TAU * (fr(qa, qab, r) + fx(qc, wk[9], pr))
            v2c[here, :] = w1c[here, :] + TAU * (fx(qb, wk[8], pr) + fr(qc, qcb, r))
        return 0

    lax.fori_loop(0, 2, aux_two, 0)

    take_a = [gather(fa, ga_s, ga_r, k, source(k)) for k in order]
    for c in take_a:
        c.wait_recv()

    def extrapolate(pr, acc):
        here = rows_of(pr)
        new = ub[here, :] - TAU * fa[here, :]
        bar = 2.0 * new - natural(u0, pr, 1, 0, CP)
        u1[here, :] = new
        ub1[here, :] = bar
        return pack_into(acc, bar, pr)

    own_bar = lax.fori_loop(0, NR, extrapolate, zero24)

    total = edge_c[...]
    for c, k in zip(send_e, order):
        c.wait_recv()
        total = total + edge_in[k]
    adj_w = jnp.concatenate([total, pltpu.roll(total, 127, 1), pltpu.roll(total, 126, 1)], 0)
    adj_w = jnp.where((j == 1) | (j == 6), adj_w, 0.0)
    bar_w = 2.0 * (wk[12] - TAU * adj_w) - wk[0]
    bar_w = jnp.where((j == 2) | (j == 3), own_bar, bar_w)
    a = wk[10] + SIGMA * fr_w(bar_w)
    b = wk[11] + SIGMA * fx_w(bar_w)
    s = shrink(norm_w(a * a + b * b), ALPHA1)
    wk[0] = bar_w
    wk[3] = b * s

    def dual_three(p, _):
        for r in range(4):
            pr = 4 * p + r
            here = rows_of(pr)
            u = ub1[here, :]
            below = ub1[rows_of(pr + 1), :] if r < 3 else None
            a = pbr[here, :] + SIGMA * fr(u, below, r)
            b = pbc[here, :] + SIGMA * fx(u, wk[0], pr)
            s = shrink(colsum(a * a + b * b), ALPHA1)
            a, b = a * s, b * s
            p2r[here, :] = a
            p2c[here, :] = b
            wo[pl.ds(pr, CP, stride=2 * NR), :] = v2r[here, :] + TAU * a
            wo[pl.ds(NR + pr, CP, stride=2 * NR), :] = v2c[here, :] + TAU * b
        return 0

    lax.fori_loop(0, 2, dual_three, 0)
    put_w = pltpu.make_async_copy(wo.at[pl.ds(0, NC * 2 * NR)], w_hbm, out_sem.at[1])
    put_w.start()

    take_b = [gather(fb, gb_s, gb_r, k, source(k)) for k in order]
    for c in take_b:
        c.wait_recv()
    for pr in range(NR):
        hg[pl.ds(3 * pr, 3), :] = fb[pl.ds(pr * CP + NC, CP - NC), :]
    hv = hg[...]
    gh, gl = split(jnp.concatenate([hv, pltpu.roll(hv, 64, 1)], 0)[:, 0:CP])

    def gram_step(i, _):
        bar = jnp.concatenate([ub1[rows_of(2 * i), :], ub1[rows_of(2 * i + 1), :]], 1)
        store_pair(gu, i, mm3(gh, gl, bar))
        return 0

    lax.fori_loop(0, 4, gram_step, 0)

    def primal_two(p, _):
        for r in range(4):
            pr = 4 * p + r
            here = rows_of(pr)
            m = mask[pl.ds(pr, 1), :].astype(f32) * (1.0 / (1.0 + SIGMA))
            adj = m * (fa[here, :] + SIGMA * (gu[here, :] - fb[here, :]))
            above = p2r[rows_of(pr - 1), :] if r > 0 else None
            div = br(p2r[here, :], above, r) + bx(p2c[here, :], wk[3], pr)
            uo[pl.ds(pr, CP, stride=NR), :] = u1[here, :] - TAU * (adj - div)
        return 0

    lax.fori_loop(0, 2, primal_two, 0)
    put_u = pltpu.make_async_copy(uo.at[pl.ds(0, NC * NR)], u_hbm, out_sem.at[0])
    put_u.start()

    for c in send_a + send_b + give_a + give_b + send_e + [edge_right, edge_left, halo_right, halo_left]:
        c.wait_send()
    put_w.wait()
    put_u.wait()


def body(nvox, signals, basis, response, shell_index, brain_mask, fodf, aux_field, grad_dual, sym_dual, data_dual):
    hbm = pl.BlockSpec(memory_space=pltpu.HBM)
    field = pltpu.VMEM((NR * CP, 128), f32)
    npeer = SIDE * SIDE
    dma = lambda n: pltpu.SemaphoreType.DMA((n,))
    edges = pltpu.VMEM((HALF, 128), f32)
    halos = pltpu.VMEM((8 * HALF, 128), f32)
    u, w = pl.pallas_call(
        functools.partial(kernel, nvox),
        out_shape=(
            jax.ShapeDtypeStruct((NC * NR, 128), f32),
            jax.ShapeDtypeStruct((NC * 2 * NR, 128), f32),
        ),
        in_specs=[hbm] * 10,
        out_specs=(hbm, hbm),
        scratch_shapes=[
            pltpu.VMEM((ND * NR, 128), bf16),
            pltpu.VMEM((NC, ND), f32),
            pltpu.VMEM((3, 5), f32),
            pltpu.VMEM((1, ND), jnp.int32),
            pltpu.VMEM((NR, 128), jnp.int32),
            field,
            pltpu.VMEM((CP * 2 * NR, 128), f32),
            pltpu.VMEM((CP * 2 * NR, 128), f32),
            pltpu.VMEM((CP * 3 * NR, 128), f32),
            pltpu.VMEM((ND * NR, 128), f32),
            pltpu.VMEM((ND * NR, 128), f32),
            pltpu.VMEM((CP, 128), f32),
            field, field, field, field,
            pltpu.VMEM((npeer, HALF, 128), f32),
            pltpu.VMEM((npeer, HALF, 128), f32),
            edges,
            halos, halos, halos,
            edges, edges, edges,
            pltpu.VMEM((8, 128), f32),
            pltpu.VMEM((npeer, 8, 128), f32),
            pltpu.VMEM((13, HALF, 128), f32),
        ]
        + [field] * 19
        + [
            field,
            pltpu.VMEM((CP * 2 * NR, 128), f32),
            dma(10), dma(2),
        ]
        + [dma(npeer)] * 10
        + [dma(4), dma(4)],
        compiler_params=pltpu.CompilerParams(
            collective_id=0, has_side_effects=True, vmem_limit_bytes=48 * 1024 * 1024
        ),
    )(
        signals.reshape(ND * NR, 128),
        basis.T,
        response,
        shell_index.reshape(1, ND),
        brain_mask.reshape(NR, 128),
        fodf.reshape(NC * NR, 128),
        aux_field.reshape(NC * 2 * NR, 128),
        grad_dual.reshape(NC * 2 * NR, 128),
        sym_dual.reshape(NC * 3 * NR, 128),
        data_dual.reshape(ND * NR, 128),
    )
    return u.reshape(fodf.shape), w.reshape(aux_field.shape)


def solution(mesh):
    placed = (
        P("dir", None, None, "vox"),
        P("dir", None),
        P(),
        P("dir"),
        P(None, None, "vox"),
        P(None, None, None, "vox"),
        P(None, None, None, None, "vox"),
        P(None, None, None, None, "vox"),
        P(None, None, None, None, "vox"),
        P("dir", None, None, "vox"),
    )
    return jax.shard_map(
        functools.partial(body, mesh.shape["vox"]),
        mesh=mesh,
        in_specs=placed,
        out_specs=(P(None, None, None, "vox"), P(None, None, None, None, "vox")),
        check_vma=False,
    )
```

```python
import functools

import jax
import jax.numpy as jnp
import numpy as np
from jax import lax
from jax.experimental import pallas as pl
from jax.experimental.pallas import tpu as pltpu
from jax.sharding import PartitionSpec as P

MESH = pl.DeviceIdType.MESH
f32 = jnp.float32
bf16 = jnp.bfloat16

SIGMA = 0.25
TAU = 0.3
ALPHA1 = 1.0
ALPHA0 = 1.5
ORDER_STARTS = (1, 6, 15, 28)

NC = 45
CP = 48
HALF = 24
ND = 72
NR = 8
SIDE = 4


def split(x):
    hi = x.astype(bf16)
    return hi, (x - hi.astype(f32)).astype(bf16)


def mm(a, b):
    return jnp.dot(a, b, preferred_element_type=f32)


def mm3(ah, al, x):
    xh, xl = split(x)
    return mm(ah, xh) + mm(ah, xl) + mm(al, xh)


def rows_of(pr):
    start = pr * CP
    return pl.ds(start if isinstance(start, int) else pl.multiple_of(start, 8), CP)


def kernel(
    nvox,
    sig_hbm, basis_hbm, resp_hbm, shell_hbm, mask_hbm, fodf_hbm, aux_hbm, grad_hbm, sym_hbm, dual_hbm,
    uo, wo,
    sig, basis, resp, shell, mask, u0, w0, p0, q0, y0, sigf,
    kt, ta, tb, fa, fb, ra, rb, hg,
    halo, halo_l, halo_r, edge, edge_l, edge_r, edge_c, edge_in, wk,
    p1r, p1c, q1a, q1b, q1c, wbr, wbc, w1r, w1c, pbr, pbc, ub, v2r, v2c, u1, ub1, gu, p2r, p2c,
    in_sem, sa_s, sa_r, sb_s, sb_r, ga_s, ga_r, gb_s, gb_r, ec_s, ec_r, vox_s, vox_r,
):
    me = lax.axis_index("dir")
    vox = lax.axis_index("vox")
    mx, my = me // SIDE, lax.rem(me, SIDE)
    npeer = SIDE * SIDE
    order = sorted(range(1, npeer), key=lambda k: -(min(k // SIDE, SIDE - k // SIDE) + min(k % SIDE, SIDE - k % SIDE)))

    def peer(k):
        return lax.rem(mx + k // SIDE, SIDE) * SIDE + lax.rem(my + k % SIDE, SIDE)

    def source(k):
        return lax.rem(mx + SIDE - k // SIDE, SIDE) * SIDE + lax.rem(my + SIDE - k % SIDE, SIDE)

    right, left = lax.rem(vox + 1, nvox), lax.rem(vox + nvox - 1, nvox)

    def load(i, src, dst):
        return pltpu.make_async_copy(src, dst, in_sem.at[i])

    loads = [
        load(0, basis_hbm, basis),
        load(1, resp_hbm, resp),
        load(2, shell_hbm, shell),
        load(3, mask_hbm, mask),
        load(4, fodf_hbm, u0.at[pl.ds(0, NC * NR)]),
        load(5, sig_hbm, sig),
        load(6, dual_hbm, y0),
        load(7, aux_hbm, w0.at[pl.ds(0, NC * 2 * NR)]),
        load(8, grad_hbm, p0.at[pl.ds(0, NC * 2 * NR)]),
        load(9, sym_hbm, q0.at[pl.ds(0, NC * 3 * NR)]),
    ]
    for c in loads:
        c.start()

    barrier = pltpu.get_barrier_semaphore()
    for k in order:
        pl.semaphore_signal(barrier, inc=1, device_id={"dir": peer(k)}, device_id_type=MESH)
    for n in (left, right):
        pl.semaphore_signal(barrier, inc=1, device_id={"vox": n}, device_id_type=MESH)

    lane = lax.broadcasted_iota(jnp.int32, (1, 128), 1)
    for ref, n in ((u0, 1), (w0, 2), (p0, 2), (q0, 3)):
        ref[pl.ds(NC * n * NR, (CP - NC) * n * NR), :] = jnp.zeros(((CP - NC) * n * NR, 128), f32)

    for c in loads[:3]:
        c.wait()
    kt[...] = jnp.zeros((CP, 128), f32)
    sh = shell[...]
    per_order = [
        jnp.where(sh == 0, resp[0:1, o : o + 1], jnp.where(sh == 1, resp[1:2, o : o + 1], resp[2:3, o : o + 1]))
        for o in range(5)
    ]
    cid = lax.broadcasted_iota(jnp.int32, (NC, 1), 0)
    scale = jnp.broadcast_to(per_order[0], (NC, ND))
    for o, start in enumerate(ORDER_STARTS):
        scale = jnp.where(cid >= start, per_order[o + 1], scale)
    kt[pl.ds(0, NC), pl.ds(0, ND)] = basis[...] * scale
    ktv = kt[...]
    knv = jnp.concatenate([ktv, jnp.zeros((128 - CP, 128), f32)], 0).T[0:ND]
    kth, ktl = split(ktv[:, 0:ND])
    knh128, knl128 = split(knv)
    knh, knl = knh128[:, 0:CP], knl128[:, 0:CP]

    for c in loads[3:7]:
        c.wait()

    def to_f32(i, _):
        at = pl.ds(pl.multiple_of(i * 96, 96), 96)
        sigf[at, :] = sig[at, :].astype(f32)
        return 0

    lax.fori_loop(0, 6, to_f32, 0)

    def natural(ref, pr, n, comp, count):
        return ref[pl.ds(comp * NR + pr, count, stride=n * NR), :]

    def pair(ref, i, count):
        return jnp.concatenate([natural(ref, 2 * i, 1, 0, count), natural(ref, 2 * i + 1, 1, 0, count)], 1)

    def store_pair(ref, i, val):
        ref[rows_of(2 * i), :] = val[:, 0:128]
        ref[rows_of(2 * i + 1), :] = val[:, 128:256]

    def data_step(i, _):
        pred = mm3(knh, knl, pair(u0, i, CP))
        m = jnp.concatenate([mask[pl.ds(2 * i, 1), :], mask[pl.ds(2 * i + 1, 1), :]], 1).astype(f32)
        y = (m * (1.0 / (1.0 + SIGMA))) * (pair(y0, i, ND) + SIGMA * (pred - pair(sigf, i, ND)))
        store_pair(ta, i, mm3(kth, ktl, y))
        return 0

    lax.fori_loop(0, 4, data_step, 0)

    def chunk(d):
        return pl.ds(pl.multiple_of(d * HALF, HALF), HALF)

    def scatter(src, dst, ss, rs, k):
        return pltpu.make_async_remote_copy(
            src_ref=src.at[chunk(peer(k))], dst_ref=dst.at[k], send_sem=ss.at[k], recv_sem=rs.at[k],
            device_id={"dir": peer(k)}, device_id_type=MESH)

    def gather(ref, ss, rs, k, at):
        return pltpu.make_async_remote_copy(
            src_ref=ref.at[chunk(at)], dst_ref=ref.at[chunk(at)], send_sem=ss.at[k], recv_sem=rs.at[k],
            device_id={"dir": peer(k)}, device_id_type=MESH)

    def to_vox(src, dst, n, k):
        return pltpu.make_async_remote_copy(
            src_ref=src, dst_ref=dst, send_sem=vox_s.at[k], recv_sem=vox_r.at[k],
            device_id={"vox": n}, device_id_type=MESH)

    pl.semaphore_wait(barrier, npeer - 1 + 2)
    send_a = [scatter(ta, ra, sa_s, sa_r, k) for k in order]
    for c in send_a:
        c.start()

    slot_of = lane // 8
    j = lax.rem(lane, 8)

    def pack_into(acc, val, pr):
        for h in range(2):
            s = h * NR + pr
            t = pltpu.roll(val[h * HALF : (h + 1) * HALF], 8 * s + 2 if isinstance(s, int) and 8 * s + 2 < 128 else lax.rem(8 * s + 2, 128), 1)
            acc = jnp.where(slot_of == s, t, acc)
        return acc

    zero24 = jnp.zeros((HALF, 128), f32)
    edge[...] = lax.fori_loop(0, NR, lambda pr, acc: pack_into(acc, ta[rows_of(pr), :], pr), zero24)
    edge_right, edge_left = to_vox(edge, edge_l, right, 0), to_vox(edge, edge_r, left, 1)
    edge_right.start()
    edge_left.start()

    def signal_step(i, _):
        s = pair(sigf, i, ND).astype(bf16)
        store_pair(tb, i, mm(kth, s) + mm(ktl, s))
        return 0

    lax.fori_loop(0, 4, signal_step, 0)
    gram = mm3(kth, ktl, knv)
    hpart = gram[0:HALF] + pltpu.roll(gram[HALF:CP], 64, 1)
    for pr in range(NR):
        tb[pl.ds(pr * CP + NC, CP - NC), :] = hpart[3 * pr : 3 * pr + 3]
    send_b = [scatter(tb, rb, sb_s, sb_r, k) for k in order]
    for c in send_b:
        c.start()

    for c in loads[7:]:
        c.wait()

    fields = ((u0, 1, 0), (w0, 2, 0), (w0, 2, 1), (p0, 2, 0), (p0, 2, 1), (q0, 3, 0), (q0, 3, 1), (q0, 3, 2))

    def pack_step(pr, accs):
        return tuple(pack_into(acc, natural(ref, pr, n, comp, CP), pr) for acc, (ref, n, comp) in zip(accs, fields))

    packed = lax.fori_loop(0, NR, pack_step, (zero24,) * 8)
    for f in range(8):
        halo[pl.ds(f * HALF, HALF), :] = packed[f]
    halo_right, halo_left = to_vox(halo, halo_l, right, 2), to_vox(halo, halo_r, left, 3)
    halo_right.start()
    halo_left.start()

    def reduce_chunk(src, scattered, recv, full):
        total = src[chunk(me), :]
        for c, k in zip(scattered, order):
            c.wait_recv()
            total = total + recv[k]
        full[chunk(me), :] = total

    reduce_chunk(ta, send_a, ra, fa)
    give_a = [gather(fa, ga_s, ga_r, k, me) for k in order]
    for c in give_a:
        c.start()

    has_left = vox > 0
    has_right = vox < nvox - 1
    edge_right.wait_recv()
    edge_left.wait_recv()
    near = jnp.where((j == 1) & has_left, edge_l[...], 0.0) + jnp.where((j == 6) & has_right, pltpu.roll(edge_r[...], 4, 1), 0.0)
    edge_c[...] = near[0:8] + pltpu.roll(near[8:16], 1, 1) + pltpu.roll(near[16:24], 2, 1)

    def spread(k):
        return pltpu.make_async_remote_copy(
            src_ref=edge_c, dst_ref=edge_in.at[k], send_sem=ec_s.at[k], recv_sem=ec_r.at[k],
            device_id={"dir": peer(k)}, device_id_type=MESH)

    send_e = [spread(k) for k in order]
    for c in send_e:
        c.start()

    halo_right.wait_recv()
    halo_left.wait_recv()

    def widen(f):
        at = pl.ds(f * HALF, HALF)
        own = halo[at, :]
        far_l = jnp.where(has_left, halo_l[at, :], 0.0)
        far_r = jnp.where(has_right, halo_r[at, :], 0.0)
        return jnp.where(j < 2, far_l, jnp.where(j < 4, own, pltpu.roll(jnp.where(j < 2, own, far_r), 4, 1)))

    col = jnp.where(j < 4, j - 2, j + 122) + vox * 128
    keep_w = ((col >= 0) & (col < nvox * 128 - 1)).astype(f32)
    rid = lax.rem(lane // 8, 4)
    low_w, high_w = (rid < 3).astype(f32), (rid >= 1).astype(f32)

    def fr_w(x):
        return (pltpu.roll(x, 120, 1) - x) * low_w

    def br_w(x):
        return x * low_w - pltpu.roll(x, 8, 1) * high_w

    def fx_w(x):
        return (pltpu.roll(x, 127, 1) - x) * keep_w

    def bx_w(x):
        return x * keep_w - pltpu.roll(x, 1, 1)

    def shrink(sq, alpha):
        return jnp.minimum(1.0, alpha * lax.rsqrt(sq))

    def norm_w(sq):
        n = jnp.sum(sq, 0, keepdims=True)
        return n + pltpu.roll(n, 64, 1)

    def dual_p_w(pr_, pc_, u_, wr_, wc_):
        a = pr_ + SIGMA * (fr_w(u_) - wr_)
        b = pc_ + SIGMA * (fx_w(u_) - wc_)
        s = shrink(norm_w(a * a + b * b), ALPHA1)
        return a * s, b * s

    def dual_q_w(qa_, qb_, qc_, wr_, wc_):
        a = qa_ + SIGMA * br_w(wr_)
        b = qb_ + SIGMA * bx_w(wc_)
        c = qc_ + (0.5 * SIGMA) * (bx_w(wr_) + br_w(wc_))
        s = shrink(norm_w(a * a + b * b + 2.0 * (c * c)), ALPHA0)
        return a * s, b * s, c * s

    uw, wrw, wcw = widen(0), widen(1), widen(2)
    p1rw, p1cw = dual_p_w(widen(3), widen(4), uw, wrw, wcw)
    q1aw, q1bw, q1cw = dual_q_w(widen(5), widen(6), widen(7), wrw, wcw)
    w1rw = wrw + TAU * (p1rw + fr_w(q1aw) + fx_w(q1cw))
    w1cw = wcw + TAU * (p1cw + fx_w(q1bw) + fr_w(q1cw))
    wbrw, wbcw = 2.0 * w1rw - wrw, 2.0 * w1cw - wcw
    _, q2bw, q2cw = dual_q_w(q1aw, q1bw, q1cw, wbrw, wbcw)
    pbrw, pbcw = p1rw - SIGMA * wbrw, p1cw - SIGMA * wbcw
    ubw = uw + TAU * (br_w(p1rw) + bx_w(p1cw))
    for n, val in enumerate((uw, wrw, wcw, p1cw, q1bw, q1cw, wbrw, wbcw, q2bw, q2cw, pbrw, pbcw, ubw)):
        wk[n] = val

    keep = jnp.where(lane + vox * 128 < nvox * 128 - 1, 1.0, 0.0).astype(f32)

    def beside(val, pr, at):
        parts = [pltpu.roll(val, at - 8 * (h * NR + pr), 1) for h in range(2)]
        return jnp.concatenate(parts, 0)

    def nxt(x, far, pr):
        return jnp.where(lane == 127, beside(far, pr, 121), pltpu.roll(x, 127, 1))

    def prv(x, far, pr):
        return jnp.where(lane == 0, beside(far, pr, 127), pltpu.roll(x, 1, 1))

    def fx(x, far, pr):
        return (nxt(x, far, pr) - x) * keep

    def bx(x, far, pr):
        return x * keep - prv(x, far, pr)

    def fr(x, below, r):
        return below - x if r < 3 else jnp.zeros_like(x)

    def br(x, above, r):
        if r == 0:
            return x
        return x - above if r < 3 else -above

    def colsum(x):
        return jnp.sum(x, 0, keepdims=True)

    def dual_one(p, _):
        for r in range(4):
            pr = 4 * p + r
            u = natural(u0, pr, 1, 0, CP)
            below = natural(u0, pr + 1, 1, 0, CP) if r < 3 else None
            wr, wc = natural(w0, pr, 2, 0, CP), natural(w0, pr, 2, 1, CP)
            a = natural(p0, pr, 2, 0, CP) + SIGMA * (fr(u, below, r) - wr)
            b = natural(p0, pr, 2, 1, CP) + SIGMA * (fx(u, wk[0], pr) - wc)
            s = shrink(colsum(a * a + b * b), ALPHA1)
            p1r[rows_of(pr), :] = a * s
            p1c[rows_of(pr), :] = b * s
            wra = natural(w0, pr - 1, 2, 0, CP) if r > 0 else None
            wca = natural(w0, pr - 1, 2, 1, CP) if r > 0 else None
            a = natural(q0, pr, 3, 0, CP) + SIGMA * br(wr, wra, r)
            b = natural(q0, pr, 3, 1, CP) + SIGMA * bx(wc, wk[2], pr)
            c = natural(q0, pr, 3, 2, CP) + (0.5 * SIGMA) * (bx(wr, wk[1], pr) + br(wc, wca, r))
            s = shrink(colsum(a * a + b * b + 2.0 * (c * c)), ALPHA0)
            q1a[rows_of(pr), :] = a * s
            q1b[rows_of(pr), :] = b * s
            q1c[rows_of(pr), :] = c * s
        return 0

    lax.fori_loop(0, 2, dual_one, 0)

    reduce_chunk(tb, send_b, rb, fb)
    give_b = [gather(fb, gb_s, gb_r, k, me) for k in order]
    for c in give_b:
        c.start()

    def primal_one(p, _):
        for r in range(4):
            pr = 4 * p + r
            here = rows_of(pr)
            pr_, pc_ = p1r[here, :], p1c[here, :]
            above = p1r[rows_of(pr - 1), :] if r > 0 else None
            ub[here, :] = natural(u0, pr, 1, 0, CP) + TAU * (br(pr_, above, r) + bx(pc_, wk[3], pr))
            qa, qb, qc = q1a[here, :], q1b[here, :], q1c[here, :]
            qab = q1a[rows_of(pr + 1), :] if r < 3 else None
            qcb = q1c[rows_of(pr + 1), :] if r < 3 else None
            wr, wc = natural(w0, pr, 2, 0, CP), natural(w0, pr, 2, 1, CP)
            dr = TAU * (pr_ + fr(qa, qab, r) + fx(qc, wk[5], pr))
            dc = TAU * (pc_ + fx(qb, wk[4], pr) + fr(qc, qcb, r))
            nr, nc = wr + 2.0 * dr, wc + 2.0 * dc
            w1r[here, :] = wr + dr
            w1c[here, :] = wc + dc
            wbr[here, :] = nr
            wbc[here, :] = nc
            pbr[here, :] = pr_ - SIGMA * nr
            pbc[here, :] = pc_ - SIGMA * nc
        return 0

    lax.fori_loop(0, 2, primal_one, 0)

    def dual_two(p, _):
        for r in range(4):
            pr = 4 * p + r
            here = rows_of(pr)
            wr, wc = wbr[here, :], wbc[here, :]
            wra = wbr[rows_of(pr - 1), :] if r > 0 else None
            wca = wbc[rows_of(pr - 1), :] if r > 0 else None
            a = q1a[here, :] + SIGMA * br(wr, wra, r)
            b = q1b[here, :] + SIGMA * bx(wc, wk[7], pr)
            c = q1c[here, :] + (0.5 * SIGMA) * (bx(wr, wk[6], pr) + br(wc, wca, r))
            s = shrink(colsum(a * a + b * b + 2.0 * (c * c)), ALPHA0)
            q1a[here, :] = a * s
            q1b[here, :] = b * s
            q1c[here, :] = c * s
        return 0

    lax.fori_loop(0, 2, dual_two, 0)

    def aux_two(p, _):
        for r in range(4):
            pr = 4 * p + r
            here = rows_of(pr)
            qa, qb, qc = q1a[here, :], q1b[here, :], q1c[here, :]
            qab = q1a[rows_of(pr + 1), :] if r < 3 else None
            qcb = q1c[rows_of(pr + 1), :] if r < 3 else None
            v2r[here, :] = w1r[here, :] + TAU * (fr(qa, qab, r) + fx(qc, wk[9], pr))
            v2c[here, :] = w1c[here, :] + TAU * (fx(qb, wk[8], pr) + fr(qc, qcb, r))
        return 0

    lax.fori_loop(0, 2, aux_two, 0)

    take_a = [gather(fa, ga_s, ga_r, k, source(k)) for k in order]
    for c in take_a:
        c.wait_recv()

    def extrapolate(pr, acc):
        here = rows_of(pr)
        new = ub[here, :] - TAU * fa[here, :]
        bar = 2.0 * new - natural(u0, pr, 1, 0, CP)
        u1[here, :] = new
        ub1[here, :] = bar
        return pack_into(acc, bar, pr)

    own_bar = lax.fori_loop(0, NR, extrapolate, zero24)

    total = edge_c[...]
    for c, k in zip(send_e, order):
        c.wait_recv()
        total = total + edge_in[k]
    adj_w = jnp.concatenate([total, pltpu.roll(total, 127, 1), pltpu.roll(total, 126, 1)], 0)
    adj_w = jnp.where((j == 1) | (j == 6), adj_w, 0.0)
    bar_w = 2.0 * (wk[12] - TAU * adj_w) - wk[0]
    bar_w = jnp.where((j == 2) | (j == 3), own_bar, bar_w)
    a = wk[10] + SIGMA * fr_w(bar_w)
    b = wk[11] + SIGMA * fx_w(bar_w)
    s = shrink(norm_w(a * a + b * b), ALPHA1)
    wk[0] = bar_w
    wk[3] = b * s

    def dual_three(p, _):
        for r in range(4):
            pr = 4 * p + r
            here = rows_of(pr)
            u = ub1[here, :]
            below = ub1[rows_of(pr + 1), :] if r < 3 else None
            a = pbr[here, :] + SIGMA * fr(u, below, r)
            b = pbc[here, :] + SIGMA * fx(u, wk[0], pr)
            s = shrink(colsum(a * a + b * b), ALPHA1)
            a, b = a * s, b * s
            p2r[here, :] = a
            p2c[here, :] = b
            wo[pl.ds(pr, CP, stride=2 * NR), :] = v2r[here, :] + TAU * a
            wo[pl.ds(NR + pr, CP, stride=2 * NR), :] = v2c[here, :] + TAU * b
        return 0

    lax.fori_loop(0, 2, dual_three, 0)

    take_b = [gather(fb, gb_s, gb_r, k, source(k)) for k in order]
    for c in take_b:
        c.wait_recv()
    for pr in range(NR):
        hg[pl.ds(3 * pr, 3), :] = fb[pl.ds(pr * CP + NC, CP - NC), :]
    hv = hg[...]
    gh, gl = split(jnp.concatenate([hv, pltpu.roll(hv, 64, 1)], 0)[:, 0:CP])

    def gram_step(i, _):
        bar = jnp.concatenate([ub1[rows_of(2 * i), :], ub1[rows_of(2 * i + 1), :]], 1)
        store_pair(gu, i, mm3(gh, gl, bar))
        return 0

    lax.fori_loop(0, 4, gram_step, 0)

    def primal_two(p, _):
        for r in range(4):
            pr = 4 * p + r
            here = rows_of(pr)
            m = mask[pl.ds(pr, 1), :].astype(f32) * (1.0 / (1.0 + SIGMA))
            adj = m * (fa[here, :] + SIGMA * (gu[here, :] - fb[here, :]))
            above = p2r[rows_of(pr - 1), :] if r > 0 else None
            div = br(p2r[here, :], above, r) + bx(p2c[here, :], wk[3], pr)
            uo[pl.ds(pr, CP, stride=NR), :] = u1[here, :] - TAU * (adj - div)
        return 0

    lax.fori_loop(0, 2, primal_two, 0)

    for c in send_a + send_b + give_a + give_b + send_e + [edge_right, edge_left, halo_right, halo_left]:
        c.wait_send()


def put_kernel(u, w, u_hbm, w_hbm, sem):
    copies = [
        pltpu.make_async_copy(w.at[pl.ds(0, NC * 2 * NR)], w_hbm, sem.at[0]),
        pltpu.make_async_copy(u.at[pl.ds(0, NC * NR)], u_hbm, sem.at[1]),
    ]
    for c in copies:
        c.start()
    for c in copies:
        c.wait()


def body(nvox, signals, basis, response, shell_index, brain_mask, fodf, aux_field, grad_dual, sym_dual, data_dual):
    hbm = pl.BlockSpec(memory_space=pltpu.HBM)
    vmem = pl.BlockSpec(memory_space=pltpu.VMEM)
    field = pltpu.VMEM((NR * CP, 128), f32)
    npeer = SIDE * SIDE
    dma = lambda n: pltpu.SemaphoreType.DMA((n,))
    edges = pltpu.VMEM((HALF, 128), f32)
    halos = pltpu.VMEM((8 * HALF, 128), f32)
    u, w = pl.pallas_call(
        functools.partial(kernel, nvox),
        out_shape=(pltpu.VMEM((NR * CP, 128), f32), pltpu.VMEM((CP * 2 * NR, 128), f32)),
        in_specs=[hbm] * 10,
        out_specs=(vmem, vmem),
        scratch_shapes=[
            pltpu.VMEM((ND * NR, 128), bf16),
            pltpu.VMEM((NC, ND), f32),
            pltpu.VMEM((3, 5), f32),
            pltpu.VMEM((1, ND), jnp.int32),
            pltpu.VMEM((NR, 128), jnp.int32),
            field,
            pltpu.VMEM((CP * 2 * NR, 128), f32),
            pltpu.VMEM((CP * 2 * NR, 128), f32),
            pltpu.VMEM((CP * 3 * NR, 128), f32),
            pltpu.VMEM((ND * NR, 128), f32),
            pltpu.VMEM((ND * NR, 128), f32),
            pltpu.VMEM((CP, 128), f32),
            field, field, field, field,
            pltpu.VMEM((npeer, HALF, 128), f32),
            pltpu.VMEM((npeer, HALF, 128), f32),
            edges,
            halos, halos, halos,
            edges, edges, edges,
            pltpu.VMEM((8, 128), f32),
            pltpu.VMEM((npeer, 8, 128), f32),
            pltpu.VMEM((13, HALF, 128), f32),
        ]
        + [field] * 19
        + [dma(10)]
        + [dma(npeer)] * 10
        + [dma(4), dma(4)],
        compiler_params=pltpu.CompilerParams(
            collective_id=0, has_side_effects=True, vmem_limit_bytes=48 * 1024 * 1024
        ),
    )(*[pltpu.with_memory_space_constraint(x, pltpu.HBM) for x in (
        signals.reshape(ND * NR, 128),
        basis.T,
        response,
        shell_index.reshape(1, ND),
        brain_mask.reshape(NR, 128),
        fodf.reshape(NC * NR, 128),
        aux_field.reshape(NC * 2 * NR, 128),
        grad_dual.reshape(NC * 2 * NR, 128),
        sym_dual.reshape(NC * 3 * NR, 128),
        data_dual.reshape(ND * NR, 128),
    )])
    u, w = pl.pallas_call(
        put_kernel,
        out_shape=(pltpu.HBM((NC * NR, 128), f32), pltpu.HBM((NC * 2 * NR, 128), f32)),
        in_specs=[vmem, vmem],
        out_specs=(hbm, hbm),
        scratch_shapes=[dma(2)],
        compiler_params=pltpu.CompilerParams(vmem_limit_bytes=4 * 1024 * 1024),
    )(pltpu.with_memory_space_constraint(u, pltpu.VMEM), pltpu.with_memory_space_constraint(w, pltpu.VMEM))
    return u.reshape(fodf.shape), w.reshape(aux_field.shape)


def solution(mesh):
    placed = (
        P("dir", None, None, "vox"),
        P("dir", None),
        P(),
        P("dir"),
        P(None, None, "vox"),
        P(None, None, None, "vox"),
        P(None, None, None, None, "vox"),
        P(None, None, None, None, "vox"),
        P(None, None, None, None, "vox"),
        P("dir", None, None, "vox"),
    )
    return jax.shard_map(
        functools.partial(body, mesh.shape["vox"]),
        mesh=mesh,
        in_specs=placed,
        out_specs=(P(None, None, None, "vox"), P(None, None, None, None, "vox")),
        check_vma=False,
    )
```

```python
import functools

import jax
import jax.numpy as jnp
import numpy as np
from jax import lax
from jax.experimental import pallas as pl
from jax.experimental.pallas import tpu as pltpu
from jax.sharding import PartitionSpec as P

MESH = pl.DeviceIdType.MESH
f32 = jnp.float32
bf16 = jnp.bfloat16

SIGMA = 0.25
TAU = 0.3
ALPHA1 = 1.0
ALPHA0 = 1.5
ORDER_STARTS = (1, 6, 15, 28)

NC = 45
CP = 48
HALF = 24
ND = 72
NR = 8
SIDE = 4


def split(x):
    hi = x.astype(bf16)
    return hi, (x - hi.astype(f32)).astype(bf16)


def mm(a, b):
    return jnp.dot(a, b, preferred_element_type=f32)


def mm3(ah, al, x):
    xh, xl = split(x)
    return mm(ah, xh) + mm(ah, xl) + mm(al, xh)


def rows_of(pr):
    start = pr * CP
    return pl.ds(start if isinstance(start, int) else pl.multiple_of(start, 8), CP)


def kernel(
    nvox,
    sig_hbm, basis_hbm, resp_hbm, shell_hbm, mask_hbm, fodf_hbm, aux_hbm, grad_hbm, sym_hbm, dual_hbm,
    uo, wo,
    sig, basis, resp, shell, mask, u0, w0, p0, q0, y0, sigf,
    kt, ta, tb, fa, fb, ra, rb, hg,
    halo, halo_l, halo_r, edge, edge_l, edge_r, edge_c, edge_in, wk,
    p1r, p1c, q1a, q1b, q1c, wbr, wbc, w1r, w1c, pbr, pbc, ub, v2r, v2c, u1, gu, p2r, p2c,
    in_sem, dir_s, dir_r, vox_s, vox_r,
):
    me = lax.axis_index("dir")
    vox = lax.axis_index("vox")
    mx, my = me // SIDE, lax.rem(me, SIDE)
    npeer = SIDE * SIDE
    order = sorted(range(1, npeer), key=lambda k: -(min(k // SIDE, SIDE - k // SIDE) + min(k % SIDE, SIDE - k % SIDE)))

    def peer(k):
        return lax.rem(mx + k // SIDE, SIDE) * SIDE + lax.rem(my + k % SIDE, SIDE)

    has_left, has_right = vox > 0, vox < nvox - 1
    left, right = vox - 1, vox + 1

    def load(i, src, dst):
        return pltpu.make_async_copy(src, dst, in_sem.at[i])

    loads = [
        load(0, basis_hbm, basis),
        load(1, resp_hbm, resp),
        load(2, shell_hbm, shell),
        load(3, mask_hbm, mask),
        load(4, fodf_hbm, u0.at[pl.ds(0, NC * NR)]),
        load(5, sig_hbm, sig),
        load(6, dual_hbm, y0),
        load(7, aux_hbm, w0.at[pl.ds(0, NC * 2 * NR)]),
        load(8, grad_hbm, p0.at[pl.ds(0, NC * 2 * NR)]),
        load(9, sym_hbm, q0.at[pl.ds(0, NC * 3 * NR)]),
    ]
    barrier = pltpu.get_barrier_semaphore()
    for k in order:
        pl.semaphore_signal(barrier, inc=1, device_id={"dir": peer(k)}, device_id_type=MESH)
    for there, n in ((has_left, left), (has_right, right)):

        @pl.when(there)
        def _():
            pl.semaphore_signal(barrier, inc=1, device_id={"vox": n}, device_id_type=MESH)

    for c in loads[:7]:
        c.start()

    lane = lax.broadcasted_iota(jnp.int32, (1, 128), 1)
    for ref, n in ((u0, 1), (w0, 2), (p0, 2), (q0, 3)):
        ref[pl.ds(NC * n * NR, (CP - NC) * n * NR), :] = jnp.zeros(((CP - NC) * n * NR, 128), f32)

    for c in loads[:3]:
        c.wait()
    kt[...] = jnp.zeros((CP, 128), f32)
    sh = shell[...]
    per_order = [
        jnp.where(sh == 0, resp[0:1, o : o + 1], jnp.where(sh == 1, resp[1:2, o : o + 1], resp[2:3, o : o + 1]))
        for o in range(5)
    ]
    cid = lax.broadcasted_iota(jnp.int32, (NC, 1), 0)
    scale = jnp.broadcast_to(per_order[0], (NC, ND))
    for o, start in enumerate(ORDER_STARTS):
        scale = jnp.where(cid >= start, per_order[o + 1], scale)
    kt[pl.ds(0, NC), pl.ds(0, ND)] = basis[...] * scale
    ktv = kt[...]
    knv = jnp.concatenate([ktv, jnp.zeros((128 - CP, 128), f32)], 0).T[0:ND]
    kth, ktl = split(ktv[:, 0:ND])
    knh128, knl128 = split(knv)
    knh, knl = knh128[:, 0:CP], knl128[:, 0:CP]

    for c in loads[7:]:
        c.start()
    gram = mm3(kth, ktl, knv)
    hg[...] = gram[0:HALF] + pltpu.roll(gram[HALF:CP], 64, 1)
    for c in loads[3:7]:
        c.wait()

    def to_f32(i, _):
        at = pl.ds(pl.multiple_of(i * 96, 96), 96)
        sigf[at, :] = sig[at, :].astype(f32)
        return 0

    lax.fori_loop(0, 6, to_f32, 0)

    def natural(ref, pr, n, comp, count):
        return ref[pl.ds(comp * NR + pr, count, stride=n * NR), :]

    def pair(ref, i, count):
        return jnp.concatenate([natural(ref, 2 * i, 1, 0, count), natural(ref, 2 * i + 1, 1, 0, count)], 1)

    def store_pair(ref, i, val):
        ref[rows_of(2 * i), :] = val[:, 0:128]
        ref[rows_of(2 * i + 1), :] = val[:, 128:256]

    def data_step(i, _):
        pred = mm3(knh, knl, pair(u0, i, CP))
        m = jnp.concatenate([mask[pl.ds(2 * i, 1), :], mask[pl.ds(2 * i + 1, 1), :]], 1).astype(f32)
        y = (m * (1.0 / (1.0 + SIGMA))) * (pair(y0, i, ND) + SIGMA * (pred - pair(sigf, i, ND)))
        store_pair(ta, i, mm3(kth, ktl, y))
        return 0

    lax.fori_loop(0, 4, data_step, 0, unroll=True)

    for pr in range(NR):
        ta[pl.ds(pr * CP + NC, CP - NC), :] = hg[pl.ds(3 * pr, 3), :]

    def chunk(d):
        return pl.ds(pl.multiple_of(d * HALF, HALF), HALF)

    def scatter(src, dst, n):
        return [
            pltpu.make_async_remote_copy(
                src_ref=src.at[chunk(peer(k))], dst_ref=dst.at[i], send_sem=dir_s.at[n], recv_sem=dir_r.at[n],
                device_id={"dir": peer(k)}, device_id_type=MESH)
            for i, k in enumerate(order)
        ]

    def gather(ref, n):
        return [
            pltpu.make_async_remote_copy(
                src_ref=ref.at[chunk(me)], dst_ref=ref.at[chunk(me)], send_sem=dir_s.at[n], recv_sem=dir_r.at[n],
                device_id={"dir": peer(k)}, device_id_type=MESH)
            for k in order
        ]

    def wait_all(sem, ref):
        pltpu.make_async_copy(ref, ref, sem).wait()

    def to_vox(src, dst, n, k):
        return pltpu.make_async_remote_copy(
            src_ref=src, dst_ref=dst, send_sem=vox_s.at[k], recv_sem=vox_r.at[k],
            device_id={"vox": n}, device_id_type=MESH)

    def start_vox(to_right, to_left):
        @pl.when(has_right)
        def _():
            to_right.start()

        @pl.when(has_left)
        def _():
            to_left.start()

    def arrive_vox(to_right, to_left):
        @pl.when(has_left)
        def _():
            to_right.wait_recv()

        @pl.when(has_right)
        def _():
            to_left.wait_recv()

    others = npeer - 1
    slots = pl.ds(0, others)
    rows_in = pl.ds(0, others * HALF)
    pl.semaphore_wait(barrier, others + has_left.astype(jnp.int32) + has_right.astype(jnp.int32))
    for c in scatter(ta, ra, 0):
        c.start()

    slot_of = lane // 8
    j = lax.rem(lane, 8)

    def pack_into(acc, val, pr):
        for h in range(2):
            s = h * NR + pr
            t = pltpu.roll(val[h * HALF : (h + 1) * HALF], 8 * s + 2 if isinstance(s, int) and 8 * s + 2 < 128 else lax.rem(8 * s + 2, 128), 1)
            acc = jnp.where(slot_of == s, t, acc)
        return acc

    zero24 = jnp.zeros((HALF, 128), f32)
    edge[...] = lax.fori_loop(0, NR, lambda pr, acc: pack_into(acc, ta[rows_of(pr), :], pr), zero24)
    edges = to_vox(edge, edge_l, right, 0), to_vox(edge, edge_r, left, 1)
    start_vox(*edges)

    def signal_step(i, _):
        s = pair(sigf, i, ND).astype(bf16)
        store_pair(tb, i, mm(kth, s) + mm(ktl, s))
        return 0

    lax.fori_loop(0, 4, signal_step, 0)
    for c in scatter(tb, rb, 1):
        c.start()

    for c in loads[7:]:
        c.wait()

    fields = ((u0, 1, 0), (w0, 2, 0), (w0, 2, 1), (p0, 2, 0), (p0, 2, 1), (q0, 3, 0), (q0, 3, 1), (q0, 3, 2))

    def pack_step(pr, accs):
        return tuple(pack_into(acc, natural(ref, pr, n, comp, CP), pr) for acc, (ref, n, comp) in zip(accs, fields))

    packed = lax.fori_loop(0, NR, pack_step, (zero24,) * 8)
    for f in range(8):
        halo[pl.ds(f * HALF, HALF), :] = packed[f]
    halos = to_vox(halo, halo_l, right, 2), to_vox(halo, halo_r, left, 3)
    start_vox(*halos)

    arrive_vox(*edges)
    near = (
        jnp.where((j == 1) & has_left, edge_l[...], 0.0)
        + jnp.where(j == 2, edge[...], 0.0)
        + jnp.where((j == 6) & has_right, pltpu.roll(edge_r[...], 4, 1), 0.0)
    )
    edge_c[pl.ds(0, 8), :] = near[0:8] + pltpu.roll(near[8:16], 2, 1)
    edge_c[pl.ds(8, 8), :] = near[16:24]
    for i, k in enumerate(order):
        pltpu.make_async_remote_copy(
            src_ref=edge_c, dst_ref=edge_in.at[i], send_sem=dir_s.at[4], recv_sem=dir_r.at[4],
            device_id={"dir": peer(k)}, device_id_type=MESH).start()

    def reduce_chunk(src, recv, n, full):
        wait_all(dir_r.at[n], recv.at[slots])
        total = src[chunk(me), :]
        for i in range(others):
            total = total + recv[i]
        full[chunk(me), :] = total
        for c in gather(full, n + 2):
            c.start()

    reduce_chunk(ta, ra, 0, fa)

    arrive_vox(*halos)

    def widen(f):
        at = pl.ds(f * HALF, HALF)
        own = halo[at, :]
        far_l = jnp.where(has_left, halo_l[at, :], 0.0)
        far_r = jnp.where(has_right, halo_r[at, :], 0.0)
        return jnp.where(j < 2, far_l, jnp.where(j < 4, own, pltpu.roll(jnp.where(j < 2, own, far_r), 4, 1)))

    col = jnp.where(j < 4, j - 2, j + 122) + vox * 128
    keep_w = ((col >= 0) & (col < nvox * 128 - 1)).astype(f32)
    rid = lax.rem(lane // 8, 4)
    low_w, high_w = (rid < 3).astype(f32), (rid >= 1).astype(f32)

    def fr_w(x):
        return (pltpu.roll(x, 120, 1) - x) * low_w

    def br_w(x):
        return x * low_w - pltpu.roll(x, 8, 1) * high_w

    def fx_w(x):
        return (pltpu.roll(x, 127, 1) - x) * keep_w

    def bx_w(x):
        return x * keep_w - pltpu.roll(x, 1, 1)

    def shrink(sq, alpha):
        return jnp.minimum(1.0, alpha * lax.rsqrt(sq))

    def norm_w(sq):
        n = jnp.sum(sq, 0, keepdims=True)
        return n + pltpu.roll(n, 64, 1)

    def dual_p_w(pr_, pc_, u_, wr_, wc_):
        a = pr_ + SIGMA * (fr_w(u_) - wr_)
        b = pc_ + SIGMA * (fx_w(u_) - wc_)
        s = shrink(norm_w(a * a + b * b), ALPHA1)
        return a * s, b * s

    def dual_q_w(qa_, qb_, qc_, wr_, wc_):
        a = qa_ + SIGMA * br_w(wr_)
        b = qb_ + SIGMA * bx_w(wc_)
        c = qc_ + (0.5 * SIGMA) * (bx_w(wr_) + br_w(wc_))
        s = shrink(norm_w(a * a + b * b + 2.0 * (c * c)), ALPHA0)
        return a * s, b * s, c * s

    uw, wrw, wcw = widen(0), widen(1), widen(2)
    p1rw, p1cw = dual_p_w(widen(3), widen(4), uw, wrw, wcw)
    q1aw, q1bw, q1cw = dual_q_w(widen(5), widen(6), widen(7), wrw, wcw)
    w1rw = wrw + TAU * (p1rw + fr_w(q1aw) + fx_w(q1cw))
    w1cw = wcw + TAU * (p1cw + fx_w(q1bw) + fr_w(q1cw))
    wbrw, wbcw = 2.0 * w1rw - wrw, 2.0 * w1cw - wcw
    _, q2bw, q2cw = dual_q_w(q1aw, q1bw, q1cw, wbrw, wbcw)
    pbrw, pbcw = p1rw - SIGMA * wbrw, p1cw - SIGMA * wbcw
    ubw = uw + TAU * (br_w(p1rw) + bx_w(p1cw))
    for n, val in enumerate((uw, wrw, wcw, p1cw, q1bw, q1cw, wbrw, wbcw, q2bw, q2cw, pbrw, pbcw, ubw)):
        wk[n] = val

    reduce_chunk(tb, rb, 1, fb)

    keep = jnp.where(lane + vox * 128 < nvox * 128 - 1, 1.0, 0.0).astype(f32)

    def beside(val, pr, at):
        parts = [pltpu.roll(val, at - 8 * (h * NR + pr), 1) for h in range(2)]
        return jnp.concatenate(parts, 0)

    def nxt(x, far, pr):
        return jnp.where(lane == 127, beside(far, pr, 121), pltpu.roll(x, 127, 1))

    def prv(x, far, pr):
        return jnp.where(lane == 0, beside(far, pr, 127), pltpu.roll(x, 1, 1))

    def fx(x, far, pr):
        return (nxt(x, far, pr) - x) * keep

    def bx(x, far, pr):
        return x * keep - prv(x, far, pr)

    def fr(x, below, r):
        return below - x if r < 3 else jnp.zeros_like(x)

    def br(x, above, r):
        if r == 0:
            return x
        return x - above if r < 3 else -above

    def colsum(x):
        return jnp.sum(x, 0, keepdims=True)

    def dual_one(p, _):
        for r in range(4):
            pr = 4 * p + r
            u = natural(u0, pr, 1, 0, CP)
            below = natural(u0, pr + 1, 1, 0, CP) if r < 3 else None
            wr, wc = natural(w0, pr, 2, 0, CP), natural(w0, pr, 2, 1, CP)
            a = natural(p0, pr, 2, 0, CP) + SIGMA * (fr(u, below, r) - wr)
            b = natural(p0, pr, 2, 1, CP) + SIGMA * (fx(u, wk[0], pr) - wc)
            s = shrink(colsum(a * a + b * b), ALPHA1)
            p1r[rows_of(pr), :] = a * s
            p1c[rows_of(pr), :] = b * s
            wra = natural(w0, pr - 1, 2, 0, CP) if r > 0 else None
            wca = natural(w0, pr - 1, 2, 1, CP) if r > 0 else None
            a = natural(q0, pr, 3, 0, CP) + SIGMA * br(wr, wra, r)
            b = natural(q0, pr, 3, 1, CP) + SIGMA * bx(wc, wk[2], pr)
            c = natural(q0, pr, 3, 2, CP) + (0.5 * SIGMA) * (bx(wr, wk[1], pr) + br(wc, wca, r))
            s = shrink(colsum(a * a + b * b + 2.0 * (c * c)), ALPHA0)
            q1a[rows_of(pr), :] = a * s
            q1b[rows_of(pr), :] = b * s
            q1c[rows_of(pr), :] = c * s
        return 0

    lax.fori_loop(0, 2, dual_one, 0)


    def primal_one(p, _):
        for r in range(4):
            pr = 4 * p + r
            here = rows_of(pr)
            pr_, pc_ = p1r[here, :], p1c[here, :]
            above = p1r[rows_of(pr - 1), :] if r > 0 else None
            ub[here, :] = natural(u0, pr, 1, 0, CP) + TAU * (br(pr_, above, r) + bx(pc_, wk[3], pr))
            qa, qb, qc = q1a[here, :], q1b[here, :], q1c[here, :]
            qab = q1a[rows_of(pr + 1), :] if r < 3 else None
            qcb = q1c[rows_of(pr + 1), :] if r < 3 else None
            wr, wc = natural(w0, pr, 2, 0, CP), natural(w0, pr, 2, 1, CP)
            dr = TAU * (pr_ + fr(qa, qab, r) + fx(qc, wk[5], pr))
            dc = TAU * (pc_ + fx(qb, wk[4], pr) + fr(qc, qcb, r))
            nr, nc = wr + 2.0 * dr, wc + 2.0 * dc
            w1r[here, :] = wr + dr
            w1c[here, :] = wc + dc
            wbr[here, :] = nr
            wbc[here, :] = nc
            pbr[here, :] = pr_ - SIGMA * nr
            pbc[here, :] = pc_ - SIGMA * nc
        return 0

    lax.fori_loop(0, 2, primal_one, 0)

    def dual_two(p, _):
        for r in range(4):
            pr = 4 * p + r
            here = rows_of(pr)
            wr, wc = wbr[here, :], wbc[here, :]
            wra = wbr[rows_of(pr - 1), :] if r > 0 else None
            wca = wbc[rows_of(pr - 1), :] if r > 0 else None
            a = q1a[here, :] + SIGMA * br(wr, wra, r)
            b = q1b[here, :] + SIGMA * bx(wc, wk[7], pr)
            c = q1c[here, :] + (0.5 * SIGMA) * (bx(wr, wk[6], pr) + br(wc, wca, r))
            s = shrink(colsum(a * a + b * b + 2.0 * (c * c)), ALPHA0)
            q1a[here, :] = a * s
            q1b[here, :] = b * s
            q1c[here, :] = c * s
        return 0

    lax.fori_loop(0, 2, dual_two, 0)

    def aux_two(p, _):
        for r in range(4):
            pr = 4 * p + r
            here = rows_of(pr)
            qa, qb, qc = q1a[here, :], q1b[here, :], q1c[here, :]
            qab = q1a[rows_of(pr + 1), :] if r < 3 else None
            qcb = q1c[rows_of(pr + 1), :] if r < 3 else None
            v2r[here, :] = w1r[here, :] + TAU * (fr(qa, qab, r) + fx(qc, wk[9], pr))
            v2c[here, :] = w1c[here, :] + TAU * (fx(qb, wk[8], pr) + fr(qc, qcb, r))
        return 0

    lax.fori_loop(0, 2, aux_two, 0)

    wait_all(dir_r.at[4], edge_in.at[slots])
    total = edge_c[...]
    for i in range(others):
        total = total + edge_in[i]
    adj_w = jnp.concatenate([total[0:8], pltpu.roll(total[0:8], 126, 1), total[8:16]], 0)
    row24 = lax.broadcasted_iota(jnp.int32, (HALF, 1), 0)
    adj_w = jnp.where(((j == 1) | (j == 2) | (j == 6)) & ((row24 < NC - HALF) | (lane < 64)), adj_w, 0.0)
    bar_w = 2.0 * (wk[12] - TAU * adj_w) - wk[0]
    a = wk[10] + SIGMA * fr_w(bar_w)
    b = wk[11] + SIGMA * fx_w(bar_w)
    s = shrink(norm_w(a * a + b * b), ALPHA1)
    wk[0] = bar_w
    wk[3] = b * s

    wait_all(dir_r.at[2], fa.at[rows_in])
    for pr in range(NR):
        hg[pl.ds(3 * pr, 3), :] = fa[pl.ds(pr * CP + NC, CP - NC), :]
    hv = hg[...]
    gh, gl = split(jnp.concatenate([hv, pltpu.roll(hv, 64, 1)], 0)[:, 0:CP])
    real = lax.broadcasted_iota(jnp.int32, (CP, 1), 0) < NC

    def dual_three(p, _):
        bars = []
        for r in range(4):
            pr = 4 * p + r
            here = rows_of(pr)
            new = ub[here, :] - TAU * jnp.where(real, fa[here, :], 0.0)
            u1[here, :] = new
            bars.append(2.0 * new - natural(u0, pr, 1, 0, CP))
        for i in range(2):
            store_pair(gu, 2 * p + i, mm3(gh, gl, jnp.concatenate(bars[2 * i : 2 * i + 2], 1)))
        for r in range(4):
            pr = 4 * p + r
            here = rows_of(pr)
            a = pbr[here, :] + SIGMA * fr(bars[r], bars[r + 1] if r < 3 else None, r)
            b = pbc[here, :] + SIGMA * fx(bars[r], wk[0], pr)
            s = shrink(colsum(a * a + b * b), ALPHA1)
            a, b = a * s, b * s
            p2r[here, :] = a
            p2c[here, :] = b
            wo[pl.ds(pr, CP, stride=2 * NR), :] = v2r[here, :] + TAU * a
            wo[pl.ds(NR + pr, CP, stride=2 * NR), :] = v2c[here, :] + TAU * b
        return 0

    lax.fori_loop(0, 2, dual_three, 0)
    wait_all(dir_r.at[3], fb.at[rows_in])

    def primal_two(p, _):
        for r in range(4):
            pr = 4 * p + r
            here = rows_of(pr)
            m = mask[pl.ds(pr, 1), :].astype(f32) * (1.0 / (1.0 + SIGMA))
            adj = m * (fa[here, :] + SIGMA * (gu[here, :] - fb[here, :]))
            above = p2r[rows_of(pr - 1), :] if r > 0 else None
            div = br(p2r[here, :], above, r) + bx(p2c[here, :], wk[3], pr)
            uo[pl.ds(pr, CP, stride=NR), :] = u1[here, :] - TAU * (adj - div)
        return 0

    lax.fori_loop(0, 2, primal_two, 0)

    wait_all(dir_s.at[0], ra.at[slots])
    wait_all(dir_s.at[1], rb.at[slots])
    wait_all(dir_s.at[2], fa.at[rows_in])
    wait_all(dir_s.at[3], fb.at[rows_in])
    wait_all(dir_s.at[4], edge_in.at[slots])
    for to_right, to_left in (edges, halos):

        @pl.when(has_right)
        def _():
            to_right.wait_send()

        @pl.when(has_left)
        def _():
            to_left.wait_send()


def put_kernel(u, w, u_hbm, w_hbm, sem):
    copies = [
        pltpu.make_async_copy(w.at[pl.ds(0, NC * 2 * NR)], w_hbm, sem.at[0]),
        pltpu.make_async_copy(u.at[pl.ds(0, NC * NR)], u_hbm, sem.at[1]),
    ]
    for c in copies:
        c.start()
    for c in copies:
        c.wait()


def body(nvox, signals, basis, response, shell_index, brain_mask, fodf, aux_field, grad_dual, sym_dual, data_dual):
    hbm = pl.BlockSpec(memory_space=pltpu.HBM)
    vmem = pl.BlockSpec(memory_space=pltpu.VMEM)
    field = pltpu.VMEM((NR * CP, 128), f32)
    npeer = SIDE * SIDE
    dma = lambda n: pltpu.SemaphoreType.DMA((n,))
    edges = pltpu.VMEM((HALF, 128), f32)
    halos = pltpu.VMEM((8 * HALF, 128), f32)
    u, w = pl.pallas_call(
        functools.partial(kernel, nvox),
        out_shape=(pltpu.VMEM((NR * CP, 128), f32), pltpu.VMEM((CP * 2 * NR, 128), f32)),
        in_specs=[hbm] * 10,
        out_specs=(vmem, vmem),
        scratch_shapes=[
            pltpu.VMEM((ND * NR, 128), bf16),
            pltpu.VMEM((NC, ND), f32),
            pltpu.VMEM((3, 5), f32),
            pltpu.VMEM((1, ND), jnp.int32),
            pltpu.VMEM((NR, 128), jnp.int32),
            field,
            pltpu.VMEM((CP * 2 * NR, 128), f32),
            pltpu.VMEM((CP * 2 * NR, 128), f32),
            pltpu.VMEM((CP * 3 * NR, 128), f32),
            pltpu.VMEM((ND * NR, 128), f32),
            pltpu.VMEM((ND * NR, 128), f32),
            pltpu.VMEM((CP, 128), f32),
            field, field, field, field,
            pltpu.VMEM((npeer, HALF, 128), f32),
            pltpu.VMEM((npeer, HALF, 128), f32),
            edges,
            halos, halos, halos,
            edges, edges, edges,
            pltpu.VMEM((16, 128), f32),
            pltpu.VMEM((npeer, 16, 128), f32),
            pltpu.VMEM((13, HALF, 128), f32),
        ]
        + [field] * 18
        + [dma(10)]
        + [dma(5), dma(5), dma(4), dma(4)],
        compiler_params=pltpu.CompilerParams(
            collective_id=0, has_side_effects=True, vmem_limit_bytes=48 * 1024 * 1024
        ),
    )(*[pltpu.with_memory_space_constraint(x, pltpu.HBM) for x in (
        signals.reshape(ND * NR, 128),
        basis.T,
        response,
        shell_index.reshape(1, ND),
        brain_mask.reshape(NR, 128),
        fodf.reshape(NC * NR, 128),
        aux_field.reshape(NC * 2 * NR, 128),
        grad_dual.reshape(NC * 2 * NR, 128),
        sym_dual.reshape(NC * 3 * NR, 128),
        data_dual.reshape(ND * NR, 128),
    )])
    u, w = pl.pallas_call(
        put_kernel,
        out_shape=(pltpu.HBM((NC * NR, 128), f32), pltpu.HBM((NC * 2 * NR, 128), f32)),
        in_specs=[vmem, vmem],
        out_specs=(hbm, hbm),
        scratch_shapes=[dma(2)],
        compiler_params=pltpu.CompilerParams(vmem_limit_bytes=4 * 1024 * 1024),
    )(pltpu.with_memory_space_constraint(u, pltpu.VMEM), pltpu.with_memory_space_constraint(w, pltpu.VMEM))
    return u.reshape(fodf.shape), w.reshape(aux_field.shape)


def solution(mesh):
    placed = (
        P("dir", None, None, "vox"),
        P("dir", None),
        P(),
        P("dir"),
        P(None, None, "vox"),
        P(None, None, None, "vox"),
        P(None, None, None, None, "vox"),
        P(None, None, None, None, "vox"),
        P(None, None, None, None, "vox"),
        P("dir", None, None, "vox"),
    )
    return jax.shard_map(
        functools.partial(body, mesh.shape["vox"]),
        mesh=mesh,
        in_specs=placed,
        out_specs=(P(None, None, None, "vox"), P(None, None, None, None, "vox")),
        check_vma=False,
    )
```

```python
import functools

import jax
import jax.numpy as jnp
import numpy as np
from jax import lax
from jax.experimental import pallas as pl
from jax.experimental.pallas import tpu as pltpu
from jax.sharding import PartitionSpec as P

MESH = pl.DeviceIdType.MESH
f32 = jnp.float32
bf16 = jnp.bfloat16

SIGMA = 0.25
TAU = 0.3
ALPHA1 = 1.0
ALPHA0 = 1.5
ORDER_STARTS = (1, 6, 15, 28)

NC = 45
CP = 48
HALF = 24
ND = 72
NR = 8
SIDE = 4


def split(x):
    hi = x.astype(bf16)
    return hi, (x - hi.astype(f32)).astype(bf16)


def mm(a, b):
    return jnp.dot(a, b, preferred_element_type=f32)


def mm3(ah, al, x):
    xh, xl = split(x)
    return mm(ah, xh) + mm(ah, xl) + mm(al, xh)


def rows_of(pr):
    start = pr * CP
    return pl.ds(start if isinstance(start, int) else pl.multiple_of(start, 8), CP)


def kernel(
    nvox,
    sig_hbm, basis_hbm, resp_hbm, shell_hbm, mask_hbm, fodf_hbm, aux_hbm, grad_hbm, sym_hbm, dual_hbm,
    uo, wo,
    sig, basis, resp, shell, mask, u0, w0, p0, q0, y0, sigf,
    kt, ta, tb, fa, fb, ra, rb, hg,
    halo, halo_l, halo_r, edge, edge_l, edge_r, edge_c, edge_in, wk,
    p1r, p1c, q1a, q1b, q1c, wbr, wbc, w1r, w1c, pbr, pbc, ub, v2r, v2c, u1, gu, p2r, p2c,
    in_sem, dir_s, dir_r, vox_s, vox_r,
):
    me = lax.axis_index("dir")
    vox = lax.axis_index("vox")
    mx, my = me // SIDE, lax.rem(me, SIDE)
    npeer = SIDE * SIDE
    order = sorted(range(1, npeer), key=lambda k: -(min(k // SIDE, SIDE - k // SIDE) + min(k % SIDE, SIDE - k % SIDE)))

    def peer(k):
        return lax.rem(mx + k // SIDE, SIDE) * SIDE + lax.rem(my + k % SIDE, SIDE)

    has_left, has_right = vox > 0, vox < nvox - 1
    left, right = vox - 1, vox + 1

    def load(i, src, dst):
        return pltpu.make_async_copy(src, dst, in_sem.at[i])

    loads = [
        load(0, basis_hbm, basis),
        load(1, resp_hbm, resp),
        load(2, shell_hbm, shell),
        load(3, mask_hbm, mask),
        load(4, fodf_hbm, u0.at[pl.ds(0, NC * NR)]),
        load(5, sig_hbm, sig),
        load(6, dual_hbm, y0),
        load(7, aux_hbm, w0.at[pl.ds(0, NC * 2 * NR)]),
        load(8, grad_hbm, p0.at[pl.ds(0, NC * 2 * NR)]),
        load(9, sym_hbm, q0.at[pl.ds(0, NC * 3 * NR)]),
    ]
    for c in loads[:7]:
        c.start()
    barrier = pltpu.get_barrier_semaphore()
    for k in order:
        pl.semaphore_signal(barrier, inc=1, device_id={"dir": peer(k)}, device_id_type=MESH)
    for there, n in ((has_left, left), (has_right, right)):

        @pl.when(there)
        def _():
            pl.semaphore_signal(barrier, inc=1, device_id={"vox": n}, device_id_type=MESH)


    lane = lax.broadcasted_iota(jnp.int32, (1, 128), 1)
    for ref, n in ((u0, 1), (w0, 2), (p0, 2), (q0, 3)):
        ref[pl.ds(NC * n * NR, (CP - NC) * n * NR), :] = jnp.zeros(((CP - NC) * n * NR, 128), f32)

    for c in loads[:3]:
        c.wait()
    kt[...] = jnp.zeros((CP, 128), f32)
    sh = shell[...]
    per_order = [
        jnp.where(sh == 0, resp[0:1, o : o + 1], jnp.where(sh == 1, resp[1:2, o : o + 1], resp[2:3, o : o + 1]))
        for o in range(5)
    ]
    cid = lax.broadcasted_iota(jnp.int32, (NC, 1), 0)
    scale = jnp.broadcast_to(per_order[0], (NC, ND))
    for o, start in enumerate(ORDER_STARTS):
        scale = jnp.where(cid >= start, per_order[o + 1], scale)
    kt[pl.ds(0, NC), pl.ds(0, ND)] = basis[...] * scale
    ktv = kt[...]
    knv = jnp.concatenate([ktv, jnp.zeros((128 - CP, 128), f32)], 0).T[0:ND]
    kth, ktl = split(ktv[:, 0:ND])
    knh128, knl128 = split(knv)
    knh, knl = knh128[:, 0:CP], knl128[:, 0:CP]

    for c in loads[7:]:
        c.start()
    gram = mm3(kth, ktl, knv)
    hg[...] = gram[0:HALF] + pltpu.roll(gram[HALF:CP], 64, 1)
    for c in loads[3:7]:
        c.wait()

    def to_f32(i, _):
        at = pl.ds(pl.multiple_of(i * 96, 96), 96)
        sigf[at, :] = sig[at, :].astype(f32)
        return 0

    lax.fori_loop(0, 6, to_f32, 0)

    def natural(ref, pr, n, comp, count):
        return ref[pl.ds(comp * NR + pr, count, stride=n * NR), :]

    def pair(ref, i, count):
        return jnp.concatenate([natural(ref, 2 * i, 1, 0, count), natural(ref, 2 * i + 1, 1, 0, count)], 1)

    def store_pair(ref, i, val):
        ref[rows_of(2 * i), :] = val[:, 0:128]
        ref[rows_of(2 * i + 1), :] = val[:, 128:256]

    def data_step(i, _):
        pred = mm3(knh, knl, pair(u0, i, CP))
        m = jnp.concatenate([mask[pl.ds(2 * i, 1), :], mask[pl.ds(2 * i + 1, 1), :]], 1).astype(f32)
        y = (m * (1.0 / (1.0 + SIGMA))) * (pair(y0, i, ND) + SIGMA * (pred - pair(sigf, i, ND)))
        store_pair(ta, i, mm3(kth, ktl, y))
        return 0

    lax.fori_loop(0, 4, data_step, 0, unroll=True)

    for pr in range(NR):
        ta[pl.ds(pr * CP + NC, CP - NC), :] = hg[pl.ds(3 * pr, 3), :]

    def signal_step(i, _):
        s = pair(sigf, i, ND).astype(bf16)
        store_pair(tb, i, mm(kth, s) + mm(ktl, s))
        return 0

    lax.fori_loop(0, 4, signal_step, 0, unroll=True)
    def chunk(d):
        return pl.ds(pl.multiple_of(d * HALF, HALF), HALF)

    def scatter(src, dst, n):
        return [
            pltpu.make_async_remote_copy(
                src_ref=src.at[chunk(peer(k))], dst_ref=dst.at[i], send_sem=dir_s.at[n], recv_sem=dir_r.at[n],
                device_id={"dir": peer(k)}, device_id_type=MESH)
            for i, k in enumerate(order)
        ]

    def gather(ref, n):
        return [
            pltpu.make_async_remote_copy(
                src_ref=ref.at[chunk(me)], dst_ref=ref.at[chunk(me)], send_sem=dir_s.at[n], recv_sem=dir_r.at[n],
                device_id={"dir": peer(k)}, device_id_type=MESH)
            for k in order
        ]

    def wait_all(sem, ref):
        pltpu.make_async_copy(ref, ref, sem).wait()

    def to_vox(src, dst, n, k):
        return pltpu.make_async_remote_copy(
            src_ref=src, dst_ref=dst, send_sem=vox_s.at[k], recv_sem=vox_r.at[k],
            device_id={"vox": n}, device_id_type=MESH)

    def start_vox(to_right, to_left):
        @pl.when(has_right)
        def _():
            to_right.start()

        @pl.when(has_left)
        def _():
            to_left.start()

    def arrive_vox(to_right, to_left):
        @pl.when(has_left)
        def _():
            to_right.wait_recv()

        @pl.when(has_right)
        def _():
            to_left.wait_recv()

    others = npeer - 1
    slots = pl.ds(0, others)
    rows_in = pl.ds(0, others * HALF)
    pl.semaphore_wait(barrier, others + has_left.astype(jnp.int32) + has_right.astype(jnp.int32))
    far = [min(k // SIDE, SIDE - k // SIDE) + min(k % SIDE, SIDE - k % SIDE) for k in order]
    sends = scatter(ta, ra, 0), scatter(tb, rb, 1)
    for n, least, most in ((0, 2, 4), (1, 3, 4), (0, 1, 1), (1, 2, 2), (1, 1, 1)):
        for c, hops in zip(sends[n], far):
            if least <= hops <= most:
                c.start()

    slot_of = lane // 8
    j = lax.rem(lane, 8)

    def pack_into(acc, val, pr):
        for h in range(2):
            s = h * NR + pr
            t = pltpu.roll(val[h * HALF : (h + 1) * HALF], 8 * s + 2 if isinstance(s, int) and 8 * s + 2 < 128 else lax.rem(8 * s + 2, 128), 1)
            acc = jnp.where(slot_of == s, t, acc)
        return acc

    zero24 = jnp.zeros((HALF, 128), f32)
    edge[...] = lax.fori_loop(0, NR, lambda pr, acc: pack_into(acc, ta[rows_of(pr), :], pr), zero24)
    edges = to_vox(edge, edge_l, right, 0), to_vox(edge, edge_r, left, 1)
    start_vox(*edges)

    for c in loads[7:]:
        c.wait()

    fields = ((u0, 1, 0), (w0, 2, 0), (w0, 2, 1), (p0, 2, 0), (p0, 2, 1), (q0, 3, 0), (q0, 3, 1), (q0, 3, 2))

    def pack_step(pr, accs):
        return tuple(pack_into(acc, natural(ref, pr, n, comp, CP), pr) for acc, (ref, n, comp) in zip(accs, fields))

    packed = lax.fori_loop(0, NR, pack_step, (zero24,) * 8)
    for f in range(8):
        halo[pl.ds(f * HALF, HALF), :] = packed[f]
    halos = to_vox(halo, halo_l, right, 2), to_vox(halo, halo_r, left, 3)
    start_vox(*halos)

    arrive_vox(*edges)
    near = (
        jnp.where((j == 1) & has_left, edge_l[...], 0.0)
        + jnp.where((j == 6) & has_right, pltpu.roll(edge_r[...], 4, 1), 0.0)
    )
    edge_c[...] = near[0:8] + pltpu.roll(near[8:16], 1, 1) + pltpu.roll(near[16:24], 2, 1)
    for i, k in enumerate(order):
        pltpu.make_async_remote_copy(
            src_ref=edge_c, dst_ref=edge_in.at[i], send_sem=dir_s.at[4], recv_sem=dir_r.at[4],
            device_id={"dir": peer(k)}, device_id_type=MESH).start()

    def reduce_chunk(src, recv, n, full):
        wait_all(dir_r.at[n], recv.at[slots])
        total = src[chunk(me), :]
        for i in range(others):
            total = total + recv[i]
        full[chunk(me), :] = total
        for c in gather(full, n + 2):
            c.start()

    reduce_chunk(ta, ra, 0, fa)
    reduce_chunk(tb, rb, 1, fb)

    arrive_vox(*halos)

    def widen(f):
        at = pl.ds(f * HALF, HALF)
        own = halo[at, :]
        far_l = jnp.where(has_left, halo_l[at, :], 0.0)
        far_r = jnp.where(has_right, halo_r[at, :], 0.0)
        return jnp.where(j < 2, far_l, jnp.where(j < 4, own, pltpu.roll(jnp.where(j < 2, own, far_r), 4, 1)))

    col = jnp.where(j < 4, j - 2, j + 122) + vox * 128
    keep_w = ((col >= 0) & (col < nvox * 128 - 1)).astype(f32)
    rid = lax.rem(lane // 8, 4)
    low_w, high_w = (rid < 3).astype(f32), (rid >= 1).astype(f32)

    def fr_w(x):
        return (pltpu.roll(x, 120, 1) - x) * low_w

    def br_w(x):
        return x * low_w - pltpu.roll(x, 8, 1) * high_w

    def fx_w(x):
        return (pltpu.roll(x, 127, 1) - x) * keep_w

    def bx_w(x):
        return x * keep_w - pltpu.roll(x, 1, 1)

    def shrink(sq, alpha):
        return jnp.minimum(1.0, alpha * lax.rsqrt(sq))

    def norm_w(sq):
        n = jnp.sum(sq, 0, keepdims=True)
        return n + pltpu.roll(n, 64, 1)

    def dual_p_w(pr_, pc_, u_, wr_, wc_):
        a = pr_ + SIGMA * (fr_w(u_) - wr_)
        b = pc_ + SIGMA * (fx_w(u_) - wc_)
        s = shrink(norm_w(a * a + b * b), ALPHA1)
        return a * s, b * s

    def dual_q_w(qa_, qb_, qc_, wr_, wc_):
        a = qa_ + SIGMA * br_w(wr_)
        b = qb_ + SIGMA * bx_w(wc_)
        c = qc_ + (0.5 * SIGMA) * (bx_w(wr_) + br_w(wc_))
        s = shrink(norm_w(a * a + b * b + 2.0 * (c * c)), ALPHA0)
        return a * s, b * s, c * s

    uw, wrw, wcw = widen(0), widen(1), widen(2)
    p1rw, p1cw = dual_p_w(widen(3), widen(4), uw, wrw, wcw)
    q1aw, q1bw, q1cw = dual_q_w(widen(5), widen(6), widen(7), wrw, wcw)
    w1rw = wrw + TAU * (p1rw + fr_w(q1aw) + fx_w(q1cw))
    w1cw = wcw + TAU * (p1cw + fx_w(q1bw) + fr_w(q1cw))
    wbrw, wbcw = 2.0 * w1rw - wrw, 2.0 * w1cw - wcw
    _, q2bw, q2cw = dual_q_w(q1aw, q1bw, q1cw, wbrw, wbcw)
    pbrw, pbcw = p1rw - SIGMA * wbrw, p1cw - SIGMA * wbcw
    ubw = uw + TAU * (br_w(p1rw) + bx_w(p1cw))
    for n, val in enumerate((uw, wrw, wcw, p1cw, q1bw, q1cw, wbrw, wbcw, q2bw, q2cw, pbrw, pbcw, ubw)):
        wk[n] = val

    keep = jnp.where(lane + vox * 128 < nvox * 128 - 1, 1.0, 0.0).astype(f32)

    def beside(val, pr, at):
        parts = [pltpu.roll(val, at - 8 * (h * NR + pr), 1) for h in range(2)]
        return jnp.concatenate(parts, 0)

    def nxt(x, far, pr):
        return jnp.where(lane == 127, beside(far, pr, 121), pltpu.roll(x, 127, 1))

    def prv(x, far, pr):
        return jnp.where(lane == 0, beside(far, pr, 127), pltpu.roll(x, 1, 1))

    def fx(x, far, pr):
        return (nxt(x, far, pr) - x) * keep

    def bx(x, far, pr):
        return x * keep - prv(x, far, pr)

    def fr(x, below, r):
        return below - x if r < 3 else jnp.zeros_like(x)

    def br(x, above, r):
        if r == 0:
            return x
        return x - above if r < 3 else -above

    def colsum(x):
        return jnp.sum(x, 0, keepdims=True)

    def dual_one(p, _):
        for r in range(4):
            pr = 4 * p + r
            u = natural(u0, pr, 1, 0, CP)
            below = natural(u0, pr + 1, 1, 0, CP) if r < 3 else None
            wr, wc = natural(w0, pr, 2, 0, CP), natural(w0, pr, 2, 1, CP)
            a = natural(p0, pr, 2, 0, CP) + SIGMA * (fr(u, below, r) - wr)
            b = natural(p0, pr, 2, 1, CP) + SIGMA * (fx(u, wk[0], pr) - wc)
            s = shrink(colsum(a * a + b * b), ALPHA1)
            p1r[rows_of(pr), :] = a * s
            p1c[rows_of(pr), :] = b * s
            wra = natural(w0, pr - 1, 2, 0, CP) if r > 0 else None
            wca = natural(w0, pr - 1, 2, 1, CP) if r > 0 else None
            a = natural(q0, pr, 3, 0, CP) + SIGMA * br(wr, wra, r)
            b = natural(q0, pr, 3, 1, CP) + SIGMA * bx(wc, wk[2], pr)
            c = natural(q0, pr, 3, 2, CP) + (0.5 * SIGMA) * (bx(wr, wk[1], pr) + br(wc, wca, r))
            s = shrink(colsum(a * a + b * b + 2.0 * (c * c)), ALPHA0)
            q1a[rows_of(pr), :] = a * s
            q1b[rows_of(pr), :] = b * s
            q1c[rows_of(pr), :] = c * s
        return 0

    lax.fori_loop(0, 2, dual_one, 0)


    def primal_one(p, _):
        for r in range(4):
            pr = 4 * p + r
            here = rows_of(pr)
            pr_, pc_ = p1r[here, :], p1c[here, :]
            above = p1r[rows_of(pr - 1), :] if r > 0 else None
            ub[here, :] = natural(u0, pr, 1, 0, CP) + TAU * (br(pr_, above, r) + bx(pc_, wk[3], pr))
            qa, qb, qc = q1a[here, :], q1b[here, :], q1c[here, :]
            qab = q1a[rows_of(pr + 1), :] if r < 3 else None
            qcb = q1c[rows_of(pr + 1), :] if r < 3 else None
            wr, wc = natural(w0, pr, 2, 0, CP), natural(w0, pr, 2, 1, CP)
            dr = TAU * (pr_ + fr(qa, qab, r) + fx(qc, wk[5], pr))
            dc = TAU * (pc_ + fx(qb, wk[4], pr) + fr(qc, qcb, r))
            nr, nc = wr + 2.0 * dr, wc + 2.0 * dc
            w1r[here, :] = wr + dr
            w1c[here, :] = wc + dc
            wbr[here, :] = nr
            wbc[here, :] = nc
            pbr[here, :] = pr_ - SIGMA * nr
            pbc[here, :] = pc_ - SIGMA * nc
        return 0

    lax.fori_loop(0, 2, primal_one, 0)

    def dual_two(p, _):
        for r in range(4):
            pr = 4 * p + r
            here = rows_of(pr)
            wr, wc = wbr[here, :], wbc[here, :]
            wra = wbr[rows_of(pr - 1), :] if r > 0 else None
            wca = wbc[rows_of(pr - 1), :] if r > 0 else None
            a = q1a[here, :] + SIGMA * br(wr, wra, r)
            b = q1b[here, :] + SIGMA * bx(wc, wk[7], pr)
            c = q1c[here, :] + (0.5 * SIGMA) * (bx(wr, wk[6], pr) + br(wc, wca, r))
            s = shrink(colsum(a * a + b * b + 2.0 * (c * c)), ALPHA0)
            q1a[here, :] = a * s
            q1b[here, :] = b * s
            q1c[here, :] = c * s
        return 0

    lax.fori_loop(0, 2, dual_two, 0)

    def aux_two(p, _):
        for r in range(4):
            pr = 4 * p + r
            here = rows_of(pr)
            qa, qb, qc = q1a[here, :], q1b[here, :], q1c[here, :]
            qab = q1a[rows_of(pr + 1), :] if r < 3 else None
            qcb = q1c[rows_of(pr + 1), :] if r < 3 else None
            v2r[here, :] = w1r[here, :] + TAU * (fr(qa, qab, r) + fx(qc, wk[9], pr))
            v2c[here, :] = w1c[here, :] + TAU * (fx(qb, wk[8], pr) + fr(qc, qcb, r))
        return 0

    lax.fori_loop(0, 2, aux_two, 0)

    wait_all(dir_r.at[4], edge_in.at[slots])
    total = edge_c[...]
    for i in range(others):
        total = total + edge_in[i]
    adj_w = jnp.concatenate([total, pltpu.roll(total, 127, 1), pltpu.roll(total, 126, 1)], 0)
    row24 = lax.broadcasted_iota(jnp.int32, (HALF, 1), 0)
    adj_w = jnp.where(((j == 1) | (j == 6)) & ((row24 < NC - HALF) | (lane < 64)), adj_w, 0.0)
    bar_w = 2.0 * (wk[12] - TAU * adj_w) - wk[0]
    wk[0] = bar_w

    wait_all(dir_r.at[2], fa.at[rows_in])
    for pr in range(NR):
        hg[pl.ds(3 * pr, 3), :] = fa[pl.ds(pr * CP + NC, CP - NC), :]
    hv = hg[...]
    gh, gl = split(jnp.concatenate([hv, pltpu.roll(hv, 64, 1)], 0)[:, 0:CP])
    real = lax.broadcasted_iota(jnp.int32, (CP, 1), 0) < NC

    def dual_three(p, own_bar):
        bars = []
        for r in range(4):
            pr = 4 * p + r
            here = rows_of(pr)
            new = ub[here, :] - TAU * jnp.where(real, fa[here, :], 0.0)
            u1[here, :] = new
            bars.append(2.0 * new - natural(u0, pr, 1, 0, CP))
            own_bar = pack_into(own_bar, bars[r], pr)
        for i in range(2):
            store_pair(gu, 2 * p + i, mm3(gh, gl, jnp.concatenate(bars[2 * i : 2 * i + 2], 1)))
        for r in range(4):
            pr = 4 * p + r
            here = rows_of(pr)
            a = pbr[here, :] + SIGMA * fr(bars[r], bars[r + 1] if r < 3 else None, r)
            b = pbc[here, :] + SIGMA * fx(bars[r], wk[0], pr)
            s = shrink(colsum(a * a + b * b), ALPHA1)
            a, b = a * s, b * s
            p2r[here, :] = a
            p2c[here, :] = b
            wo[pl.ds(pr, CP, stride=2 * NR), :] = v2r[here, :] + TAU * a
            wo[pl.ds(NR + pr, CP, stride=2 * NR), :] = v2c[here, :] + TAU * b
        return own_bar

    own_bar = lax.fori_loop(0, 2, dual_three, zero24)
    bar_w = jnp.where(j == 2, own_bar, wk[0])
    a = wk[10] + SIGMA * fr_w(bar_w)
    b = wk[11] + SIGMA * fx_w(bar_w)
    s = shrink(norm_w(a * a + b * b), ALPHA1)
    wk[3] = b * s
    def primal_two(p, _):
        for r in range(4):
            pr = 4 * p + r
            here = rows_of(pr)
            m = mask[pl.ds(pr, 1), :].astype(f32) * (1.0 / (1.0 + SIGMA))
            above = p2r[rows_of(pr - 1), :] if r > 0 else None
            div = br(p2r[here, :], above, r) + bx(p2c[here, :], wk[3], pr)
            adj = m * (fa[here, :] + SIGMA * gu[here, :])
            u1[here, :] = u1[here, :] - TAU * (adj - div)
        return 0

    lax.fori_loop(0, 2, primal_two, 0)
    wait_all(dir_r.at[3], fb.at[rows_in])

    def add_signals(pr, _):
        m = mask[pl.ds(pr, 1), :].astype(f32) * (TAU * SIGMA / (1.0 + SIGMA))
        uo[pl.ds(pr, CP, stride=NR), :] = u1[rows_of(pr), :] + m * fb[rows_of(pr), :]
        return 0

    lax.fori_loop(0, NR, add_signals, 0, unroll=True)

    wait_all(dir_s.at[0], ra.at[slots])
    wait_all(dir_s.at[1], rb.at[slots])
    wait_all(dir_s.at[2], fa.at[rows_in])
    wait_all(dir_s.at[3], fb.at[rows_in])
    wait_all(dir_s.at[4], edge_in.at[slots])
    for to_right, to_left in (edges, halos):

        @pl.when(has_right)
        def _():
            to_right.wait_send()

        @pl.when(has_left)
        def _():
            to_left.wait_send()


def put_kernel(u, w, u_hbm, w_hbm, sem):
    copies = [
        pltpu.make_async_copy(w.at[pl.ds(0, NC * 2 * NR)], w_hbm, sem.at[0]),
        pltpu.make_async_copy(u.at[pl.ds(0, NC * NR)], u_hbm, sem.at[1]),
    ]
    for c in copies:
        c.start()
    for c in copies:
        c.wait()


def body(nvox, signals, basis, response, shell_index, brain_mask, fodf, aux_field, grad_dual, sym_dual, data_dual):
    hbm = pl.BlockSpec(memory_space=pltpu.HBM)
    vmem = pl.BlockSpec(memory_space=pltpu.VMEM)
    field = pltpu.VMEM((NR * CP, 128), f32)
    npeer = SIDE * SIDE
    dma = lambda n: pltpu.SemaphoreType.DMA((n,))
    edges = pltpu.VMEM((HALF, 128), f32)
    halos = pltpu.VMEM((8 * HALF, 128), f32)
    u, w = pl.pallas_call(
        functools.partial(kernel, nvox),
        out_shape=(pltpu.VMEM((NR * CP, 128), f32), pltpu.VMEM((CP * 2 * NR, 128), f32)),
        in_specs=[hbm] * 10,
        out_specs=(vmem, vmem),
        scratch_shapes=[
            pltpu.VMEM((ND * NR, 128), bf16),
            pltpu.VMEM((NC, ND), f32),
            pltpu.VMEM((3, 5), f32),
            pltpu.VMEM((1, ND), jnp.int32),
            pltpu.VMEM((NR, 128), jnp.int32),
            field,
            pltpu.VMEM((CP * 2 * NR, 128), f32),
            pltpu.VMEM((CP * 2 * NR, 128), f32),
            pltpu.VMEM((CP * 3 * NR, 128), f32),
            pltpu.VMEM((ND * NR, 128), f32),
            pltpu.VMEM((ND * NR, 128), f32),
            pltpu.VMEM((CP, 128), f32),
            field, field, field, field,
            pltpu.VMEM((npeer, HALF, 128), f32),
            pltpu.VMEM((npeer, HALF, 128), f32),
            edges,
            halos, halos, halos,
            edges, edges, edges,
            pltpu.VMEM((8, 128), f32),
            pltpu.VMEM((npeer, 8, 128), f32),
            pltpu.VMEM((13, HALF, 128), f32),
        ]
        + [field] * 18
        + [dma(10)]
        + [dma(5), dma(5), dma(4), dma(4)],
        compiler_params=pltpu.CompilerParams(
            collective_id=0, has_side_effects=True, vmem_limit_bytes=48 * 1024 * 1024
        ),
    )(*[pltpu.with_memory_space_constraint(x, pltpu.HBM) for x in (
        signals.reshape(ND * NR, 128),
        basis.T,
        response,
        shell_index.reshape(1, ND),
        brain_mask.reshape(NR, 128),
        fodf.reshape(NC * NR, 128),
        aux_field.reshape(NC * 2 * NR, 128),
        grad_dual.reshape(NC * 2 * NR, 128),
        sym_dual.reshape(NC * 3 * NR, 128),
        data_dual.reshape(ND * NR, 128),
    )])
    u, w = pl.pallas_call(
        put_kernel,
        out_shape=(pltpu.HBM((NC * NR, 128), f32), pltpu.HBM((NC * 2 * NR, 128), f32)),
        in_specs=[vmem, vmem],
        out_specs=(hbm, hbm),
        scratch_shapes=[dma(2)],
        compiler_params=pltpu.CompilerParams(vmem_limit_bytes=4 * 1024 * 1024),
    )(pltpu.with_memory_space_constraint(u, pltpu.VMEM), pltpu.with_memory_space_constraint(w, pltpu.VMEM))
    return u.reshape(fodf.shape), w.reshape(aux_field.shape)


def solution(mesh):
    placed = (
        P("dir", None, None, "vox"),
        P("dir", None),
        P(),
        P("dir"),
        P(None, None, "vox"),
        P(None, None, None, "vox"),
        P(None, None, None, None, "vox"),
        P(None, None, None, None, "vox"),
        P(None, None, None, None, "vox"),
        P("dir", None, None, "vox"),
    )
    return jax.shard_map(
        functools.partial(body, mesh.shape["vox"]),
        mesh=mesh,
        in_specs=placed,
        out_specs=(P(None, None, None, "vox"), P(None, None, None, None, "vox")),
        check_vma=False,
    )
```

```python
import functools

import jax
import jax.numpy as jnp
import numpy as np
from jax import lax
from jax.experimental import pallas as pl
from jax.experimental.pallas import tpu as pltpu
from jax.sharding import PartitionSpec as P

MESH = pl.DeviceIdType.MESH
f32 = jnp.float32
bf16 = jnp.bfloat16

SIGMA = 0.25
TAU = 0.3
ALPHA1 = 1.0
ALPHA0 = 1.5
ORDER_STARTS = (1, 6, 15, 28)

NC = 45
CP = 48
HALF = 24
ND = 72
NR = 8
SIDE = 4


def split(x):
    hi = x.astype(bf16)
    return hi, (x - hi.astype(f32)).astype(bf16)


def mm(a, b):
    return jnp.dot(a, b, preferred_element_type=f32)


def mm3(ah, al, x):
    xh, xl = split(x)
    return mm(ah, xh) + mm(ah, xl) + mm(al, xh)


def rows_of(pr):
    start = pr * CP
    return pl.ds(start if isinstance(start, int) else pl.multiple_of(start, 8), CP)


def kernel(
    nvox,
    sig_hbm, basis_hbm, resp_hbm, shell_hbm, mask_hbm, fodf_hbm, aux_hbm, grad_hbm, sym_hbm, dual_hbm,
    uo, wo,
    sig, basis, resp, shell, mask, u0, w0, p0, q0, y0, sigf,
    kt, ta, tb, fa, fb, ra, rb, hg,
    halo, halo_l, halo_r, edge, edge_l, edge_r, edge_c, edge_in, wk,
    p1r, p1c, q1a, q1b, q1c, wbr, wbc, w1r, w1c, pbr, pbc, ub, v2r, v2c, u1, gu, p2r, p2c,
    in_sem, dir_s, dir_r, vox_s, vox_r,
):
    me = lax.axis_index("dir")
    vox = lax.axis_index("vox")
    mx, my = me // SIDE, lax.rem(me, SIDE)
    npeer = SIDE * SIDE
    order = [10, 6, 9, 14, 11, 2, 8, 5, 15, 7, 13, 1, 4, 3, 12]

    def peer(k):
        return lax.rem(mx + k // SIDE, SIDE) * SIDE + lax.rem(my + k % SIDE, SIDE)

    has_left, has_right = vox > 0, vox < nvox - 1
    left, right = vox - 1, vox + 1

    def load(i, src, dst):
        return pltpu.make_async_copy(src, dst, in_sem.at[i])

    loads = [
        load(0, basis_hbm, basis),
        load(1, resp_hbm, resp),
        load(2, shell_hbm, shell),
        load(3, mask_hbm, mask.at[pl.ds(0, NR)]),
        load(4, fodf_hbm, u0.at[pl.ds(0, NC * NR)]),
        load(5, sig_hbm, sig),
        load(6, dual_hbm, y0.at[pl.ds(0, ND * NR)]),
        load(7, aux_hbm, w0.at[pl.ds(0, NC * 2 * NR)]),
        load(8, grad_hbm, p0.at[pl.ds(0, NC * 2 * NR)]),
        load(9, sym_hbm, q0.at[pl.ds(0, NC * 3 * NR)]),
    ]
    for c in loads[:7]:
        c.start()
    barrier = pltpu.get_barrier_semaphore()
    for k in order:
        pl.semaphore_signal(barrier, inc=1, device_id={"dir": peer(k)}, device_id_type=MESH)
    for there, n in ((has_left, left), (has_right, right)):

        @pl.when(there)
        def _():
            pl.semaphore_signal(barrier, inc=1, device_id={"vox": n}, device_id_type=MESH)


    lane = lax.broadcasted_iota(jnp.int32, (1, 128), 1)
    for ref, n in ((u0, 1), (w0, 2), (p0, 2), (q0, 3)):
        ref[pl.ds(NC * n * NR, (CP - NC) * n * NR), :] = jnp.zeros(((CP - NC) * n * NR, 128), f32)

    for c in loads[:3]:
        c.wait()
    kt[...] = jnp.zeros((CP, 128), f32)
    sh = shell[...]
    per_order = [
        jnp.where(sh == 0, resp[0:1, o : o + 1], jnp.where(sh == 1, resp[1:2, o : o + 1], resp[2:3, o : o + 1]))
        for o in range(5)
    ]
    cid = lax.broadcasted_iota(jnp.int32, (NC, 1), 0)
    scale = jnp.broadcast_to(per_order[0], (NC, ND))
    for o, start in enumerate(ORDER_STARTS):
        scale = jnp.where(cid >= start, per_order[o + 1], scale)
    kt[pl.ds(0, NC), pl.ds(0, ND)] = basis[...] * scale
    ktv = kt[...]
    knv = jnp.concatenate([ktv, jnp.zeros((128 - CP, 128), f32)], 0).T[0:ND]
    kth, ktl = split(ktv[:, 0:ND])
    knh128, knl128 = split(knv)
    knh, knl = knh128[:, 0:CP], knl128[:, 0:CP]

    for c in loads[7:]:
        c.start()
    gram = mm3(kth, ktl, knv)
    hg[pl.ds(0, HALF), :] = gram[0:HALF] + pltpu.roll(gram[HALF:CP], 64, 1)
    for c in loads[3:7]:
        c.wait()

    def to_f32(i, _):
        at = pl.ds(pl.multiple_of(i * 96, 96), 96)
        sigf[at, :] = sig[at, :].astype(f32)
        return 0

    lax.fori_loop(0, 6, to_f32, 0)

    def natural(ref, pr, n, comp, count):
        return ref[pl.ds(comp * NR + pr, count, stride=n * NR), :]

    def pair(ref, i, count):
        return jnp.concatenate([natural(ref, 2 * i, 1, 0, count), natural(ref, 2 * i + 1, 1, 0, count)], 1)

    def store_pair(ref, i, val):
        ref[rows_of(2 * i), :] = val[:, 0:128]
        ref[rows_of(2 * i + 1), :] = val[:, 128:256]

    def data_step(i, _):
        pred = mm3(knh, knl, pair(u0, i, CP))
        m = jnp.concatenate([mask[pl.ds(2 * i, 1), :], mask[pl.ds(2 * i + 1, 1), :]], 1).astype(f32)
        y = (m * (1.0 / (1.0 + SIGMA))) * (pair(y0, i, ND) + SIGMA * (pred - pair(sigf, i, ND)))
        store_pair(ta, i, mm3(kth, ktl, y))
        return 0

    lax.fori_loop(0, 4, data_step, 0, unroll=True)

    for pr in range(NR):
        ta[pl.ds(pr * CP + NC, CP - NC), :] = hg[pl.ds(3 * pr, 3), :]

    def signal_step(i, _):
        s = pair(sigf, i, ND).astype(bf16)
        store_pair(tb, i, mm(kth, s) + mm(ktl, s))
        return 0

    lax.fori_loop(0, 4, signal_step, 0, unroll=True)
    def chunk(d):
        return pl.ds(pl.multiple_of(d * HALF, HALF), HALF)

    def scatter(src, dst, n):
        return [
            pltpu.make_async_remote_copy(
                src_ref=src.at[chunk(peer(k))], dst_ref=dst.at[i], send_sem=dir_s.at[n], recv_sem=dir_r.at[n],
                device_id={"dir": peer(k)}, device_id_type=MESH)
            for i, k in enumerate(order)
        ]

    def gather(ref, n):
        return [
            pltpu.make_async_remote_copy(
                src_ref=ref.at[chunk(me)], dst_ref=ref.at[chunk(me)], send_sem=dir_s.at[n], recv_sem=dir_r.at[n],
                device_id={"dir": peer(k)}, device_id_type=MESH)
            for k in order
        ]

    def wait_all(sem, ref):
        pltpu.make_async_copy(ref, ref, sem).wait()

    def to_vox(src, dst, n, k):
        return pltpu.make_async_remote_copy(
            src_ref=src, dst_ref=dst, send_sem=vox_s.at[k], recv_sem=vox_r.at[k],
            device_id={"vox": n}, device_id_type=MESH)

    def start_vox(to_right, to_left):
        @pl.when(has_right)
        def _():
            to_right.start()

        @pl.when(has_left)
        def _():
            to_left.start()

    def arrive_vox(to_right, to_left):
        @pl.when(has_left)
        def _():
            to_right.wait_recv()

        @pl.when(has_right)
        def _():
            to_left.wait_recv()

    others = npeer - 1
    slots = pl.ds(0, others)
    rows_in = pl.ds(0, others * HALF)
    slot_of = lane // 8
    j = lax.rem(lane, 8)

    def pack_into(acc, val, pr):
        for h in range(2):
            s = h * NR + pr
            t = pltpu.roll(val[h * HALF : (h + 1) * HALF], 8 * s + 2 if isinstance(s, int) and 8 * s + 2 < 128 else lax.rem(8 * s + 2, 128), 1)
            acc = jnp.where(slot_of == s, t, acc)
        return acc

    zero24 = jnp.zeros((HALF, 128), f32)
    edge[...] = lax.fori_loop(0, NR, lambda pr, acc: pack_into(acc, ta[rows_of(pr), :], pr), zero24)

    pl.semaphore_wait(barrier, others + has_left.astype(jnp.int32) + has_right.astype(jnp.int32))
    edges = to_vox(edge, edge_l, right, 0), to_vox(edge, edge_r, left, 1)
    start_vox(*edges)
    far = [min(k // SIDE, SIDE - k // SIDE) + min(k % SIDE, SIDE - k % SIDE) for k in order]
    sends = scatter(ta, ra, 0), scatter(tb, rb, 1)
    for n, least, most in ((0, 2, 4), (1, 3, 4), (0, 1, 1), (1, 2, 2), (1, 1, 1)):
        for c, hops in zip(sends[n], far):
            if least <= hops <= most:
                c.start()

    for c in loads[7:]:
        c.wait()

    fields = ((u0, 1, 0), (w0, 2, 0), (w0, 2, 1), (p0, 2, 0), (p0, 2, 1), (q0, 3, 0), (q0, 3, 1), (q0, 3, 2))

    def pack_step(pr, accs):
        return tuple(pack_into(acc, natural(ref, pr, n, comp, CP), pr) for acc, (ref, n, comp) in zip(accs, fields))

    packed = lax.fori_loop(0, NR, pack_step, (zero24,) * 8)
    for f in range(8):
        halo[pl.ds(f * HALF, HALF), :] = packed[f]
    halos = to_vox(halo, halo_l, right, 2), to_vox(halo, halo_r, left, 3)
    start_vox(*halos)

    arrive_vox(*edges)
    near = (
        jnp.where((j == 1) & has_left, edge_l[...], 0.0)
        + jnp.where((j == 6) & has_right, pltpu.roll(edge_r[...], 4, 1), 0.0)
    )
    edge_c[...] = near[0:8] + pltpu.roll(near[8:16], 1, 1) + pltpu.roll(near[16:24], 2, 1)
    for i, k in enumerate(order):
        pltpu.make_async_remote_copy(
            src_ref=edge_c, dst_ref=edge_in.at[i], send_sem=dir_s.at[4], recv_sem=dir_r.at[4],
            device_id={"dir": peer(k)}, device_id_type=MESH).start()

    def reduce_chunk(src, recv, n, full):
        wait_all(dir_r.at[n], recv.at[slots])
        total = src[chunk(me), :]
        for i in range(others):
            total = total + recv[i]
        full[chunk(me), :] = total
        for c in gather(full, n + 2):
            c.start()

    reduce_chunk(ta, ra, 0, fa)
    reduce_chunk(tb, rb, 1, fb)

    arrive_vox(*halos)

    def widen(f):
        at = pl.ds(f * HALF, HALF)
        own = halo[at, :]
        far_l = jnp.where(has_left, halo_l[at, :], 0.0)
        far_r = jnp.where(has_right, halo_r[at, :], 0.0)
        return jnp.where(j < 2, far_l, jnp.where(j < 4, own, pltpu.roll(jnp.where(j < 2, own, far_r), 4, 1)))

    col = jnp.where(j < 4, j - 2, j + 122) + vox * 128
    keep_w = ((col >= 0) & (col < nvox * 128 - 1)).astype(f32)
    rid = lax.rem(lane // 8, 4)
    low_w, high_w = (rid < 3).astype(f32), (rid >= 1).astype(f32)

    def fr_w(x):
        return (pltpu.roll(x, 120, 1) - x) * low_w

    def br_w(x):
        return x * low_w - pltpu.roll(x, 8, 1) * high_w

    def fx_w(x):
        return (pltpu.roll(x, 127, 1) - x) * keep_w

    def bx_w(x):
        return x * keep_w - pltpu.roll(x, 1, 1)

    def shrink(sq, alpha):
        return jnp.minimum(1.0, alpha * lax.rsqrt(sq))

    def norm_w(sq):
        n = jnp.sum(sq, 0, keepdims=True)
        return n + pltpu.roll(n, 64, 1)

    def dual_p_w(pr_, pc_, u_, wr_, wc_):
        a = pr_ + SIGMA * (fr_w(u_) - wr_)
        b = pc_ + SIGMA * (fx_w(u_) - wc_)
        s = shrink(norm_w(a * a + b * b), ALPHA1)
        return a * s, b * s

    def dual_q_w(qa_, qb_, qc_, wr_, wc_):
        a = qa_ + SIGMA * br_w(wr_)
        b = qb_ + SIGMA * bx_w(wc_)
        c = qc_ + (0.5 * SIGMA) * (bx_w(wr_) + br_w(wc_))
        s = shrink(norm_w(a * a + b * b + 2.0 * (c * c)), ALPHA0)
        return a * s, b * s, c * s

    uw, wrw, wcw = widen(0), widen(1), widen(2)
    p1rw, p1cw = dual_p_w(widen(3), widen(4), uw, wrw, wcw)
    q1aw, q1bw, q1cw = dual_q_w(widen(5), widen(6), widen(7), wrw, wcw)
    w1rw = wrw + TAU * (p1rw + fr_w(q1aw) + fx_w(q1cw))
    w1cw = wcw + TAU * (p1cw + fx_w(q1bw) + fr_w(q1cw))
    wbrw, wbcw = 2.0 * w1rw - wrw, 2.0 * w1cw - wcw
    _, q2bw, q2cw = dual_q_w(q1aw, q1bw, q1cw, wbrw, wbcw)
    pbrw, pbcw = p1rw - SIGMA * wbrw, p1cw - SIGMA * wbcw
    ubw = uw + TAU * (br_w(p1rw) + bx_w(p1cw))
    for n, val in enumerate((uw, wrw, wcw, p1cw, q1bw, q1cw, wbrw, wbcw, q2bw, q2cw, pbrw, pbcw, ubw)):
        wk[n] = val

    keep = jnp.where(lane + vox * 128 < nvox * 128 - 1, 1.0, 0.0).astype(f32)

    def beside(val, pr, at):
        parts = [pltpu.roll(val, at - 8 * (h * NR + pr), 1) for h in range(2)]
        return jnp.concatenate(parts, 0)

    def nxt(x, far, pr):
        return jnp.where(lane == 127, beside(far, pr, 121), pltpu.roll(x, 127, 1))

    def prv(x, far, pr):
        return jnp.where(lane == 0, beside(far, pr, 127), pltpu.roll(x, 1, 1))

    def fx(x, far, pr):
        return (nxt(x, far, pr) - x) * keep

    def bx(x, far, pr):
        return x * keep - prv(x, far, pr)

    def fr(x, below, r):
        return below - x if r < 3 else jnp.zeros_like(x)

    def br(x, above, r):
        if r == 0:
            return x
        return x - above if r < 3 else -above

    def colsum(x):
        return jnp.sum(x, 0, keepdims=True)

    def dual_one(p, _):
        for r in range(4):
            pr = 4 * p + r
            u = natural(u0, pr, 1, 0, CP)
            below = natural(u0, pr + 1, 1, 0, CP) if r < 3 else None
            wr, wc = natural(w0, pr, 2, 0, CP), natural(w0, pr, 2, 1, CP)
            a = natural(p0, pr, 2, 0, CP) + SIGMA * (fr(u, below, r) - wr)
            b = natural(p0, pr, 2, 1, CP) + SIGMA * (fx(u, wk[0], pr) - wc)
            s = shrink(colsum(a * a + b * b), ALPHA1)
            p1r[rows_of(pr), :] = a * s
            p1c[rows_of(pr), :] = b * s
            wra = natural(w0, pr - 1, 2, 0, CP) if r > 0 else None
            wca = natural(w0, pr - 1, 2, 1, CP) if r > 0 else None
            a = natural(q0, pr, 3, 0, CP) + SIGMA * br(wr, wra, r)
            b = natural(q0, pr, 3, 1, CP) + SIGMA * bx(wc, wk[2], pr)
            c = natural(q0, pr, 3, 2, CP) + (0.5 * SIGMA) * (bx(wr, wk[1], pr) + br(wc, wca, r))
            s = shrink(colsum(a * a + b * b + 2.0 * (c * c)), ALPHA0)
            q1a[rows_of(pr), :] = a * s
            q1b[rows_of(pr), :] = b * s
            q1c[rows_of(pr), :] = c * s
        return 0

    lax.fori_loop(0, 2, dual_one, 0)


    def primal_one(p, _):
        for r in range(4):
            pr = 4 * p + r
            here = rows_of(pr)
            pr_, pc_ = p1r[here, :], p1c[here, :]
            above = p1r[rows_of(pr - 1), :] if r > 0 else None
            ub[here, :] = natural(u0, pr, 1, 0, CP) + TAU * (br(pr_, above, r) + bx(pc_, wk[3], pr))
            qa, qb, qc = q1a[here, :], q1b[here, :], q1c[here, :]
            qab = q1a[rows_of(pr + 1), :] if r < 3 else None
            qcb = q1c[rows_of(pr + 1), :] if r < 3 else None
            wr, wc = natural(w0, pr, 2, 0, CP), natural(w0, pr, 2, 1, CP)
            dr = TAU * (pr_ + fr(qa, qab, r) + fx(qc, wk[5], pr))
            dc = TAU * (pc_ + fx(qb, wk[4], pr) + fr(qc, qcb, r))
            nr, nc = wr + 2.0 * dr, wc + 2.0 * dc
            w1r[here, :] = wr + dr
            w1c[here, :] = wc + dc
            wbr[here, :] = nr
            wbc[here, :] = nc
            pbr[here, :] = pr_ - SIGMA * nr
            pbc[here, :] = pc_ - SIGMA * nc
        return 0

    lax.fori_loop(0, 2, primal_one, 0)

    def dual_two(p, _):
        for r in range(4):
            pr = 4 * p + r
            here = rows_of(pr)
            wr, wc = wbr[here, :], wbc[here, :]
            wra = wbr[rows_of(pr - 1), :] if r > 0 else None
            wca = wbc[rows_of(pr - 1), :] if r > 0 else None
            a = q1a[here, :] + SIGMA * br(wr, wra, r)
            b = q1b[here, :] + SIGMA * bx(wc, wk[7], pr)
            c = q1c[here, :] + (0.5 * SIGMA) * (bx(wr, wk[6], pr) + br(wc, wca, r))
            s = shrink(colsum(a * a + b * b + 2.0 * (c * c)), ALPHA0)
            q1a[here, :] = a * s
            q1b[here, :] = b * s
            q1c[here, :] = c * s
        return 0

    lax.fori_loop(0, 2, dual_two, 0)

    def aux_two(p, _):
        for r in range(4):
            pr = 4 * p + r
            here = rows_of(pr)
            qa, qb, qc = q1a[here, :], q1b[here, :], q1c[here, :]
            qab = q1a[rows_of(pr + 1), :] if r < 3 else None
            qcb = q1c[rows_of(pr + 1), :] if r < 3 else None
            v2r[here, :] = w1r[here, :] + TAU * (fr(qa, qab, r) + fx(qc, wk[9], pr))
            v2c[here, :] = w1c[here, :] + TAU * (fx(qb, wk[8], pr) + fr(qc, qcb, r))
        return 0

    lax.fori_loop(0, 2, aux_two, 0)

    wait_all(dir_r.at[4], edge_in.at[slots])
    total = edge_c[...]
    for i in range(others):
        total = total + edge_in[i]
    adj_w = jnp.concatenate([total, pltpu.roll(total, 127, 1), pltpu.roll(total, 126, 1)], 0)
    row24 = lax.broadcasted_iota(jnp.int32, (HALF, 1), 0)
    adj_w = jnp.where(((j == 1) | (j == 6)) & ((row24 < NC - HALF) | (lane < 64)), adj_w, 0.0)
    bar_w = 2.0 * (wk[12] - TAU * adj_w) - wk[0]
    wk[0] = bar_w

    wait_all(dir_r.at[2], fa.at[rows_in])
    for pr in range(NR):
        hg[pl.ds(3 * pr, 3), :] = fa[pl.ds(pr * CP + NC, CP - NC), :]
    hv = hg[pl.ds(0, HALF), :]
    gh, gl = split(jnp.concatenate([hv, pltpu.roll(hv, 64, 1)], 0)[:, 0:CP])
    real = lax.broadcasted_iota(jnp.int32, (CP, 1), 0) < NC

    def dual_three(p, own_bar):
        bars = []
        for r in range(4):
            pr = 4 * p + r
            here = rows_of(pr)
            new = ub[here, :] - TAU * jnp.where(real, fa[here, :], 0.0)
            u1[here, :] = new
            bars.append(2.0 * new - natural(u0, pr, 1, 0, CP))
            own_bar = pack_into(own_bar, bars[r], pr)
        for i in range(2):
            store_pair(gu, 2 * p + i, mm3(gh, gl, jnp.concatenate(bars[2 * i : 2 * i + 2], 1)))
        for r in range(4):
            pr = 4 * p + r
            here = rows_of(pr)
            a = pbr[here, :] + SIGMA * fr(bars[r], bars[r + 1] if r < 3 else None, r)
            b = pbc[here, :] + SIGMA * fx(bars[r], wk[0], pr)
            s = shrink(colsum(a * a + b * b), ALPHA1)
            a, b = a * s, b * s
            p2r[here, :] = a
            p2c[here, :] = b
            wo[pl.ds(pr, CP, stride=2 * NR), :] = v2r[here, :] + TAU * a
            wo[pl.ds(NR + pr, CP, stride=2 * NR), :] = v2c[here, :] + TAU * b
        return own_bar

    own_bar = lax.fori_loop(0, 2, dual_three, zero24)
    bar_w = jnp.where(j == 2, own_bar, wk[0])
    a = wk[10] + SIGMA * fr_w(bar_w)
    b = wk[11] + SIGMA * fx_w(bar_w)
    s = shrink(norm_w(a * a + b * b), ALPHA1)
    wk[3] = b * s
    def primal_two(p, _):
        for r in range(4):
            pr = 4 * p + r
            here = rows_of(pr)
            m = mask[pl.ds(pr, 1), :].astype(f32) * (1.0 / (1.0 + SIGMA))
            above = p2r[rows_of(pr - 1), :] if r > 0 else None
            div = br(p2r[here, :], above, r) + bx(p2c[here, :], wk[3], pr)
            adj = m * (fa[here, :] + SIGMA * gu[here, :])
            u1[here, :] = u1[here, :] - TAU * (adj - div)
        return 0

    lax.fori_loop(0, 2, primal_two, 0)
    wait_all(dir_s.at[0], ra.at[slots])
    wait_all(dir_s.at[1], rb.at[slots])
    wait_all(dir_s.at[2], fa.at[rows_in])
    wait_all(dir_s.at[4], edge_in.at[slots])
    for to_right, to_left in (edges, halos):

        @pl.when(has_right)
        def _():
            to_right.wait_send()

        @pl.when(has_left)
        def _():
            to_left.wait_send()

    wait_all(dir_r.at[3], fb.at[rows_in])

    def add_signals(pr, _):
        m = mask[pl.ds(pr, 1), :].astype(f32) * (TAU * SIGMA / (1.0 + SIGMA))
        uo[pl.ds(pr, CP, stride=NR), :] = u1[rows_of(pr), :] + m * fb[rows_of(pr), :]
        return 0

    lax.fori_loop(0, NR, add_signals, 0, unroll=True)

    wait_all(dir_s.at[3], fb.at[rows_in])


def put_kernel(u, w, u_hbm, w_hbm, sem):
    copies = [
        pltpu.make_async_copy(w.at[pl.ds(0, NC * 2 * NR)], w_hbm, sem.at[0]),
        pltpu.make_async_copy(u.at[pl.ds(0, NC * NR)], u_hbm, sem.at[1]),
    ]
    for c in copies:
        c.start()
    for c in copies:
        c.wait()


def body(nvox, signals, basis, response, shell_index, brain_mask, fodf, aux_field, grad_dual, sym_dual, data_dual):
    hbm = pl.BlockSpec(memory_space=pltpu.HBM)
    vmem = pl.BlockSpec(memory_space=pltpu.VMEM)
    field = pltpu.VMEM((NR * CP + 8, 128), f32)
    pairs = pltpu.VMEM((CP * 2 * NR + 16, 128), f32)
    triples = pltpu.VMEM((CP * 3 * NR + 24, 128), f32)
    measured = pltpu.VMEM((ND * NR + 8, 128), f32)
    npeer = SIDE * SIDE
    dma = lambda n: pltpu.SemaphoreType.DMA((n,))
    edges = pltpu.VMEM((HALF, 128), f32)
    halos = pltpu.VMEM((8 * HALF, 128), f32)
    u, w = pl.pallas_call(
        functools.partial(kernel, nvox),
        out_shape=(field, pairs),
        in_specs=[hbm] * 10,
        out_specs=(vmem, vmem),
        scratch_shapes=[
            pltpu.VMEM((ND * NR, 128), bf16),
            pltpu.VMEM((NC, ND), f32),
            pltpu.VMEM((3, 5), f32),
            pltpu.VMEM((1, ND), jnp.int32),
            pltpu.VMEM((2 * NR, 128), jnp.int32),
            field,
            pairs, pairs, triples,
            measured, measured,
            pltpu.VMEM((CP, 128), f32),
            field, field, field, field,
            pltpu.VMEM((npeer, HALF, 128), f32),
            pltpu.VMEM((npeer, HALF, 128), f32),
            pltpu.VMEM((HALF + 8, 128), f32),
            halos, halos, halos,
            edges, edges, edges,
            pltpu.VMEM((8, 128), f32),
            pltpu.VMEM((npeer, 8, 128), f32),
            pltpu.VMEM((13, HALF, 128), f32),
        ]
        + [field] * 18
        + [dma(10)]
        + [dma(5), dma(5), dma(4), dma(4)],
        compiler_params=pltpu.CompilerParams(
            collective_id=0, has_side_effects=True, vmem_limit_bytes=48 * 1024 * 1024
        ),
    )(*[pltpu.with_memory_space_constraint(x, pltpu.HBM) for x in (
        signals.reshape(ND * NR, 128),
        basis.T,
        response,
        shell_index.reshape(1, ND),
        brain_mask.reshape(NR, 128),
        fodf.reshape(NC * NR, 128),
        aux_field.reshape(NC * 2 * NR, 128),
        grad_dual.reshape(NC * 2 * NR, 128),
        sym_dual.reshape(NC * 3 * NR, 128),
        data_dual.reshape(ND * NR, 128),
    )])
    u, w = pl.pallas_call(
        put_kernel,
        out_shape=(pltpu.HBM((NC * NR, 128), f32), pltpu.HBM((NC * 2 * NR, 128), f32)),
        in_specs=[vmem, vmem],
        out_specs=(hbm, hbm),
        scratch_shapes=[dma(2)],
        compiler_params=pltpu.CompilerParams(vmem_limit_bytes=4 * 1024 * 1024),
    )(pltpu.with_memory_space_constraint(u, pltpu.VMEM), pltpu.with_memory_space_constraint(w, pltpu.VMEM))
    return u.reshape(fodf.shape), w.reshape(aux_field.shape)


def solution(mesh):
    placed = (
        P("dir", None, None, "vox"),
        P("dir", None),
        P(),
        P("dir"),
        P(None, None, "vox"),
        P(None, None, None, "vox"),
        P(None, None, None, None, "vox"),
        P(None, None, None, None, "vox"),
        P(None, None, None, None, "vox"),
        P("dir", None, None, "vox"),
    )
    return jax.shard_map(
        functools.partial(body, mesh.shape["vox"]),
        mesh=mesh,
        in_specs=placed,
        out_specs=(P(None, None, None, "vox"), P(None, None, None, None, "vox")),
        check_vma=False,
    )
```

```python
import functools

import jax
import jax.numpy as jnp
import numpy as np
from jax import lax
from jax.experimental import pallas as pl
from jax.experimental.pallas import tpu as pltpu
from jax.sharding import PartitionSpec as P

MESH = pl.DeviceIdType.MESH
f32 = jnp.float32
bf16 = jnp.bfloat16

SIGMA = 0.25
TAU = 0.3
ALPHA1 = 1.0
ALPHA0 = 1.5
ORDER_STARTS = (1, 6, 15, 28)

NC = 45
CP = 48
HALF = 24
ND = 72
NR = 8
SIDE = 4


def split(x):
    hi = x.astype(bf16)
    return hi, (x - hi.astype(f32)).astype(bf16)


def mm(a, b):
    return jnp.dot(a, b, preferred_element_type=f32)


def mm3(ah, al, x):
    xh, xl = split(x)
    return mm(ah, xh) + mm(ah, xl) + mm(al, xh)


def rows_of(pr):
    start = pr * CP
    return pl.ds(start if isinstance(start, int) else pl.multiple_of(start, 8), CP)


def kernel(
    nvox,
    sig_hbm, basis_hbm, resp_hbm, shell_hbm, mask_hbm, fodf_hbm, aux_hbm, grad_hbm, sym_hbm, dual_hbm,
    uo, wo,
    sig, basis, resp, shell, mask, u0, w0, p0, q0, y0, sigf,
    kt, ta, tb, fa, fb, ra, rb, hg,
    halo, halo_l, halo_r, edge, edge_l, edge_r, edge_c, edge_in, wk,
    p1r, p1c, q1a, q1b, q1c, wbr, wbc, w1r, w1c, pbr, pbc, ub, v2r, v2c, u1, gu, p2r, p2c,
    in_sem, dir_s, dir_r, vox_s, vox_r,
):
    me = lax.axis_index("dir")
    vox = lax.axis_index("vox")
    mx, my = me // SIDE, lax.rem(me, SIDE)
    npeer = SIDE * SIDE
    order = [10, 6, 9, 14, 11, 2, 8, 5, 15, 7, 13, 1, 4, 3, 12]

    def peer(k):
        return lax.rem(mx + k // SIDE, SIDE) * SIDE + lax.rem(my + k % SIDE, SIDE)

    has_left, has_right = vox > 0, vox < nvox - 1
    left, right = vox - 1, vox + 1

    def load(i, src, dst):
        return pltpu.make_async_copy(src, dst, in_sem.at[i])

    loads = [
        load(0, basis_hbm, basis),
        load(1, resp_hbm, resp),
        load(2, shell_hbm, shell),
        load(3, mask_hbm, mask.at[pl.ds(0, NR)]),
        load(4, fodf_hbm, u0.at[pl.ds(0, NC * NR)]),
        load(5, sig_hbm, sig),
        load(6, dual_hbm, y0.at[pl.ds(0, ND * NR)]),
        load(7, aux_hbm, w0.at[pl.ds(0, NC * 2 * NR)]),
        load(8, grad_hbm, p0.at[pl.ds(0, NC * 2 * NR)]),
        load(9, sym_hbm, q0.at[pl.ds(0, NC * 3 * NR)]),
    ]
    barrier = pltpu.get_barrier_semaphore()
    for k in order:
        pl.semaphore_signal(barrier, inc=1, device_id={"dir": peer(k)}, device_id_type=MESH)
    for there, n in ((has_left, left), (has_right, right)):

        @pl.when(there)
        def _():
            pl.semaphore_signal(barrier, inc=1, device_id={"vox": n}, device_id_type=MESH)


    for c in loads[:7]:
        c.start()
    lane = lax.broadcasted_iota(jnp.int32, (1, 128), 1)
    for ref, n in ((u0, 1), (w0, 2), (p0, 2), (q0, 3)):
        ref[pl.ds(NC * n * NR, (CP - NC) * n * NR), :] = jnp.zeros(((CP - NC) * n * NR, 128), f32)

    for c in loads[:3]:
        c.wait()
    kt[...] = jnp.zeros((CP, 128), f32)
    sh = shell[...]
    per_order = [
        jnp.where(sh == 0, resp[0:1, o : o + 1], jnp.where(sh == 1, resp[1:2, o : o + 1], resp[2:3, o : o + 1]))
        for o in range(5)
    ]
    cid = lax.broadcasted_iota(jnp.int32, (NC, 1), 0)
    scale = jnp.broadcast_to(per_order[0], (NC, ND))
    for o, start in enumerate(ORDER_STARTS):
        scale = jnp.where(cid >= start, per_order[o + 1], scale)
    kt[pl.ds(0, NC), pl.ds(0, ND)] = basis[...] * scale
    ktv = kt[...]
    knv = jnp.concatenate([ktv, jnp.zeros((128 - CP, 128), f32)], 0).T[0:ND]
    kth, ktl = split(ktv[:, 0:ND])
    knh128, knl128 = split(knv)
    knh, knl = knh128[:, 0:CP], knl128[:, 0:CP]

    for c in loads[7:]:
        c.start()
    gram = mm3(kth, ktl, knv)
    hg[pl.ds(0, HALF), :] = gram[0:HALF] + pltpu.roll(gram[HALF:CP], 64, 1)
    for c in loads[3:7]:
        c.wait()

    def to_f32(i, _):
        at = pl.ds(pl.multiple_of(i * 96, 96), 96)
        sigf[at, :] = sig[at, :].astype(f32)
        return 0

    lax.fori_loop(0, 6, to_f32, 0)

    def natural(ref, pr, n, comp, count):
        return ref[pl.ds(comp * NR + pr, count, stride=n * NR), :]

    def pair(ref, i, count):
        return jnp.concatenate([natural(ref, 2 * i, 1, 0, count), natural(ref, 2 * i + 1, 1, 0, count)], 1)

    def store_pair(ref, i, val):
        ref[rows_of(2 * i), :] = val[:, 0:128]
        ref[rows_of(2 * i + 1), :] = val[:, 128:256]

    def data_step(i, _):
        pred = mm3(knh, knl, pair(u0, i, CP))
        m = jnp.concatenate([mask[pl.ds(2 * i, 1), :], mask[pl.ds(2 * i + 1, 1), :]], 1).astype(f32)
        y = (m * (1.0 / (1.0 + SIGMA))) * (pair(y0, i, ND) + SIGMA * (pred - pair(sigf, i, ND)))
        store_pair(ta, i, mm3(kth, ktl, y))
        return 0

    lax.fori_loop(0, 4, data_step, 0, unroll=True)

    for pr in range(NR):
        ta[pl.ds(pr * CP + NC, CP - NC), :] = hg[pl.ds(3 * pr, 3), :]

    def chunk(d):
        return pl.ds(pl.multiple_of(d * HALF, HALF), HALF)

    def scatter(src, dst, n):
        return [
            pltpu.make_async_remote_copy(
                src_ref=src.at[chunk(peer(k))], dst_ref=dst.at[i], send_sem=dir_s.at[n], recv_sem=dir_r.at[n],
                device_id={"dir": peer(k)}, device_id_type=MESH)
            for i, k in enumerate(order)
        ]

    def gather(ref, n):
        return [
            pltpu.make_async_remote_copy(
                src_ref=ref.at[chunk(me)], dst_ref=ref.at[chunk(me)], send_sem=dir_s.at[n], recv_sem=dir_r.at[n],
                device_id={"dir": peer(k)}, device_id_type=MESH)
            for k in order
        ]

    def wait_all(sem, ref):
        pltpu.make_async_copy(ref, ref, sem).wait()

    def to_vox(src, dst, n, k):
        return pltpu.make_async_remote_copy(
            src_ref=src, dst_ref=dst, send_sem=vox_s.at[k], recv_sem=vox_r.at[k],
            device_id={"vox": n}, device_id_type=MESH)

    def start_vox(to_right, to_left):
        @pl.when(has_right)
        def _():
            to_right.start()

        @pl.when(has_left)
        def _():
            to_left.start()

    def arrive_vox(to_right, to_left):
        @pl.when(has_left)
        def _():
            to_right.wait_recv()

        @pl.when(has_right)
        def _():
            to_left.wait_recv()

    others = npeer - 1
    slots = pl.ds(0, others)
    rows_in = pl.ds(0, others * HALF)
    slot_of = lane // 8
    j = lax.rem(lane, 8)

    def pack_into(acc, val, pr):
        for h in range(2):
            s = h * NR + pr
            t = pltpu.roll(val[h * HALF : (h + 1) * HALF], 8 * s + 2 if isinstance(s, int) and 8 * s + 2 < 128 else lax.rem(8 * s + 2, 128), 1)
            acc = jnp.where(slot_of == s, t, acc)
        return acc

    zero24 = jnp.zeros((HALF, 128), f32)
    edge[...] = lax.fori_loop(0, NR, lambda pr, acc: pack_into(acc, ta[rows_of(pr), :], pr), zero24)

    pl.semaphore_wait(barrier, others + has_left.astype(jnp.int32) + has_right.astype(jnp.int32))
    edges = to_vox(edge, edge_l, right, 0), to_vox(edge, edge_r, left, 1)
    start_vox(*edges)
    sends = scatter(ta, ra, 0), scatter(tb, rb, 1)
    for c in sends[0]:
        c.start()

    def signal_step(i, _):
        s = pair(sigf, i, ND).astype(bf16)
        store_pair(tb, i, mm(kth, s) + mm(ktl, s))
        return 0

    lax.fori_loop(0, 4, signal_step, 0, unroll=True)
    for c in sends[1]:
        c.start()

    for c in loads[7:]:
        c.wait()

    fields = ((u0, 1, 0), (w0, 2, 0), (w0, 2, 1), (p0, 2, 0), (p0, 2, 1), (q0, 3, 0), (q0, 3, 1), (q0, 3, 2))

    def pack_step(pr, accs):
        return tuple(pack_into(acc, natural(ref, pr, n, comp, CP), pr) for acc, (ref, n, comp) in zip(accs, fields))

    packed = lax.fori_loop(0, NR, pack_step, (zero24,) * 8)
    for f in range(8):
        halo[pl.ds(f * HALF, HALF), :] = packed[f]
    halos = to_vox(halo, halo_l, right, 2), to_vox(halo, halo_r, left, 3)
    start_vox(*halos)

    arrive_vox(*edges)
    near = (
        jnp.where((j == 1) & has_left, edge_l[...], 0.0)
        + jnp.where((j == 6) & has_right, pltpu.roll(edge_r[...], 4, 1), 0.0)
    )
    edge_c[...] = near[0:8] + pltpu.roll(near[8:16], 1, 1) + pltpu.roll(near[16:24], 2, 1)
    for i, k in enumerate(order):
        pltpu.make_async_remote_copy(
            src_ref=edge_c, dst_ref=edge_in.at[i], send_sem=dir_s.at[4], recv_sem=dir_r.at[4],
            device_id={"dir": peer(k)}, device_id_type=MESH).start()

    def reduce_chunk(src, recv, n, full):
        wait_all(dir_r.at[n], recv.at[slots])
        total = src[chunk(me), :]
        for i in range(others):
            total = total + recv[i]
        full[chunk(me), :] = total
        for c in gather(full, n + 2):
            c.start()

    reduce_chunk(ta, ra, 0, fa)
    reduce_chunk(tb, rb, 1, fb)

    arrive_vox(*halos)

    def widen(f):
        at = pl.ds(f * HALF, HALF)
        own = halo[at, :]
        far_l = jnp.where(has_left, halo_l[at, :], 0.0)
        far_r = jnp.where(has_right, halo_r[at, :], 0.0)
        return jnp.where(j < 2, far_l, jnp.where(j < 4, own, pltpu.roll(jnp.where(j < 2, own, far_r), 4, 1)))

    col = jnp.where(j < 4, j - 2, j + 122) + vox * 128
    keep_w = ((col >= 0) & (col < nvox * 128 - 1)).astype(f32)
    rid = lax.rem(lane // 8, 4)
    low_w, high_w = (rid < 3).astype(f32), (rid >= 1).astype(f32)

    def fr_w(x):
        return (pltpu.roll(x, 120, 1) - x) * low_w

    def br_w(x):
        return x * low_w - pltpu.roll(x, 8, 1) * high_w

    def fx_w(x):
        return (pltpu.roll(x, 127, 1) - x) * keep_w

    def bx_w(x):
        return x * keep_w - pltpu.roll(x, 1, 1)

    def shrink(sq, alpha):
        return jnp.minimum(1.0, alpha * lax.rsqrt(sq))

    def norm_w(sq):
        n = jnp.sum(sq, 0, keepdims=True)
        return n + pltpu.roll(n, 64, 1)

    def dual_p_w(pr_, pc_, u_, wr_, wc_):
        a = pr_ + SIGMA * (fr_w(u_) - wr_)
        b = pc_ + SIGMA * (fx_w(u_) - wc_)
        s = shrink(norm_w(a * a + b * b), ALPHA1)
        return a * s, b * s

    def dual_q_w(qa_, qb_, qc_, wr_, wc_):
        a = qa_ + SIGMA * br_w(wr_)
        b = qb_ + SIGMA * bx_w(wc_)
        c = qc_ + (0.5 * SIGMA) * (bx_w(wr_) + br_w(wc_))
        s = shrink(norm_w(a * a + b * b + 2.0 * (c * c)), ALPHA0)
        return a * s, b * s, c * s

    uw, wrw, wcw = widen(0), widen(1), widen(2)
    p1rw, p1cw = dual_p_w(widen(3), widen(4), uw, wrw, wcw)
    q1aw, q1bw, q1cw = dual_q_w(widen(5), widen(6), widen(7), wrw, wcw)
    w1rw = wrw + TAU * (p1rw + fr_w(q1aw) + fx_w(q1cw))
    w1cw = wcw + TAU * (p1cw + fx_w(q1bw) + fr_w(q1cw))
    wbrw, wbcw = 2.0 * w1rw - wrw, 2.0 * w1cw - wcw
    _, q2bw, q2cw = dual_q_w(q1aw, q1bw, q1cw, wbrw, wbcw)
    pbrw, pbcw = p1rw - SIGMA * wbrw, p1cw - SIGMA * wbcw
    ubw = uw + TAU * (br_w(p1rw) + bx_w(p1cw))
    for n, val in enumerate((uw, wrw, wcw, p1cw, q1bw, q1cw, wbrw, wbcw, q2bw, q2cw, pbrw, pbcw, ubw)):
        wk[n] = val

    keep = jnp.where(lane + vox * 128 < nvox * 128 - 1, 1.0, 0.0).astype(f32)

    def beside(val, pr, at):
        parts = [pltpu.roll(val, at - 8 * (h * NR + pr), 1) for h in range(2)]
        return jnp.concatenate(parts, 0)

    def nxt(x, far, pr):
        return jnp.where(lane == 127, beside(far, pr, 121), pltpu.roll(x, 127, 1))

    def prv(x, far, pr):
        return jnp.where(lane == 0, beside(far, pr, 127), pltpu.roll(x, 1, 1))

    def fx(x, far, pr):
        return (nxt(x, far, pr) - x) * keep

    def bx(x, far, pr):
        return x * keep - prv(x, far, pr)

    def fr(x, below, r):
        return below - x if r < 3 else jnp.zeros_like(x)

    def br(x, above, r):
        if r == 0:
            return x
        return x - above if r < 3 else -above

    def colsum(x):
        return jnp.sum(x, 0, keepdims=True)

    def dual_one(p, _):
        for r in range(4):
            pr = 4 * p + r
            u = natural(u0, pr, 1, 0, CP)
            below = natural(u0, pr + 1, 1, 0, CP) if r < 3 else None
            wr, wc = natural(w0, pr, 2, 0, CP), natural(w0, pr, 2, 1, CP)
            a = natural(p0, pr, 2, 0, CP) + SIGMA * (fr(u, below, r) - wr)
            b = natural(p0, pr, 2, 1, CP) + SIGMA * (fx(u, wk[0], pr) - wc)
            s = shrink(colsum(a * a + b * b), ALPHA1)
            p1r[rows_of(pr), :] = a * s
            p1c[rows_of(pr), :] = b * s
            wra = natural(w0, pr - 1, 2, 0, CP) if r > 0 else None
            wca = natural(w0, pr - 1, 2, 1, CP) if r > 0 else None
            a = natural(q0, pr, 3, 0, CP) + SIGMA * br(wr, wra, r)
            b = natural(q0, pr, 3, 1, CP) + SIGMA * bx(wc, wk[2], pr)
            c = natural(q0, pr, 3, 2, CP) + (0.5 * SIGMA) * (bx(wr, wk[1], pr) + br(wc, wca, r))
            s = shrink(colsum(a * a + b * b + 2.0 * (c * c)), ALPHA0)
            q1a[rows_of(pr), :] = a * s
            q1b[rows_of(pr), :] = b * s
            q1c[rows_of(pr), :] = c * s
        return 0

    lax.fori_loop(0, 2, dual_one, 0)


    def primal_one(p, _):
        for r in range(4):
            pr = 4 * p + r
            here = rows_of(pr)
            pr_, pc_ = p1r[here, :], p1c[here, :]
            above = p1r[rows_of(pr - 1), :] if r > 0 else None
            ub[here, :] = natural(u0, pr, 1, 0, CP) + TAU * (br(pr_, above, r) + bx(pc_, wk[3], pr))
            qa, qb, qc = q1a[here, :], q1b[here, :], q1c[here, :]
            qab = q1a[rows_of(pr + 1), :] if r < 3 else None
            qcb = q1c[rows_of(pr + 1), :] if r < 3 else None
            wr, wc = natural(w0, pr, 2, 0, CP), natural(w0, pr, 2, 1, CP)
            dr = TAU * (pr_ + fr(qa, qab, r) + fx(qc, wk[5], pr))
            dc = TAU * (pc_ + fx(qb, wk[4], pr) + fr(qc, qcb, r))
            nr, nc = wr + 2.0 * dr, wc + 2.0 * dc
            w1r[here, :] = wr + dr
            w1c[here, :] = wc + dc
            wbr[here, :] = nr
            wbc[here, :] = nc
            pbr[here, :] = pr_ - SIGMA * nr
            pbc[here, :] = pc_ - SIGMA * nc
        return 0

    lax.fori_loop(0, 2, primal_one, 0)

    def dual_two(p, _):
        for r in range(4):
            pr = 4 * p + r
            here = rows_of(pr)
            wr, wc = wbr[here, :], wbc[here, :]
            wra = wbr[rows_of(pr - 1), :] if r > 0 else None
            wca = wbc[rows_of(pr - 1), :] if r > 0 else None
            a = q1a[here, :] + SIGMA * br(wr, wra, r)
            b = q1b[here, :] + SIGMA * bx(wc, wk[7], pr)
            c = q1c[here, :] + (0.5 * SIGMA) * (bx(wr, wk[6], pr) + br(wc, wca, r))
            s = shrink(colsum(a * a + b * b + 2.0 * (c * c)), ALPHA0)
            q1a[here, :] = a * s
            q1b[here, :] = b * s
            q1c[here, :] = c * s
        return 0

    lax.fori_loop(0, 2, dual_two, 0)

    def aux_two(p, _):
        for r in range(4):
            pr = 4 * p + r
            here = rows_of(pr)
            qa, qb, qc = q1a[here, :], q1b[here, :], q1c[here, :]
            qab = q1a[rows_of(pr + 1), :] if r < 3 else None
            qcb = q1c[rows_of(pr + 1), :] if r < 3 else None
            v2r[here, :] = w1r[here, :] + TAU * (fr(qa, qab, r) + fx(qc, wk[9], pr))
            v2c[here, :] = w1c[here, :] + TAU * (fx(qb, wk[8], pr) + fr(qc, qcb, r))
        return 0

    lax.fori_loop(0, 2, aux_two, 0)

    wait_all(dir_r.at[4], edge_in.at[slots])
    total = edge_c[...]
    for i in range(others):
        total = total + edge_in[i]
    adj_w = jnp.concatenate([total, pltpu.roll(total, 127, 1), pltpu.roll(total, 126, 1)], 0)
    row24 = lax.broadcasted_iota(jnp.int32, (HALF, 1), 0)
    adj_w = jnp.where(((j == 1) | (j == 6)) & ((row24 < NC - HALF) | (lane < 64)), adj_w, 0.0)
    bar_w = 2.0 * (wk[12] - TAU * adj_w) - wk[0]
    wk[0] = bar_w

    wait_all(dir_r.at[2], fa.at[rows_in])
    for pr in range(NR):
        hg[pl.ds(3 * pr, 3), :] = fa[pl.ds(pr * CP + NC, CP - NC), :]
    hv = hg[pl.ds(0, HALF), :]
    gh, gl = split(jnp.concatenate([hv, pltpu.roll(hv, 64, 1)], 0)[:, 0:CP])
    real = lax.broadcasted_iota(jnp.int32, (CP, 1), 0) < NC

    def dual_three(p, own_bar):
        bars = []
        for r in range(4):
            pr = 4 * p + r
            here = rows_of(pr)
            new = ub[here, :] - TAU * jnp.where(real, fa[here, :], 0.0)
            u1[here, :] = new
            bars.append(2.0 * new - natural(u0, pr, 1, 0, CP))
            own_bar = pack_into(own_bar, bars[r], pr)
        for i in range(2):
            store_pair(gu, 2 * p + i, mm3(gh, gl, jnp.concatenate(bars[2 * i : 2 * i + 2], 1)))
        for r in range(4):
            pr = 4 * p + r
            here = rows_of(pr)
            a = pbr[here, :] + SIGMA * fr(bars[r], bars[r + 1] if r < 3 else None, r)
            b = pbc[here, :] + SIGMA * fx(bars[r], wk[0], pr)
            s = shrink(colsum(a * a + b * b), ALPHA1)
            a, b = a * s, b * s
            p2r[here, :] = a
            p2c[here, :] = b
            wo[pl.ds(pr, CP, stride=2 * NR), :] = v2r[here, :] + TAU * a
            wo[pl.ds(NR + pr, CP, stride=2 * NR), :] = v2c[here, :] + TAU * b
        return own_bar

    own_bar = lax.fori_loop(0, 2, dual_three, zero24)
    bar_w = jnp.where(j == 2, own_bar, wk[0])
    a = wk[10] + SIGMA * fr_w(bar_w)
    b = wk[11] + SIGMA * fx_w(bar_w)
    s = shrink(norm_w(a * a + b * b), ALPHA1)
    wk[3] = b * s
    def primal_two(p, _):
        for r in range(4):
            pr = 4 * p + r
            here = rows_of(pr)
            m = mask[pl.ds(pr, 1), :].astype(f32) * (1.0 / (1.0 + SIGMA))
            above = p2r[rows_of(pr - 1), :] if r > 0 else None
            div = br(p2r[here, :], above, r) + bx(p2c[here, :], wk[3], pr)
            adj = m * (fa[here, :] + SIGMA * gu[here, :])
            u1[here, :] = u1[here, :] - TAU * (adj - div)
        return 0

    lax.fori_loop(0, 2, primal_two, 0)
    wait_all(dir_s.at[0], ra.at[slots])
    wait_all(dir_s.at[1], rb.at[slots])
    wait_all(dir_s.at[2], fa.at[rows_in])
    wait_all(dir_s.at[4], edge_in.at[slots])
    for to_right, to_left in (edges, halos):

        @pl.when(has_right)
        def _():
            to_right.wait_send()

        @pl.when(has_left)
        def _():
            to_left.wait_send()

    wait_all(dir_r.at[3], fb.at[rows_in])

    def add_signals(pr, _):
        m = mask[pl.ds(pr, 1), :].astype(f32) * (TAU * SIGMA / (1.0 + SIGMA))
        uo[pl.ds(pr, CP, stride=NR), :] = u1[rows_of(pr), :] + m * fb[rows_of(pr), :]
        return 0

    lax.fori_loop(0, NR, add_signals, 0, unroll=True)

    wait_all(dir_s.at[3], fb.at[rows_in])


def put_kernel(u, w, u_hbm, w_hbm, sem):
    copies = [
        pltpu.make_async_copy(w.at[pl.ds(0, NC * 2 * NR)], w_hbm, sem.at[0]),
        pltpu.make_async_copy(u.at[pl.ds(0, NC * NR)], u_hbm, sem.at[1]),
    ]
    for c in copies:
        c.start()
    for c in copies:
        c.wait()


def body(nvox, signals, basis, response, shell_index, brain_mask, fodf, aux_field, grad_dual, sym_dual, data_dual):
    hbm = pl.BlockSpec(memory_space=pltpu.HBM)
    vmem = pl.BlockSpec(memory_space=pltpu.VMEM)
    field = pltpu.VMEM((NR * CP + 8, 128), f32)
    pairs = pltpu.VMEM((CP * 2 * NR + 16, 128), f32)
    triples = pltpu.VMEM((CP * 3 * NR + 24, 128), f32)
    measured = pltpu.VMEM((ND * NR + 8, 128), f32)
    npeer = SIDE * SIDE
    dma = lambda n: pltpu.SemaphoreType.DMA((n,))
    edges = pltpu.VMEM((HALF, 128), f32)
    halos = pltpu.VMEM((8 * HALF, 128), f32)
    u, w = pl.pallas_call(
        functools.partial(kernel, nvox),
        out_shape=(field, pairs),
        in_specs=[hbm] * 10,
        out_specs=(vmem, vmem),
        scratch_shapes=[
            pltpu.VMEM((ND * NR, 128), bf16),
            pltpu.VMEM((NC, ND), f32),
            pltpu.VMEM((3, 5), f32),
            pltpu.VMEM((1, ND), jnp.int32),
            pltpu.VMEM((2 * NR, 128), jnp.int32),
            field,
            pairs, pairs, triples,
            measured, measured,
            pltpu.VMEM((CP, 128), f32),
            field, field, field, field,
            pltpu.VMEM((npeer, HALF, 128), f32),
            pltpu.VMEM((npeer, HALF, 128), f32),
            pltpu.VMEM((HALF + 8, 128), f32),
            halos, halos, halos,
            edges, edges, edges,
            pltpu.VMEM((8, 128), f32),
            pltpu.VMEM((npeer, 8, 128), f32),
            pltpu.VMEM((13, HALF, 128), f32),
        ]
        + [field] * 18
        + [dma(10)]
        + [dma(5), dma(5), dma(4), dma(4)],
        compiler_params=pltpu.CompilerParams(
            collective_id=0, has_side_effects=True, vmem_limit_bytes=48 * 1024 * 1024
        ),
    )(*[pltpu.with_memory_space_constraint(x, pltpu.HBM) for x in (
        signals.reshape(ND * NR, 128),
        basis.T,
        response,
        shell_index.reshape(1, ND),
        brain_mask.reshape(NR, 128),
        fodf.reshape(NC * NR, 128),
        aux_field.reshape(NC * 2 * NR, 128),
        grad_dual.reshape(NC * 2 * NR, 128),
        sym_dual.reshape(NC * 3 * NR, 128),
        data_dual.reshape(ND * NR, 128),
    )])
    u, w = pl.pallas_call(
        put_kernel,
        out_shape=(pltpu.HBM((NC * NR, 128), f32), pltpu.HBM((NC * 2 * NR, 128), f32)),
        in_specs=[vmem, vmem],
        out_specs=(hbm, hbm),
        scratch_shapes=[dma(2)],
        compiler_params=pltpu.CompilerParams(vmem_limit_bytes=4 * 1024 * 1024),
    )(pltpu.with_memory_space_constraint(u, pltpu.VMEM), pltpu.with_memory_space_constraint(w, pltpu.VMEM))
    return u.reshape(fodf.shape), w.reshape(aux_field.shape)


def solution(mesh):
    placed = (
        P("dir", None, None, "vox"),
        P("dir", None),
        P(),
        P("dir"),
        P(None, None, "vox"),
        P(None, None, None, "vox"),
        P(None, None, None, None, "vox"),
        P(None, None, None, None, "vox"),
        P(None, None, None, None, "vox"),
        P("dir", None, None, "vox"),
    )
    return jax.shard_map(
        functools.partial(body, mesh.shape["vox"]),
        mesh=mesh,
        in_specs=placed,
        out_specs=(P(None, None, None, "vox"), P(None, None, None, None, "vox")),
        check_vma=False,
    )
```

```python
import functools

import jax
import jax.numpy as jnp
import numpy as np
from jax import lax
from jax.experimental import pallas as pl
from jax.experimental.pallas import tpu as pltpu
from jax.sharding import PartitionSpec as P

MESH = pl.DeviceIdType.MESH
f32 = jnp.float32
bf16 = jnp.bfloat16

SIGMA = 0.25
TAU = 0.3
ALPHA1 = 1.0
ALPHA0 = 1.5
ORDER_STARTS = (1, 6, 15, 28)

NC = 45
CP = 48
HALF = 24
ND = 72
NR = 8
SIDE = 4


def split(x):
    hi = x.astype(bf16)
    return hi, (x - hi.astype(f32)).astype(bf16)


def mm(a, b):
    return jnp.dot(a, b, preferred_element_type=f32)


def mm3(ah, al, x):
    xh, xl = split(x)
    return mm(ah, xh) + mm(ah, xl) + mm(al, xh)


def rows_of(pr):
    start = pr * CP
    return pl.ds(start if isinstance(start, int) else pl.multiple_of(start, 8), CP)


def kernel(
    nvox,
    sig_hbm, basis_hbm, resp_hbm, shell_hbm, mask_hbm, fodf_hbm, aux_hbm, grad_hbm, sym_hbm, dual_hbm,
    uo, wo,
    sig, basis, resp, shell, mask, u0, w0, p0, q0, y0, sigf,
    kt, ta, tb, fa, fb, ra, rb, hg,
    halo, halo_l, halo_r, edge, edge_l, edge_r, edge_c, edge_in, wk,
    p1r, p1c, q1a, q1b, q1c, wbr, wbc, w1r, w1c, pbr, pbc, ub, v2r, v2c, u1, gu, p2r, p2c,
    in_sem, dir_s, dir_r, vox_s, vox_r,
):
    me = lax.axis_index("dir")
    vox = lax.axis_index("vox")
    odd = lax.rem(vox, 2) == 1
    mx, my = me // SIDE, lax.rem(me, SIDE)
    npeer = SIDE * SIDE
    order = [10, 6, 9, 14, 11, 2, 8, 5, 15, 7, 13, 1, 4, 3, 12]

    def peer(k):
        dx, dy = k // SIDE, k % SIDE
        ex, ey = jnp.where(odd, (SIDE - dy) % SIDE, dx), jnp.where(odd, (SIDE - dx) % SIDE, dy)
        return lax.rem(mx + ex, SIDE) * SIDE + lax.rem(my + ey, SIDE)

    has_left, has_right = vox > 0, vox < nvox - 1
    left, right = vox - 1, vox + 1

    def load(i, src, dst):
        return pltpu.make_async_copy(src, dst, in_sem.at[i])

    loads = [
        load(0, basis_hbm, basis),
        load(1, resp_hbm, resp),
        load(2, shell_hbm, shell),
        load(3, mask_hbm, mask.at[pl.ds(0, NR)]),
        load(4, fodf_hbm, u0.at[pl.ds(0, NC * NR)]),
        load(5, sig_hbm, sig),
        load(6, dual_hbm, y0.at[pl.ds(0, ND * NR)]),
        load(7, aux_hbm, w0.at[pl.ds(0, NC * 2 * NR)]),
        load(8, grad_hbm, p0.at[pl.ds(0, NC * 2 * NR)]),
        load(9, sym_hbm, q0.at[pl.ds(0, NC * 3 * NR)]),
    ]
    for c in loads[:7]:
        c.start()
    barrier = pltpu.get_barrier_semaphore()
    for k in order:
        pl.semaphore_signal(barrier, inc=1, device_id={"dir": peer(k)}, device_id_type=MESH)
    for there, n in ((has_left, left), (has_right, right)):

        @pl.when(there)
        def _():
            pl.semaphore_signal(barrier, inc=1, device_id={"vox": n}, device_id_type=MESH)


    lane = lax.broadcasted_iota(jnp.int32, (1, 128), 1)
    for ref, n in ((u0, 1), (w0, 2), (p0, 2), (q0, 3)):
        ref[pl.ds(NC * n * NR, (CP - NC) * n * NR), :] = jnp.zeros(((CP - NC) * n * NR, 128), f32)

    for c in loads[:3]:
        c.wait()
    kt[...] = jnp.zeros((CP, 128), f32)
    sh = shell[...]
    per_order = [
        jnp.where(sh == 0, resp[0:1, o : o + 1], jnp.where(sh == 1, resp[1:2, o : o + 1], resp[2:3, o : o + 1]))
        for o in range(5)
    ]
    cid = lax.broadcasted_iota(jnp.int32, (NC, 1), 0)
    scale = jnp.broadcast_to(per_order[0], (NC, ND))
    for o, start in enumerate(ORDER_STARTS):
        scale = jnp.where(cid >= start, per_order[o + 1], scale)
    kt[pl.ds(0, NC), pl.ds(0, ND)] = basis[...] * scale
    ktv = kt[...]
    knv = jnp.concatenate([ktv, jnp.zeros((128 - CP, 128), f32)], 0).T[0:ND]
    kth, ktl = split(ktv[:, 0:ND])
    knh128, knl128 = split(knv)
    knh, knl = knh128[:, 0:CP], knl128[:, 0:CP]

    for c in loads[7:]:
        c.start()
    gram = mm3(kth, ktl, knv)
    hg[pl.ds(0, HALF), :] = gram[0:HALF] + pltpu.roll(gram[HALF:CP], 64, 1)
    for c in loads[3:7]:
        c.wait()

    def to_f32(i, _):
        at = pl.ds(pl.multiple_of(i * 96, 96), 96)
        sigf[at, :] = sig[at, :].astype(f32)
        return 0

    lax.fori_loop(0, 6, to_f32, 0)

    def natural(ref, pr, n, comp, count):
        return ref[pl.ds(comp * NR + pr, count, stride=n * NR), :]

    def pair(ref, i, count):
        return jnp.concatenate([natural(ref, 2 * i, 1, 0, count), natural(ref, 2 * i + 1, 1, 0, count)], 1)

    def store_pair(ref, i, val):
        ref[rows_of(2 * i), :] = val[:, 0:128]
        ref[rows_of(2 * i + 1), :] = val[:, 128:256]

    def data_step(i, _):
        pred = mm3(knh, knl, pair(u0, i, CP))
        m = jnp.concatenate([mask[pl.ds(2 * i, 1), :], mask[pl.ds(2 * i + 1, 1), :]], 1).astype(f32)
        y = (m * (1.0 / (1.0 + SIGMA))) * (pair(y0, i, ND) + SIGMA * (pred - pair(sigf, i, ND)))
        store_pair(ta, i, mm3(kth, ktl, y))
        return 0

    lax.fori_loop(0, 4, data_step, 0, unroll=True)

    for pr in range(NR):
        ta[pl.ds(pr * CP + NC, CP - NC), :] = hg[pl.ds(3 * pr, 3), :]

    def signal_step(i, _):
        s = pair(sigf, i, ND).astype(bf16)
        store_pair(tb, i, mm(kth, s) + mm(ktl, s))
        return 0

    lax.fori_loop(0, 4, signal_step, 0, unroll=True)
    def chunk(d):
        return pl.ds(pl.multiple_of(d * HALF, HALF), HALF)

    def scatter(src, dst, n):
        return [
            pltpu.make_async_remote_copy(
                src_ref=src.at[chunk(peer(k))], dst_ref=dst.at[i], send_sem=dir_s.at[n], recv_sem=dir_r.at[n],
                device_id={"dir": peer(k)}, device_id_type=MESH)
            for i, k in enumerate(order)
        ]

    def gather(ref, n):
        return [
            pltpu.make_async_remote_copy(
                src_ref=ref.at[chunk(me)], dst_ref=ref.at[chunk(me)], send_sem=dir_s.at[n], recv_sem=dir_r.at[n],
                device_id={"dir": peer(k)}, device_id_type=MESH)
            for k in order
        ]

    def wait_all(sem, ref):
        pltpu.make_async_copy(ref, ref, sem).wait()

    def to_vox(src, dst, n, k):
        return pltpu.make_async_remote_copy(
            src_ref=src, dst_ref=dst, send_sem=vox_s.at[k], recv_sem=vox_r.at[k],
            device_id={"vox": n}, device_id_type=MESH)

    def start_vox(to_right, to_left):
        @pl.when(has_right)
        def _():
            to_right.start()

        @pl.when(has_left)
        def _():
            to_left.start()

    def arrive_vox(to_right, to_left):
        @pl.when(has_left)
        def _():
            to_right.wait_recv()

        @pl.when(has_right)
        def _():
            to_left.wait_recv()

    others = npeer - 1
    slots = pl.ds(0, others)
    rows_in = pl.ds(0, others * HALF)
    slot_of = lane // 8
    j = lax.rem(lane, 8)

    def pack_into(acc, val, pr):
        for h in range(2):
            s = h * NR + pr
            t = pltpu.roll(val[h * HALF : (h + 1) * HALF], 8 * s + 2 if isinstance(s, int) and 8 * s + 2 < 128 else lax.rem(8 * s + 2, 128), 1)
            acc = jnp.where(slot_of == s, t, acc)
        return acc

    zero24 = jnp.zeros((HALF, 128), f32)
    edge[...] = lax.fori_loop(0, NR, lambda pr, acc: pack_into(acc, ta[rows_of(pr), :], pr), zero24)

    pl.semaphore_wait(barrier, others + has_left.astype(jnp.int32) + has_right.astype(jnp.int32))
    edges = to_vox(edge, edge_l, right, 0), to_vox(edge, edge_r, left, 1)
    start_vox(*edges)
    far = [min(k // SIDE, SIDE - k // SIDE) + min(k % SIDE, SIDE - k % SIDE) for k in order]
    sends = scatter(ta, ra, 0), scatter(tb, rb, 1)
    for n, least, most in ((0, 2, 4), (1, 3, 4), (0, 1, 1), (1, 2, 2), (1, 1, 1)):
        for c, hops in zip(sends[n], far):
            if least <= hops <= most:
                c.start()

    for c in loads[7:]:
        c.wait()

    fields = ((u0, 1, 0), (w0, 2, 0), (w0, 2, 1), (p0, 2, 0), (p0, 2, 1), (q0, 3, 0), (q0, 3, 1), (q0, 3, 2))

    def pack_step(pr, accs):
        return tuple(pack_into(acc, natural(ref, pr, n, comp, CP), pr) for acc, (ref, n, comp) in zip(accs, fields))

    packed = lax.fori_loop(0, NR, pack_step, (zero24,) * 8)
    for f in range(8):
        halo[pl.ds(f * HALF, HALF), :] = packed[f]
    halos = to_vox(halo, halo_l, right, 2), to_vox(halo, halo_r, left, 3)
    start_vox(*halos)

    arrive_vox(*edges)
    near = (
        jnp.where((j == 1) & has_left, edge_l[...], 0.0)
        + jnp.where((j == 6) & has_right, pltpu.roll(edge_r[...], 4, 1), 0.0)
    )
    edge_c[...] = near[0:8] + pltpu.roll(near[8:16], 1, 1) + pltpu.roll(near[16:24], 2, 1)
    for i, k in enumerate(order):
        pltpu.make_async_remote_copy(
            src_ref=edge_c, dst_ref=edge_in.at[i], send_sem=dir_s.at[4], recv_sem=dir_r.at[4],
            device_id={"dir": peer(k)}, device_id_type=MESH).start()

    def reduce_chunk(src, recv, n, full):
        wait_all(dir_r.at[n], recv.at[slots])
        total = src[chunk(me), :]
        for i in range(others):
            total = total + recv[i]
        full[chunk(me), :] = total
        for c in gather(full, n + 2):
            c.start()

    reduce_chunk(ta, ra, 0, fa)
    reduce_chunk(tb, rb, 1, fb)

    arrive_vox(*halos)

    def widen(f):
        at = pl.ds(f * HALF, HALF)
        own = halo[at, :]
        far_l = jnp.where(has_left, halo_l[at, :], 0.0)
        far_r = jnp.where(has_right, halo_r[at, :], 0.0)
        return jnp.where(j < 2, far_l, jnp.where(j < 4, own, pltpu.roll(jnp.where(j < 2, own, far_r), 4, 1)))

    col = jnp.where(j < 4, j - 2, j + 122) + vox * 128
    keep_w = ((col >= 0) & (col < nvox * 128 - 1)).astype(f32)
    rid = lax.rem(lane // 8, 4)
    low_w, high_w = (rid < 3).astype(f32), (rid >= 1).astype(f32)

    def fr_w(x):
        return (pltpu.roll(x, 120, 1) - x) * low_w

    def br_w(x):
        return x * low_w - pltpu.roll(x, 8, 1) * high_w

    def fx_w(x):
        return (pltpu.roll(x, 127, 1) - x) * keep_w

    def bx_w(x):
        return x * keep_w - pltpu.roll(x, 1, 1)

    def shrink(sq, alpha):
        return jnp.minimum(1.0, alpha * lax.rsqrt(sq))

    def norm_w(sq):
        n = jnp.sum(sq, 0, keepdims=True)
        return n + pltpu.roll(n, 64, 1)

    def dual_p_w(pr_, pc_, u_, wr_, wc_):
        a = pr_ + SIGMA * (fr_w(u_) - wr_)
        b = pc_ + SIGMA * (fx_w(u_) - wc_)
        s = shrink(norm_w(a * a + b * b), ALPHA1)
        return a * s, b * s

    def dual_q_w(qa_, qb_, qc_, wr_, wc_):
        a = qa_ + SIGMA * br_w(wr_)
        b = qb_ + SIGMA * bx_w(wc_)
        c = qc_ + (0.5 * SIGMA) * (bx_w(wr_) + br_w(wc_))
        s = shrink(norm_w(a * a + b * b + 2.0 * (c * c)), ALPHA0)
        return a * s, b * s, c * s

    uw, wrw, wcw = widen(0), widen(1), widen(2)
    p1rw, p1cw = dual_p_w(widen(3), widen(4), uw, wrw, wcw)
    q1aw, q1bw, q1cw = dual_q_w(widen(5), widen(6), widen(7), wrw, wcw)
    w1rw = wrw + TAU * (p1rw + fr_w(q1aw) + fx_w(q1cw))
    w1cw = wcw + TAU * (p1cw + fx_w(q1bw) + fr_w(q1cw))
    wbrw, wbcw = 2.0 * w1rw - wrw, 2.0 * w1cw - wcw
    _, q2bw, q2cw = dual_q_w(q1aw, q1bw, q1cw, wbrw, wbcw)
    pbrw, pbcw = p1rw - SIGMA * wbrw, p1cw - SIGMA * wbcw
    ubw = uw + TAU * (br_w(p1rw) + bx_w(p1cw))
    for n, val in enumerate((uw, wrw, wcw, p1cw, q1bw, q1cw, wbrw, wbcw, q2bw, q2cw, pbrw, pbcw, ubw)):
        wk[n] = val

    keep = jnp.where(lane + vox * 128 < nvox * 128 - 1, 1.0, 0.0).astype(f32)

    def beside(val, pr, at):
        parts = [pltpu.roll(val, at - 8 * (h * NR + pr), 1) for h in range(2)]
        return jnp.concatenate(parts, 0)

    def nxt(x, far, pr):
        return jnp.where(lane == 127, beside(far, pr, 121), pltpu.roll(x, 127, 1))

    def prv(x, far, pr):
        return jnp.where(lane == 0, beside(far, pr, 127), pltpu.roll(x, 1, 1))

    def fx(x, far, pr):
        return (nxt(x, far, pr) - x) * keep

    def bx(x, far, pr):
        return x * keep - prv(x, far, pr)

    def fr(x, below, r):
        return below - x if r < 3 else jnp.zeros_like(x)

    def br(x, above, r):
        if r == 0:
            return x
        return x - above if r < 3 else -above

    def colsum(x):
        return jnp.sum(x, 0, keepdims=True)

    def dual_one(p, _):
        for r in range(4):
            pr = 4 * p + r
            u = natural(u0, pr, 1, 0, CP)
            below = natural(u0, pr + 1, 1, 0, CP) if r < 3 else None
            wr, wc = natural(w0, pr, 2, 0, CP), natural(w0, pr, 2, 1, CP)
            a = natural(p0, pr, 2, 0, CP) + SIGMA * (fr(u, below, r) - wr)
            b = natural(p0, pr, 2, 1, CP) + SIGMA * (fx(u, wk[0], pr) - wc)
            s = shrink(colsum(a * a + b * b), ALPHA1)
            p1r[rows_of(pr), :] = a * s
            p1c[rows_of(pr), :] = b * s
            wra = natural(w0, pr - 1, 2, 0, CP) if r > 0 else None
            wca = natural(w0, pr - 1, 2, 1, CP) if r > 0 else None
            a = natural(q0, pr, 3, 0, CP) + SIGMA * br(wr, wra, r)
            b = natural(q0, pr, 3, 1, CP) + SIGMA * bx(wc, wk[2], pr)
            c = natural(q0, pr, 3, 2, CP) + (0.5 * SIGMA) * (bx(wr, wk[1], pr) + br(wc, wca, r))
            s = shrink(colsum(a * a + b * b + 2.0 * (c * c)), ALPHA0)
            q1a[rows_of(pr), :] = a * s
            q1b[rows_of(pr), :] = b * s
            q1c[rows_of(pr), :] = c * s
        return 0

    lax.fori_loop(0, 2, dual_one, 0)


    def primal_one(p, _):
        for r in range(4):
            pr = 4 * p + r
            here = rows_of(pr)
            pr_, pc_ = p1r[here, :], p1c[here, :]
            above = p1r[rows_of(pr - 1), :] if r > 0 else None
            ub[here, :] = natural(u0, pr, 1, 0, CP) + TAU * (br(pr_, above, r) + bx(pc_, wk[3], pr))
            qa, qb, qc = q1a[here, :], q1b[here, :], q1c[here, :]
            qab = q1a[rows_of(pr + 1), :] if r < 3 else None
            qcb = q1c[rows_of(pr + 1), :] if r < 3 else None
            wr, wc = natural(w0, pr, 2, 0, CP), natural(w0, pr, 2, 1, CP)
            dr = TAU * (pr_ + fr(qa, qab, r) + fx(qc, wk[5], pr))
            dc = TAU * (pc_ + fx(qb, wk[4], pr) + fr(qc, qcb, r))
            nr, nc = wr + 2.0 * dr, wc + 2.0 * dc
            w1r[here, :] = wr + dr
            w1c[here, :] = wc + dc
            wbr[here, :] = nr
            wbc[here, :] = nc
            pbr[here, :] = pr_ - SIGMA * nr
            pbc[here, :] = pc_ - SIGMA * nc
        return 0

    lax.fori_loop(0, 2, primal_one, 0)

    def dual_two(p, _):
        for r in range(4):
            pr = 4 * p + r
            here = rows_of(pr)
            wr, wc = wbr[here, :], wbc[here, :]
            wra = wbr[rows_of(pr - 1), :] if r > 0 else None
            wca = wbc[rows_of(pr - 1), :] if r > 0 else None
            a = q1a[here, :] + SIGMA * br(wr, wra, r)
            b = q1b[here, :] + SIGMA * bx(wc, wk[7], pr)
            c = q1c[here, :] + (0.5 * SIGMA) * (bx(wr, wk[6], pr) + br(wc, wca, r))
            s = shrink(colsum(a * a + b * b + 2.0 * (c * c)), ALPHA0)
            q1a[here, :] = a * s
            q1b[here, :] = b * s
            q1c[here, :] = c * s
        return 0

    lax.fori_loop(0, 2, dual_two, 0)

    def aux_two(p, _):
        for r in range(4):
            pr = 4 * p + r
            here = rows_of(pr)
            qa, qb, qc = q1a[here, :], q1b[here, :], q1c[here, :]
            qab = q1a[rows_of(pr + 1), :] if r < 3 else None
            qcb = q1c[rows_of(pr + 1), :] if r < 3 else None
            v2r[here, :] = w1r[here, :] + TAU * (fr(qa, qab, r) + fx(qc, wk[9], pr))
            v2c[here, :] = w1c[here, :] + TAU * (fx(qb, wk[8], pr) + fr(qc, qcb, r))
        return 0

    lax.fori_loop(0, 2, aux_two, 0)

    wait_all(dir_r.at[4], edge_in.at[slots])
    total = edge_c[...]
    for i in range(others):
        total = total + edge_in[i]
    adj_w = jnp.concatenate([total, pltpu.roll(total, 127, 1), pltpu.roll(total, 126, 1)], 0)
    row24 = lax.broadcasted_iota(jnp.int32, (HALF, 1), 0)
    adj_w = jnp.where(((j == 1) | (j == 6)) & ((row24 < NC - HALF) | (lane < 64)), adj_w, 0.0)
    bar_w = 2.0 * (wk[12] - TAU * adj_w) - wk[0]
    wk[0] = bar_w

    wait_all(dir_r.at[2], fa.at[rows_in])
    for pr in range(NR):
        hg[pl.ds(3 * pr, 3), :] = fa[pl.ds(pr * CP + NC, CP - NC), :]
    hv = hg[pl.ds(0, HALF), :]
    gh, gl = split(jnp.concatenate([hv, pltpu.roll(hv, 64, 1)], 0)[:, 0:CP])
    real = lax.broadcasted_iota(jnp.int32, (CP, 1), 0) < NC

    def dual_three(p, own_bar):
        bars = []
        for r in range(4):
            pr = 4 * p + r
            here = rows_of(pr)
            new = ub[here, :] - TAU * jnp.where(real, fa[here, :], 0.0)
            u1[here, :] = new
            bars.append(2.0 * new - natural(u0, pr, 1, 0, CP))
            own_bar = pack_into(own_bar, bars[r], pr)
        for i in range(2):
            store_pair(gu, 2 * p + i, mm3(gh, gl, jnp.concatenate(bars[2 * i : 2 * i + 2], 1)))
        for r in range(4):
            pr = 4 * p + r
            here = rows_of(pr)
            a = pbr[here, :] + SIGMA * fr(bars[r], bars[r + 1] if r < 3 else None, r)
            b = pbc[here, :] + SIGMA * fx(bars[r], wk[0], pr)
            s = shrink(colsum(a * a + b * b), ALPHA1)
            a, b = a * s, b * s
            p2r[here, :] = a
            p2c[here, :] = b
            wo[pl.ds(pr, CP, stride=2 * NR), :] = v2r[here, :] + TAU * a
            wo[pl.ds(NR + pr, CP, stride=2 * NR), :] = v2c[here, :] + TAU * b
        return own_bar

    own_bar = lax.fori_loop(0, 2, dual_three, zero24)
    bar_w = jnp.where(j == 2, own_bar, wk[0])
    a = wk[10] + SIGMA * fr_w(bar_w)
    b = wk[11] + SIGMA * fx_w(bar_w)
    s = shrink(norm_w(a * a + b * b), ALPHA1)
    wk[3] = b * s
    def primal_two(p, _):
        for r in range(4):
            pr = 4 * p + r
            here = rows_of(pr)
            m = mask[pl.ds(pr, 1), :].astype(f32) * (1.0 / (1.0 + SIGMA))
            above = p2r[rows_of(pr - 1), :] if r > 0 else None
            div = br(p2r[here, :], above, r) + bx(p2c[here, :], wk[3], pr)
            adj = m * (fa[here, :] + SIGMA * gu[here, :])
            u1[here, :] = u1[here, :] - TAU * (adj - div)
        return 0

    lax.fori_loop(0, 2, primal_two, 0)
    wait_all(dir_s.at[0], ra.at[slots])
    wait_all(dir_s.at[1], rb.at[slots])
    wait_all(dir_s.at[2], fa.at[rows_in])
    wait_all(dir_s.at[4], edge_in.at[slots])
    for to_right, to_left in (edges, halos):

        @pl.when(has_right)
        def _():
            to_right.wait_send()

        @pl.when(has_left)
        def _():
            to_left.wait_send()

    wait_all(dir_r.at[3], fb.at[rows_in])

    def add_signals(pr, _):
        m = mask[pl.ds(pr, 1), :].astype(f32) * (TAU * SIGMA / (1.0 + SIGMA))
        uo[pl.ds(pr, CP, stride=NR), :] = u1[rows_of(pr), :] + m * fb[rows_of(pr), :]
        return 0

    lax.fori_loop(0, NR, add_signals, 0, unroll=True)

    wait_all(dir_s.at[3], fb.at[rows_in])


def put_kernel(u, w, u_hbm, w_hbm, sem):
    copies = [
        pltpu.make_async_copy(w.at[pl.ds(0, NC * 2 * NR)], w_hbm, sem.at[0]),
        pltpu.make_async_copy(u.at[pl.ds(0, NC * NR)], u_hbm, sem.at[1]),
    ]
    for c in copies:
        c.start()
    for c in copies:
        c.wait()


def body(nvox, signals, basis, response, shell_index, brain_mask, fodf, aux_field, grad_dual, sym_dual, data_dual):
    hbm = pl.BlockSpec(memory_space=pltpu.HBM)
    vmem = pl.BlockSpec(memory_space=pltpu.VMEM)
    field = pltpu.VMEM((NR * CP + 8, 128), f32)
    pairs = pltpu.VMEM((CP * 2 * NR + 16, 128), f32)
    triples = pltpu.VMEM((CP * 3 * NR + 24, 128), f32)
    measured = pltpu.VMEM((ND * NR + 8, 128), f32)
    npeer = SIDE * SIDE
    dma = lambda n: pltpu.SemaphoreType.DMA((n,))
    edges = pltpu.VMEM((HALF, 128), f32)
    halos = pltpu.VMEM((8 * HALF, 128), f32)
    u, w = pl.pallas_call(
        functools.partial(kernel, nvox),
        out_shape=(field, pairs),
        in_specs=[hbm] * 10,
        out_specs=(vmem, vmem),
        scratch_shapes=[
            pltpu.VMEM((ND * NR, 128), bf16),
            pltpu.VMEM((NC, ND), f32),
            pltpu.VMEM((3, 5), f32),
            pltpu.VMEM((1, ND), jnp.int32),
            pltpu.VMEM((2 * NR, 128), jnp.int32),
            field,
            pairs, pairs, triples,
            measured, measured,
            pltpu.VMEM((CP, 128), f32),
            field, field, field, field,
            pltpu.VMEM((npeer, HALF, 128), f32),
            pltpu.VMEM((npeer, HALF, 128), f32),
            pltpu.VMEM((HALF + 8, 128), f32),
            halos, halos, halos,
            edges, edges, edges,
            pltpu.VMEM((8, 128), f32),
            pltpu.VMEM((npeer, 8, 128), f32),
            pltpu.VMEM((13, HALF, 128), f32),
        ]
        + [field] * 18
        + [dma(10)]
        + [dma(5), dma(5), dma(4), dma(4)],
        compiler_params=pltpu.CompilerParams(
            collective_id=0, has_side_effects=True, vmem_limit_bytes=48 * 1024 * 1024
        ),
    )(*[pltpu.with_memory_space_constraint(x, pltpu.HBM) for x in (
        signals.reshape(ND * NR, 128),
        basis.T,
        response,
        shell_index.reshape(1, ND),
        brain_mask.reshape(NR, 128),
        fodf.reshape(NC * NR, 128),
        aux_field.reshape(NC * 2 * NR, 128),
        grad_dual.reshape(NC * 2 * NR, 128),
        sym_dual.reshape(NC * 3 * NR, 128),
        data_dual.reshape(ND * NR, 128),
    )])
    u, w = pl.pallas_call(
        put_kernel,
        out_shape=(pltpu.HBM((NC * NR, 128), f32), pltpu.HBM((NC * 2 * NR, 128), f32)),
        in_specs=[vmem, vmem],
        out_specs=(hbm, hbm),
        scratch_shapes=[dma(2)],
        compiler_params=pltpu.CompilerParams(vmem_limit_bytes=4 * 1024 * 1024),
    )(pltpu.with_memory_space_constraint(u, pltpu.VMEM), pltpu.with_memory_space_constraint(w, pltpu.VMEM))
    return u.reshape(fodf.shape), w.reshape(aux_field.shape)


def solution(mesh):
    placed = (
        P("dir", None, None, "vox"),
        P("dir", None),
        P(),
        P("dir"),
        P(None, None, "vox"),
        P(None, None, None, "vox"),
        P(None, None, None, None, "vox"),
        P(None, None, None, None, "vox"),
        P(None, None, None, None, "vox"),
        P("dir", None, None, "vox"),
    )
    return jax.shard_map(
        functools.partial(body, mesh.shape["vox"]),
        mesh=mesh,
        in_specs=placed,
        out_specs=(P(None, None, None, "vox"), P(None, None, None, None, "vox")),
        check_vma=False,
    )
```
